32 devices in a mesh: gx: 2 (over y), gy: 4 (over z), gz: 4 (over x, core).
Axes of the slice: x: 2, y: 2, z: 4, core: 2. Of those that a mesh axis runs over, the one named last changes fastest.
Arguments:
- populations: float32 [19, 32, 64, 512], P(None, 'gx', 'gy', 'gz'), may hold values from 0.02 to 0.1
- solid_flags: int32 [32, 64, 512], P('gx', 'gy', 'gz'), may hold values 0 or 1
- positions: float32 [448, 3, 128], P(('gx', 'gy', 'gz')), may hold values from -4 to 4
- anchors: float32 [448, 3, 128], P(('gx', 'gy', 'gz')), may hold values from -4 to 4
- base_cell: int32 [448, 3, 128], P(('gx', 'gy', 'gz')), may hold values from 0 to 510, as said below
- weights: float32 [448, 8, 128], P(('gx', 'gy', 'gz')), may hold values from 0.1 to 0.2
- intersection: int32 [448, 2], P(('gx', 'gy', 'gz')), may hold values from 0 to 15, as said below
Outputs:
- read: float32 [19, 32, 64, 512], P(None, 'gx', 'gy', 'gz')
- vertex_velocity: float32 [448, 3, 128], P(('gx', 'gy', 'gz'))
The draws below stay inside these ranges and needn't reach their ends.
Inputs may be any that keep to these rules, and one draw needn't show every extreme that they name: `intersection`: patch p's two bricks differ and lie in its owner's slab. For every owner, no brick is listed by more than 4 of its patches, and in every slab a quarter of the bricks are listed by exactly 4 patches of every owner of that slab. `base_cell`: all eight kernel cells of a vertex lie in one brick, in the slab of the patch's owner, and that brick is on the patch's list.
All inputs are finite; a program needn't handle non-finite values. No bound on the sum of `solid_flags` on one device may be relied on, other than what follows from the above.
Results may differ from the reference program's by a relative error of at most 0.00011.
Values sent between devices are 32-bit elements; how exact they have to be, the bound alone decides.
No kernel may reach another device: no remote copies, remote signals or barrier semaphores. Data moves between devices by JAX's collectives and lax.ppermute only.
A program may use at most 320 MiB of HBM per device.

```python
import jax
import jax.numpy as jnp
import numpy as np
from jax import lax

CX = 16
CY = 16
CZ = 128
VERT = 128
SLOT_CAP = 4
SLABS = 2
BRICKS_Z = 4
BRICKS = 16
PATCH_DEV = 14
PATCHES = 448
NX = 32
NY = 64
NZ = 512


def intersection_table(key):
    counts = np.where(np.arange(BRICKS) < BRICKS // 4, SLOT_CAP, SLOT_CAP // 4)
    rank_list = np.repeat(np.arange(BRICKS), counts)
    slab_keys = jax.random.split(jax.random.fold_in(key, 101), SLABS)
    dense_rank = jax.vmap(lambda sub_key: jax.random.permutation(sub_key, BRICKS))(slab_keys)
    grouped = dense_rank[:, rank_list].astype(jnp.int32)
    owner_keys = jax.random.split(jax.random.fold_in(key, 202), SLABS * BRICKS)
    patch_order = jax.vmap(lambda sub_key: jax.random.permutation(sub_key, PATCH_DEV))(owner_keys)
    patch_order = patch_order.reshape(SLABS, BRICKS, PATCH_DEV).astype(jnp.int32)
    spread_out = jnp.broadcast_to(grouped[:, None, :], (SLABS, BRICKS, 2 * PATCH_DEV))
    first_brick = jnp.take_along_axis(spread_out, patch_order, 2)
    second_brick = jnp.take_along_axis(spread_out, patch_order + PATCH_DEV, 2)
    swapped = jax.random.randint(jax.random.fold_in(key, 303), (SLABS, BRICKS, PATCH_DEV), 0, 2)
    left_brick = jnp.where(swapped == 1, second_brick, first_brick)
    right_brick = jnp.where(swapped == 1, first_brick, second_brick)
    return jnp.stack([left_brick, right_brick], axis=-1).reshape(PATCHES, 2).astype(jnp.int32)


def draw_intersection(key, part):
    return intersection_table(key)


def draw_base_cell(key, part):
    lists = intersection_table(key)
    which_brick = jax.random.randint(jax.random.fold_in(key, 404), (PATCHES, VERT), 0, 2)
    home_brick = jnp.where(which_brick == 0, lists[:, 0:1], lists[:, 1:2])
    owner_slab = (jnp.arange(PATCHES, dtype=jnp.int32) // (PATCH_DEV * BRICKS))[:, None]
    cell_x = owner_slab * CX + jax.random.randint(jax.random.fold_in(key, 505), (PATCHES, VERT), 0, CX - 1)
    cell_y = home_brick // BRICKS_Z * CY + jax.random.randint(jax.random.fold_in(key, 606), (PATCHES, VERT), 0, CY - 1)
    cell_z = home_brick % BRICKS_Z * CZ + jax.random.randint(jax.random.fold_in(key, 707), (PATCHES, VERT), 0, CZ - 1)
    return jnp.stack([cell_x, cell_y, cell_z], axis=1).astype(jnp.int32)


def touch_ends(values, rng, low, high):
    longest = values.shape.index(max(values.shape))
    spots = []
    for shift in (0, 1):
        where = [jax.random.randint(jax.random.fold_in(rng, axis), (), 0, length) for axis, length in enumerate(values.shape)]
        where[longest] = (where[longest] + shift) % values.shape[longest]
        spots.append(tuple(where))
    return values.at[spots[0]].set(low).at[spots[1]].set(high)


def block_scale(stream_key, extent, cuts, least, top_value):
    loudness, own = 1.0, jax.random.fold_in(stream_key, 6)
    for position, shards_of in cuts:
        heights = jnp.exp(jax.random.uniform(jax.random.fold_in(own, position), (shards_of,), jnp.float32, least / len(cuts), top_value / len(cuts)))
        loudness = loudness * jnp.repeat(heights, extent[position] // shards_of).reshape([-1 if axis == position else 1 for axis in range(len(extent))])
    return loudness


def bell_draw(key, dims, spread, bound, cuts=(), held_as=jnp.bfloat16):
    level = block_scale(key, dims, cuts, -0.22, 0.18) if cuts else 1.0
    drawn = jax.random.normal(key, dims, jnp.float32) * spread * level
    return jnp.minimum(jnp.maximum(drawn, -bound), bound).astype(held_as)


def setup_inputs(seed: int = 0) -> dict:
    keys = jax.random.split(jax.random.key(seed), 8)
    populations = jnp.clip(0.02 + 0.08 * jax.random.uniform(keys[0], (19, NX, NY, NZ), jnp.float32) ** block_scale(keys[0], (19, NX, NY, NZ), ((1, 2), (2, 4), (3, 4)), -0.2, 0.2), 0.02, 0.1)
    solid_flags = touch_ends((jax.random.randint(keys[1], (NX, NY, NZ), 0, 8) < 1).astype(jnp.int32), jax.random.fold_in(keys[1], 1), 0, 1)
    positions = bell_draw(keys[2], (PATCHES, 3, VERT), 1.0, 4.0, ((0, 32),), jnp.float32)
    anchors = bell_draw(keys[3], (PATCHES, 3, VERT), 1.0, 4.0, ((0, 32),), jnp.float32)
    base_cell = draw_base_cell(jax.random.fold_in(keys[7], 71), 0)
    weights = jnp.clip(0.1 + 0.1 * jax.random.uniform(keys[5], (PATCHES, 8, VERT), jnp.float32) ** block_scale(keys[5], (PATCHES, 8, VERT), ((0, 32),), -0.2, 0.2), 0.1, 0.2)
    intersection = draw_intersection(jax.random.fold_in(keys[7], 71), 0)
    return dict(populations=populations, solid_flags=solid_flags, positions=positions, anchors=anchors, base_cell=base_cell, weights=weights, intersection=intersection)


RELAXATION = 0.8
TENSION = 0.05
TETHER = 0.5
VELOCITIES = [(0, 0, 0), (1, 0, 0), (-1, 0, 0), (0, 1, 0), (0, -1, 0), (0, 0, 1), (0, 0, -1),
              (1, 1, 0), (-1, -1, 0), (1, -1, 0), (-1, 1, 0), (1, 0, 1), (-1, 0, -1),
              (1, 0, -1), (-1, 0, 1), (0, 1, 1), (0, -1, -1), (0, 1, -1), (0, -1, 1)]
OPPOSITE = [0, 2, 1, 4, 3, 6, 5, 8, 7, 10, 9, 12, 11, 14, 13, 16, 15, 18, 17]
LATTICE_WEIGHTS = [1.0 / 3.0] + [1.0 / 18.0] * 6 + [1.0 / 36.0] * 12


def membrane_force(positions, anchors):
    cycle_term = jnp.roll(positions, 1, axis=2) + jnp.roll(positions, -1, axis=2) - 2.0 * positions
    return TENSION * cycle_term + TETHER * (anchors - positions)


def collide(populations, solid_flags, force_field):
    lattice = jnp.asarray(VELOCITIES, jnp.float32)
    density = jnp.sum(populations, axis=0)
    momentum = jnp.einsum("qa,qxyz->axyz", lattice, populations, precision=lax.Precision.HIGHEST)
    velocity = (momentum + 0.5 * force_field) / density
    speed_sq = velocity[0] * velocity[0] + velocity[1] * velocity[1] + velocity[2] * velocity[2]
    u_dot_f = velocity[0] * force_field[0] + velocity[1] * force_field[1] + velocity[2] * force_field[2]
    factor = 1.0 - 0.5 / RELAXATION
    outputs = []
    for direction in range(19):
        move_x, move_y, move_z = VELOCITIES[direction]
        along_u = move_x * velocity[0] + move_y * velocity[1] + move_z * velocity[2]
        along_f = move_x * force_field[0] + move_y * force_field[1] + move_z * force_field[2]
        weight_q = LATTICE_WEIGHTS[direction]
        equilibrium = weight_q * density * (1.0 + 3.0 * along_u + 4.5 * along_u * along_u - 1.5 * speed_sq)
        forcing = factor * weight_q * (3.0 * (along_f - u_dot_f) + 9.0 * along_u * along_f)
        current = populations[direction]
        relaxed = current - (current - equilibrium) / RELAXATION + forcing
        outputs.append(jnp.where(solid_flags == 1, populations[OPPOSITE[direction]], relaxed))
    return jnp.stack(outputs), velocity


def reference(populations, solid_flags, positions, anchors, base_cell, weights, intersection):
    forces = membrane_force(positions, anchors)
    owner_slab = jnp.arange(PATCHES, dtype=jnp.int32) // (PATCH_DEV * BRICKS)
    cell_x = base_cell[:, 0, :]
    cell_y = base_cell[:, 1, :]
    cell_z = base_cell[:, 2, :]
    home_brick = (cell_y // CY) * BRICKS_Z + cell_z // CZ
    live_mask = (cell_x // CX == owner_slab[:, None]) & ((home_brick == intersection[:, 0:1]) | (home_brick == intersection[:, 1:2]))
    kernel = weights * live_mask[:, None, :].astype(jnp.float32)
    force_field = jnp.zeros((3, NX * NY * NZ), jnp.float32)
    index_list = []
    for corner in range(8):
        offset_x = (corner >> 2) & 1
        offset_y = (corner >> 1) & 1
        offset_z = corner & 1
        cell_index = ((cell_x + offset_x) * NY + cell_y + offset_y) * NZ + cell_z + offset_z
        cell_index = cell_index.astype(jnp.int32).reshape(-1)
        index_list.append(cell_index)
        contrib = kernel[:, corner, :][:, None, :] * forces
        force_field = force_field.at[:, cell_index].add(jnp.transpose(contrib, (1, 0, 2)).reshape(3, -1))
    force_field = force_field.reshape(3, NX, NY, NZ)
    post_collision, velocity = collide(populations, solid_flags, force_field)
    read = jnp.stack([jnp.roll(post_collision[direction], VELOCITIES[direction], (0, 1, 2)) for direction in range(19)])
    flat_velocity = velocity.reshape(3, -1)
    vertex_velocity = jnp.zeros((PATCHES, 3, VERT), jnp.float32)
    for corner in range(8):
        sampled = jnp.transpose(flat_velocity[:, index_list[corner]].reshape(3, PATCHES, VERT), (1, 0, 2))
        vertex_velocity = vertex_velocity + kernel[:, corner, :][:, None, :] * sampled
    return read, vertex_velocity
```

```python
import functools

import jax
import jax.numpy as jnp
from jax import lax
from jax.experimental import pallas as pl
from jax.experimental.pallas import tpu as pltpu
from jax.sharding import PartitionSpec as P

SLOT_CAP = 4
GROUPS = 7
MERGE = 4
UNROLL = 5
PART = 32

RELAXATION = 0.8
TENSION = 0.05
TETHER = 0.5
VELOCITIES = [
    (0, 0, 0),
    (1, 0, 0),
    (-1, 0, 0),
    (0, 1, 0),
    (0, -1, 0),
    (0, 0, 1),
    (0, 0, -1),
    (1, 1, 0),
    (-1, -1, 0),
    (1, -1, 0),
    (-1, 1, 0),
    (1, 0, 1),
    (-1, 0, -1),
    (1, 0, -1),
    (-1, 0, 1),
    (0, 1, 1),
    (0, -1, -1),
    (0, 1, -1),
    (0, -1, 1),
]
LATTICE_WEIGHTS = [1.0 / 3.0] + [1.0 / 18.0] * 6 + [1.0 / 36.0] * 12


def crossing(axis, sign):
    return [q for q in range(19) if VELOCITIES[q][axis] == sign]


X_LISTS = {1: crossing(0, 1), -1: crossing(0, -1)}
Y_LISTS = {1: crossing(1, 1), -1: crossing(1, -1)}
Z_LISTS = {1: crossing(2, 1), -1: crossing(2, -1)}
Y_EDGES = {s: [q for q in Y_LISTS[s] if VELOCITIES[q][0] != 0] for s in (1, -1)}
Z_EDGES = {
    s: [q for q in Z_LISTS[s] if VELOCITIES[q][0] != 0 or VELOCITIES[q][1] != 0] for s in (1, -1)
}

BF = jnp.bfloat16
F32 = jnp.float32
MIB = 1024 * 1024
NT = (((1,), (1,)), ((), ()))
NN = (((1,), (0,)), ((), ()))


def settings(mib):
    return pltpu.CompilerParams(vmem_limit_bytes=mib * MIB)


def cost(flops, size):
    return pl.CostEstimate(flops=flops, bytes_accessed=size, transcendentals=0)


def vmem():
    return pl.BlockSpec(memory_space=pltpu.VMEM)


def smem():
    return pl.BlockSpec(memory_space=pltpu.SMEM)


def list_kernel(
    bricks_z,
    inter_ref,
    pos_ref,
    anchor_ref,
    cell_ref,
    weight_ref,
    near_ref,
    far_ref,
    rank_ref,
    base_ref,
    payload,
    lists,
    count_ref,
    extent,
):
    patches, verts = pos_ref.shape[1:]
    bricks = near_ref.shape[0]
    pos = pos_ref[...]
    cycle_term = pltpu.roll(pos, 1, 2) + pltpu.roll(pos, verts - 1, 2) - 2.0 * pos
    forces = TENSION * cycle_term + TETHER * (anchor_ref[...] - pos)
    cells = cell_ref[...].astype(F32)
    payload[:, 0:8, :] = weight_ref[...]
    for p in range(patches):
        payload[p, 8:11, :] = forces[:, p, :]
        payload[p, 11:14, :] = cells[:, p, :] + 1.0
        payload[p, 14:16, :] = jnp.zeros((2, verts), F32)
    lists[...] = jnp.zeros(lists.shape, F32)

    @pl.loop(0, bricks)
    def _(b):
        count_ref[b] = 0

    lane = lax.broadcasted_iota(jnp.int32, (patches, verts), 1)
    row = lax.broadcasted_iota(jnp.int32, (patches, verts), 0)
    upper = (
        lax.broadcasted_iota(jnp.int32, (verts, verts), 0)
        <= lax.broadcasted_iota(jnp.int32, (verts, verts), 1)
    ).astype(F32)
    codes, sums = [], []
    for i in range(2):
        first_y = jnp.zeros((patches, verts), F32)
        first_z = jnp.zeros((patches, verts), F32)
        for p in range(patches):
            brick = inter_ref[i, p]
            first_y = jnp.where(row == p, (brick // bricks_z * extent[1]).astype(F32), first_y)
            first_z = jnp.where(row == p, (brick % bricks_z * extent[2]).astype(F32), first_z)
        live = (
            (cells[1] >= first_y)
            & (cells[1] < first_y + extent[1])
            & (cells[2] >= first_z)
            & (cells[2] < first_z + extent[2])
        )
        mask = live.astype(F32)
        total = jnp.dot(mask.astype(BF), upper.astype(BF), preferred_element_type=F32)
        rank = (total - mask).astype(jnp.int32)
        rank_ref[i] = jnp.where(live, rank, -1)
        code = jnp.where(live, (lane - rank) + lane * 256 + 65536, 0)
        step = 1
        while step < verts:
            moving = jnp.where((code & step) != 0, code, 0)
            code = (code - moving) + pltpu.roll(moving, verts - step, 1)
            step *= 2
        codes.append(code)
        sums.append(total)
    wide_lane = lax.broadcasted_iota(jnp.int32, (16, verts), 1)
    for p in range(patches):
        for i in range(2):
            brick = inter_ref[i, p]
            base = count_ref[brick]
            base_ref[2 * p + i] = base
            count_ref[brick] = base + jnp.max(sums[i][p : p + 1, :]).astype(jnp.int32)
            block = lax.shift_right_logical(base, 7)
            shift = base & (verts - 1)
            code = jnp.broadcast_to(codes[i][p : p + 1, :], (8, verts))
            code = pltpu.roll(code, shift, 1)
            code = jnp.concatenate([code, code], axis=0)
            source = lax.shift_right_logical(code, 8) & (verts - 1)
            moved = jnp.take_along_axis(payload[p], source, axis=1)
            moved = jnp.where(code >= 65536, moved, 0.0)
            lists[brick, block] += jnp.where(wide_lane >= shift, moved, 0.0)
            lists[brick, block + 1] += jnp.where(wide_lane < shift, moved, 0.0)

    @pl.loop(0, bricks)
    def _(b):
        for half, out_ref in ((0, near_ref), (1, far_ref)):
            for j in range(2):
                value = lists[b, 2 * half + j]
                for g in range(3):
                    out_ref[b, 3 * j + g] = value[4 * g : 4 * g + 4]
                out_ref[b, 6, 2 * j : 2 * j + 2] = value[12:14]


def build_lists(intersection, positions, anchors, base_cell, weights, bricks, bricks_z, extent):
    _, patches, verts = positions.shape
    half = jax.ShapeDtypeStruct((bricks, GROUPS, 4, verts), F32)

    def kernel(*refs):
        list_kernel(bricks_z, *refs, extent)

    return pl.pallas_call(
        kernel,
        out_shape=(
            half,
            half,
            jax.ShapeDtypeStruct((2, patches, verts), jnp.int32),
            jax.ShapeDtypeStruct((2 * patches,), jnp.int32),
        ),
        in_specs=[smem(), vmem(), vmem(), vmem(), vmem()],
        out_specs=(vmem(), vmem(), vmem(), smem()),
        scratch_shapes=[
            pltpu.VMEM((patches, 16, verts), F32),
            pltpu.VMEM((bricks, SLOT_CAP + 1, 16, verts), F32),
            pltpu.SMEM((bricks,), jnp.int32),
        ],
        compiler_params=settings(56),
        name="vertex_lists",
    )(intersection, positions, anchors, base_cell, weights)


def block_rows(table_ref, owner, j):
    weight = jnp.concatenate([table_ref[owner, 3 * j], table_ref[owner, 3 * j + 1]], axis=0)
    third = table_ref[owner, 3 * j + 2]
    last = table_ref[owner, 6]
    cells = jnp.concatenate([third[3:4], last[2 * j : 2 * j + 2]], axis=0)
    return weight, third[0:3], cells


def merged_rows(table_ref, first):
    parts = None
    for m in range(MERGE):
        rows = block_rows(table_ref, first + m, 0)
        if m:
            rows = [pltpu.roll(value, m * PART, 1) for value in rows]
        parts = rows if parts is None else [a + b for a, b in zip(parts, rows)]
    return parts


def spills(table_ref):
    owners, _, _, verts = table_ref.shape
    lane = lax.broadcasted_iota(jnp.int32, (4, verts), 1)
    row = lax.broadcasted_iota(jnp.int32, (4, verts), 0)
    most = jnp.zeros((4, verts), F32)
    for owner in range(owners):
        own = jnp.maximum(jnp.where(lane >= PART, table_ref[owner, 2], 0.0), table_ref[owner, 5])
        most = jnp.maximum(most, jnp.where(row == 3, own, 0.0))
    return jnp.max(most) > 0.0


def far_blocks(table_ref, rows_buf, spilled, step):
    def keep(blocks):
        for j, (weight, force, cells) in enumerate(blocks):
            rows_buf[j, 0:8] = weight
            rows_buf[j, 8:11] = force
            rows_buf[j, 11:14] = cells

    @pl.when(jnp.logical_not(spilled))
    def _():
        first = step * (MERGE * SLOT_CAP)
        keep([merged_rows(table_ref, first + MERGE * m) for m in range(SLOT_CAP)])

    @pl.when(spilled)
    def _():
        keep(pair_blocks(table_ref, step))

    return [(rows_buf[j, 0:8], rows_buf[j, 8:11], rows_buf[j, 11:14]) for j in range(SLOT_CAP)]


def far_steps(owners, spilled):
    return jnp.where(spilled, owners // 2, owners // (MERGE * SLOT_CAP))


def place_rows(place_ref, rows, extent):
    weight, force, cells = rows
    local, inside = [], None
    for d in range(3):
        value = cells[d : d + 1] - (place_ref[d] + 1).astype(F32)
        ok = (value >= 0.0) & (value < float(extent[d]))
        inside = ok if inside is None else inside & ok
        local.append(value)
    weight = weight * jnp.broadcast_to(inside.astype(F32), weight.shape)
    return weight, force, local


def halves(value):
    high = value.astype(BF).astype(F32)
    return high, value - high


def spread_scratch(extent, verts):
    size_x, size_y, size_z = extent
    depth = SLOT_CAP * 2 * verts
    return [
        pltpu.VMEM((2, 2, size_x * size_y, depth), BF),
        pltpu.VMEM((2, 6 * size_z, depth), BF),
        pltpu.VMEM((2, SLOT_CAP, 16, verts), F32),
        pltpu.VMEM((2, SLOT_CAP, 8, verts), F32),
        pltpu.VMEM((2, SLOT_CAP, 8, verts), F32),
    ]


def spread_tools(place_ref, extent, verts, total, a_buf, zf_buf, w_rows, f_rows, c_rows):
    size_x, size_y, size_z = extent
    iota_y = lax.broadcasted_iota(jnp.int32, (16, verts), 0).astype(F32).astype(BF)
    zero = jnp.zeros((16, verts), BF)

    def wide(ref, slot, j, row):
        return jnp.broadcast_to(ref[slot, j, row : row + 1, :], (16, verts)).astype(BF)

    def build(blocks, slot):
        for j, rows in enumerate(blocks):
            weight, force, local = place_rows(place_ref, rows, extent)
            w_hi, w_lo = halves(weight)
            f_hi, f_lo = halves(force)
            w_rows[slot, j, 0:8] = w_hi
            w_rows[slot, j, 8:16] = w_lo
            f_rows[slot, j, 0:3] = f_hi
            f_rows[slot, j, 4:7] = f_lo
            for d in range(3):
                c_rows[slot, j, d : d + 1] = local[d]
        for j in range(len(blocks)):
            xl = wide(c_rows, slot, j, 0)
            yl = wide(c_rows, slot, j, 1)
            zl = wide(c_rows, slot, j, 2)
            at_y0 = iota_y == yl
            at_y1 = iota_y == yl + 1.0
            lines = {}
            for part in range(2):
                for dx in range(2):
                    for dz in range(2):
                        first = part * 8 + dx * 4 + dz
                        lines[part, dx, dz] = jnp.where(
                            at_y0,
                            wide(w_rows, slot, j, first),
                            jnp.where(at_y1, wide(w_rows, slot, j, first + 2), zero),
                        )
            before = None
            for x in range(size_x):
                here = xl == float(x)
                for part in range(2):
                    for dz in range(2):
                        value = jnp.where(here, lines[part, 0, dz], zero)
                        if before is not None:
                            value = jnp.where(before, lines[part, 1, dz], value)
                        column = (j * 2 + dz) * verts
                        a_buf[slot, part, x * 16 : (x + 1) * 16, column : column + verts] = value
                before = here
            force = [wide(f_rows, slot, j, part * 4 + c) for part in range(2) for c in range(3)]
            for zb in range(size_z // 16):
                for dz in range(2):
                    at_z = iota_y == zl + float(dz - 16 * zb)
                    column = (j * 2 + dz) * verts
                    for part in range(2):
                        for c in range(3):
                            line = (part * 3 + c) * size_z + zb * 16
                            zf_buf[slot, line : line + 16, column : column + verts] = jnp.where(
                                at_z, force[part * 3 + c], zero
                            )

    def product(slot):
        lines = 3 * size_z
        high = lax.dot_general(zf_buf[slot], a_buf[slot, 0], NT, preferred_element_type=F32)
        low = lax.dot_general(
            zf_buf[slot, :lines], a_buf[slot, 1], NT, preferred_element_type=F32
        )
        total[...] += high[:lines] + high[lines:] + low

    return build, product


def pair_blocks(table_ref, step):
    return [block_rows(table_ref, 2 * step + oo, j) for oo in range(2) for j in range(2)]


def near_kernel(extent, place_ref, table_ref, total, *scratch):
    owners, _, _, verts = table_ref.shape
    build, product = spread_tools(place_ref, extent, verts, total, *scratch)
    steps = owners // 2
    total[...] = jnp.zeros(total.shape, F32)
    build(pair_blocks(table_ref, 0), 0)

    @pl.loop(0, steps // 2)
    def _(i):
        build(pair_blocks(table_ref, 2 * i + 1), 1)
        product(0)
        build(pair_blocks(table_ref, jnp.minimum(2 * i + 2, steps - 1)), 0)
        product(1)


def spread_near(place, table, extent):
    owners, _, _, verts = table.shape
    size_x, size_y, size_z = extent
    cross = size_x * size_y
    return pl.pallas_call(
        functools.partial(near_kernel, extent),
        out_shape=jax.ShapeDtypeStruct((3 * size_z, cross), F32),
        in_specs=[smem(), vmem()],
        out_specs=vmem(),
        scratch_shapes=spread_scratch(extent, verts),
        compiler_params=settings(16),
        cost_estimate=cost(6 * owners * 3 * size_z * cross * 4 * verts, MIB),
        name="spread_near",
    )(place, table)


def collide_kernel(
    place_ref,
    table_ref,
    near_ref,
    pop_hbm,
    solid_hbm,
    post_hbm,
    xface_ref,
    yfp_ref,
    yfm_ref,
    zfp_ref,
    zfm_ref,
    unit_ref,
    pop,
    solid,
    post,
    total,
    field,
    rows_buf,
    sems,
    store_sems,
    *scratch,
):
    size_x, size_y, size_z = solid.shape
    owners, _, _, verts = table_ref.shape
    load_pop = pltpu.make_async_copy(pop_hbm, pop, sems.at[0])
    load_solid = pltpu.make_async_copy(solid_hbm, solid, sems.at[1])
    load_pop.start()
    load_solid.start()
    build, product = spread_tools(place_ref, solid.shape, verts, total, *scratch)
    total[...] = near_ref[...]
    spilled = spills(table_ref)

    @pl.loop(0, far_steps(owners, spilled))
    def _(step):
        build(far_blocks(table_ref, rows_buf, spilled, step), 0)
        product(0)

    for c in range(3):
        for half in range(size_x * size_y // 128):
            field[c, half * 128 : (half + 1) * 128, :] = jnp.transpose(
                total[c * size_z : (c + 1) * size_z, half * 128 : (half + 1) * 128]
            )

    load_pop.wait()
    load_solid.wait()
    lane = lax.broadcasted_iota(jnp.int32, (size_y, size_z), 1)
    factor = 1.0 - 0.5 / RELAXATION
    keep = 1.0 - 1.0 / RELAXATION
    rate = 1.0 / RELAXATION

    def plane(x, z_out):
        z_out = dict(zip((1, -1), z_out))
        lines = pl.ds(pl.multiple_of(x * 16, 16), 16)
        cells = [pop[q, x] for q in range(19)]
        rho = cells[0]
        for q in range(1, 19):
            rho = rho + cells[q]
        force = [field[c, lines, :] for c in range(3)]
        inverse = 1.0 / rho
        vel = []
        for c in range(3):
            moment = None
            for q in range(1, 19, 2):
                if VELOCITIES[q][c] != 0:
                    term = cells[q] - cells[q + 1]
                    if VELOCITIES[q][c] < 0:
                        term = -term
                    moment = term if moment is None else moment + term
            vel.append((moment + 0.5 * force[c]) * inverse)
        for c in range(3):
            high, low = halves(vel[c])
            first = pl.ds(pl.multiple_of((x * 3 + c) * 16, 16), 16)
            unit_ref[first, 0:size_z] = high.astype(BF)
            unit_ref[first, size_z : 2 * size_z] = low.astype(BF)
        speed = vel[0] * vel[0] + vel[1] * vel[1] + vel[2] * vel[2]
        u_dot_f = vel[0] * force[0] + vel[1] * force[1] + vel[2] * force[2]
        rest = rate * rho * (1.0 - 1.5 * speed) - (3.0 * factor) * u_dot_f
        quad = (4.5 * rate) * rho
        linear = (3.0 * rate) * rho
        wall = solid[x] == 1
        results = [None] * 19
        results[0] = jnp.where(wall, cells[0], keep * cells[0] + LATTICE_WEIGHTS[0] * rest)

        def along(vector, q):
            value = None
            for c in range(3):
                move = VELOCITIES[q][c]
                if move == 0:
                    continue
                if value is None:
                    value = vector[c] if move > 0 else -vector[c]
                else:
                    value = value + vector[c] if move > 0 else value - vector[c]
            return value

        for q in range(1, 19, 2):
            a = along(vel, q)
            b = along(force, q)
            weight = LATTICE_WEIGHTS[q]
            even = weight * (rest + a * (quad * a + (9.0 * factor) * b))
            odd = weight * (linear * a + (3.0 * factor) * b)
            results[q] = jnp.where(wall, cells[q + 1], keep * cells[q] + (even + odd))
            results[q + 1] = jnp.where(wall, cells[q], keep * cells[q + 1] + (even - odd))
        for q in range(19):
            post[q, x] = results[q]
        pltpu.make_async_copy(post.at[:, x], post_hbm.at[:, x], store_sems.at[x]).start()
        for sign, line, face in ((1, size_y - 1, yfp_ref), (-1, 0, yfm_ref)):
            for k, q in enumerate(Y_LISTS[sign]):
                face[k, pl.ds(x, 1), :] = results[q][line : line + 1, :]
        for sign, column in ((1, size_z - 1), (-1, 0)):
            for k, q in enumerate(Z_LISTS[sign]):
                place = k * 16 + x
                moved = pltpu.roll(results[q], (place - column + size_z) & (size_z - 1), 1)
                z_out[sign] = jnp.where(lane == place, moved, z_out[sign])
        return z_out[1], z_out[-1]

    empty = jnp.zeros((size_y, size_z), F32)
    zfp_ref[...], zfm_ref[...] = lax.fori_loop(0, size_x, plane, (empty, empty), unroll=2)
    for k, q in enumerate(X_LISTS[1]):
        xface_ref[k] = post[q, size_x - 1]
    for k, q in enumerate(X_LISTS[-1]):
        xface_ref[5 + k] = post[q, 0]
    for x in range(size_x):
        pltpu.make_async_copy(post.at[:, x], post_hbm.at[:, x], store_sems.at[x]).wait()


def collide(place, table, near, populations, solid):
    _, size_x, size_y, size_z = populations.shape
    verts = table.shape[3]
    cross = size_x * size_y
    anyspace = pl.BlockSpec(memory_space=pl.ANY)
    face_y = jax.ShapeDtypeStruct((5, size_x, size_z), F32)
    face_z = jax.ShapeDtypeStruct((size_y, size_z), F32)
    return pl.pallas_call(
        collide_kernel,
        out_shape=(
            jax.ShapeDtypeStruct(populations.shape, F32),
            jax.ShapeDtypeStruct((10, size_y, size_z), F32),
            face_y,
            face_y,
            face_z,
            face_z,
            jax.ShapeDtypeStruct((cross * 3, 2 * size_z), BF),
        ),
        in_specs=[smem(), vmem(), vmem(), anyspace, anyspace],
        out_specs=(anyspace,) + (vmem(),) * 6,
        scratch_shapes=[
            pltpu.VMEM(populations.shape, F32),
            pltpu.VMEM(solid.shape, jnp.int32),
            pltpu.VMEM(populations.shape, F32),
            pltpu.VMEM((3 * size_z, cross), F32),
            pltpu.VMEM((3, cross, size_z), F32),
            pltpu.VMEM((SLOT_CAP, 16, verts), F32),
            pltpu.SemaphoreType.DMA((2,)),
            pltpu.SemaphoreType.DMA((size_x,)),
        ]
        + spread_scratch(solid.shape, verts),
        compiler_params=settings(24),
        cost_estimate=cost(4 * MIB * 1024, 6 * MIB),
        name="collide",
    )(place, table, near, populations, solid)


def sample_scratch(extent, verts):
    size_x, size_y, size_z = extent
    return [
        pltpu.VMEM((2, SLOT_CAP, 2 * size_z, 2 * verts), BF),
        pltpu.VMEM((2, 3 * size_x * size_y, 2 * verts), F32),
        pltpu.VMEM((2, SLOT_CAP, 8, verts), F32),
        pltpu.VMEM((2, SLOT_CAP, 8, verts), F32),
    ]


def sample_tools(place_ref, unit_ref, extent, verts, hot, grid_buf, w_rows, c_rows):
    size_x, size_y, size_z = extent
    iota_y = lax.broadcasted_iota(jnp.int32, (16, verts), 0).astype(F32)
    iota_b = iota_y.astype(BF)
    one = jnp.ones((16, verts), BF)
    zero_b = jnp.zeros((16, verts), BF)
    zero = jnp.zeros((16, verts), F32)

    def wide(ref, slot, j, row):
        return jnp.broadcast_to(ref[slot, j, row : row + 1, :], (16, verts))

    def prepare(blocks, slot):
        for j, rows in enumerate(blocks):
            weight, _, local = place_rows(place_ref, rows, extent)
            w_rows[slot, j] = weight
            for d in range(3):
                c_rows[slot, j, d : d + 1] = local[d]
        for j in range(len(blocks)):
            zl = wide(c_rows, slot, j, 2).astype(BF)
            for zb in range(size_z // 16):
                for dz in range(2):
                    value = jnp.where(iota_b == zl + float(dz - 16 * zb), one, zero_b)
                    for part in range(2):
                        line = part * size_z + zb * 16
                        hot[slot, j, line : line + 16, dz * verts : (dz + 1) * verts] = value

    def product(slot, j):
        grid_buf[j % 2] = lax.dot_general(unit_ref[...], hot[slot, j], NN, preferred_element_type=F32)

    def select(slot, j):
        xl = wide(c_rows, slot, j, 0)
        yl = wide(c_rows, slot, j, 1)
        at_y0 = iota_y == yl
        at_y1 = iota_y == yl + 1.0
        lines = {}
        for dx in range(2):
            for dz in range(2):
                first = dx * 4 + dz
                lines[dx, dz] = jnp.where(
                    at_y0,
                    wide(w_rows, slot, j, first),
                    jnp.where(at_y1, wide(w_rows, slot, j, first + 2), zero),
                )
        sums = [zero, zero, zero]
        before = None
        for x in range(size_x):
            here = xl == float(x)
            for dz in range(2):
                value = jnp.where(here, lines[0, dz], zero)
                if before is not None:
                    value = jnp.where(before, lines[1, dz], value)
                for c in range(3):
                    first = (x * 3 + c) * 16
                    part = grid_buf[j % 2, first : first + 16, dz * verts : (dz + 1) * verts]
                    sums[c] = sums[c] + value * part
            before = here
        return [jnp.sum(value, axis=0, keepdims=True) for value in sums]

    def work(slot, store):
        product(slot, 0)
        for j in range(SLOT_CAP):
            if j + 1 < SLOT_CAP:
                product(slot, j + 1)
            store(j, select(slot, j))

    return prepare, work


def sample_near_kernel(extent, place_ref, table_ref, unit_ref, out_ref, *scratch):
    owners, _, _, verts = table_ref.shape
    prepare, work = sample_tools(place_ref, unit_ref, extent, verts, *scratch)
    steps = owners // 2
    prepare(pair_blocks(table_ref, 0), 0)

    def store(step):
        def place(j, values):
            for c in range(3):
                out_ref[2 * step + j // 2, j % 2, c : c + 1, :] = values[c]

        return place

    @pl.loop(0, steps // 2)
    def _(i):
        prepare(pair_blocks(table_ref, 2 * i + 1), 1)
        work(0, store(2 * i))
        prepare(pair_blocks(table_ref, jnp.minimum(2 * i + 2, steps - 1)), 0)
        work(1, store(2 * i + 1))


def sample_near(place, table, unit, extent):
    owners, _, _, verts = table.shape
    size_x, size_y, size_z = extent
    return pl.pallas_call(
        functools.partial(sample_near_kernel, extent),
        out_shape=jax.ShapeDtypeStruct((owners, 2, 4, verts), F32),
        in_specs=[smem(), vmem(), vmem()],
        out_specs=vmem(),
        scratch_shapes=sample_scratch(extent, verts),
        compiler_params=settings(12),
        cost_estimate=cost(16 * owners * 3 * size_x * size_y * size_z * verts, MIB),
        name="sample_near",
    )(place, table, unit)


def x_plane(xr_ref, q):
    sign = VELOCITIES[q][0]
    return xr_ref[(0 if sign > 0 else 5) + X_LISTS[sign].index(q)]


def return_kernel(
    extent, place_ref, table_ref, unit_ref, near_ref, xr_ref, yrp_ref, yrm_ref, out_ref, rows_buf, found, *scratch
):
    owners, _, _, verts = table_ref.shape
    _, size_y, size_z = extent
    prepare, work = sample_tools(place_ref, unit_ref, extent, verts, *scratch)
    out_ref[:, 0:2] = near_ref[...]
    out_ref[:, 2:4] = jnp.zeros((owners, 2, 4, verts), F32)
    for owner in range(owners):
        for row in range(4):
            out_ref[owner, row, 3:4, :] = jnp.zeros((1, verts), F32)
    spilled = spills(table_ref)

    def store(j, values):
        for c in range(3):
            found[j, c : c + 1, :] = values[c]

    @pl.loop(0, far_steps(owners, spilled))
    def _(step):
        prepare(far_blocks(table_ref, rows_buf, spilled, step), 0)
        work(0, store)

        @pl.when(jnp.logical_not(spilled))
        def _():
            for j in range(SLOT_CAP):
                value = found[j]
                for m in range(MERGE):
                    if m:
                        value = pltpu.roll(value, verts - PART, 1)
                    owner = (step * SLOT_CAP + j) * MERGE + m
                    out_ref[owner, 2, 0:3, :] = value[0:3]

        @pl.when(spilled)
        def _():
            for j in range(SLOT_CAP):
                out_ref[2 * step + j // 2, 2 + j % 2, 0:3, :] = found[j, 0:3]

    y_halo = {1: yrp_ref, -1: yrm_ref}
    gy, gz, ny, nz = [place_ref[n] for n in (4, 5, 7, 8)]
    lane = lax.broadcasted_iota(jnp.int32, (size_y, size_z), 1)
    for sign in (1, -1):
        to_y = lax.rem(gy + sign + ny, ny) * nz + gz
        line = size_y - 1 if sign > 0 else 0
        for e, q in enumerate(Y_EDGES[sign]):
            out_ref[to_y, e, 3:4, :] = x_plane(xr_ref, q)[line : line + 1, :]
        to_z = gy * nz + lax.rem(gz + sign + nz, nz)
        column = size_z - 1 if sign > 0 else 0
        block = jnp.zeros((size_y, size_z), F32)
        for e, q in enumerate(Z_EDGES[sign]):
            if VELOCITIES[q][0] != 0:
                plane = x_plane(xr_ref, q)
            else:
                y_sign = VELOCITIES[q][1]
                plane = y_halo[y_sign][Y_LISTS[y_sign].index(q)]
            block = jnp.where(lane == e, pltpu.roll(plane, (e - column) % size_z, 1), block)
        block = jnp.concatenate([block, jnp.zeros((size_z - size_y, size_z), F32)], axis=0)
        block = jnp.transpose(block)
        for e in range(len(Z_EDGES[sign])):
            out_ref[to_z, e, 3:4, :] = block[e : e + 1, :]


def sample_return(place, table, unit, near, x_halo, y_plus, y_minus, extent):
    owners, _, _, verts = table.shape
    return pl.pallas_call(
        functools.partial(return_kernel, extent),
        out_shape=jax.ShapeDtypeStruct((owners, 4, 4, verts), F32),
        in_specs=[smem()] + [vmem()] * 6,
        out_specs=vmem(),
        scratch_shapes=[
            pltpu.VMEM((SLOT_CAP, 16, verts), F32),
            pltpu.VMEM((SLOT_CAP, 8, verts), F32),
        ]
        + sample_scratch(extent, verts),
        compiler_params=settings(12),
        cost_estimate=cost(1024 * MIB, 4 * MIB),
        name="sample_return",
    )(place, table, unit, near, x_halo, y_plus, y_minus)


def stream_kernel(
    post_hbm, xr_ref, yrp_ref, yrm_ref, zrp_ref, zrm_ref, read_hbm, post, read, shifted_rows, in_sem, out_sem
):
    _, size_x, size_y, size_z = post.shape
    y_halo = {1: yrp_ref, -1: yrm_ref}
    z_halo = {1: zrp_ref, -1: zrm_ref}
    loads = [pltpu.make_async_copy(post_hbm.at[q], post.at[q], in_sem.at[q]) for q in range(19)]
    stores = [pltpu.make_async_copy(read.at[q], read_hbm.at[q], out_sem.at[q]) for q in range(19)]
    for load in loads:
        load.start()
    lane = lax.broadcasted_iota(jnp.int32, (size_y, size_z), 1)
    row = lax.broadcasted_iota(jnp.int32, (size_y, size_z), 0)

    def shift_z(plane, cz, place):
        moved = pltpu.roll(plane, cz % size_z, 1)
        if place is None:
            return moved
        target = 0 if cz > 0 else size_z - 1
        column = pltpu.roll(z_halo[cz][...], (target - place + size_z) & (size_z - 1), 1)
        return jnp.where(lane == target, column, moved)

    for q in range(19):
        cx, cy, cz = VELOCITIES[q]
        rows = None
        if cy != 0:
            rows = y_halo[cy][Y_LISTS[cy].index(q)]
            if cz != 0:
                rows = shift_z(rows, cz, None)
        loads[q].wait()

        def put(x, plane, line, place):
            if cz != 0:
                plane = shift_z(plane, cz, place)
            if cy != 0:
                moved = pltpu.roll(plane, cy % size_y, 0)
                target = 0 if cy > 0 else size_y - 1
                plane = moved
                if line is not None:
                    line = jnp.broadcast_to(line, moved.shape)
                    plane = jnp.where(row == target, line, moved)
            read[q, x] = plane

        if rows is not None:
            shifted_rows[...] = rows

        @pl.loop(max(cx, 0), size_x + min(cx, 0), unroll=UNROLL)
        def _(x):
            source = x - cx
            line = None if cy == 0 else shifted_rows[pl.ds(source, 1), :]
            place = None if cz == 0 else Z_LISTS[cz].index(q) * 16 + source
            put(x, post[q, source], line, place)

        if cx != 0:
            put(0 if cx > 0 else size_x - 1, x_plane(xr_ref, q), None, None)
        stores[q].start()
    for store in stores:
        store.wait()


def stream(post, x_halo, y_plus, y_minus, z_plus, z_minus):
    anyspace = pl.BlockSpec(memory_space=pl.ANY)
    return pl.pallas_call(
        stream_kernel,
        out_shape=jax.ShapeDtypeStruct(post.shape, F32),
        in_specs=[anyspace] + [vmem()] * 5,
        out_specs=anyspace,
        scratch_shapes=[
            pltpu.VMEM(post.shape, F32),
            pltpu.VMEM(post.shape, F32),
            pltpu.VMEM(post.shape[1:4:2], F32),
            pltpu.SemaphoreType.DMA((19,)),
            pltpu.SemaphoreType.DMA((19,)),
        ],
        compiler_params=settings(10),
        cost_estimate=cost(MIB, 16 * MIB),
        name="stream_populations",
    )(post, x_halo, y_plus, y_minus, z_plus, z_minus)


def finish_kernel(
    extent,
    place_ref,
    inter_ref,
    base_ref,
    rank_ref,
    back_hbm,
    old_hbm,
    read_hbm,
    out_ref,
    back_ref,
    line_buf,
    xz_buf,
    yz_buf,
    in_sem,
    out_sem,
):
    size_x, size_y, size_z = extent
    patches, verts = rank_ref.shape[1:]
    gy, gz, ny, nz = [place_ref[n] for n in (4, 5, 7, 8)]
    lines = Y_EDGES[1] + Y_EDGES[-1]
    planes = Z_EDGES[1] + Z_EDGES[-1]
    xz = [q for q in planes if VELOCITIES[q][0] != 0]
    yz = [q for q in planes if VELOCITIES[q][0] == 0]
    moves = []
    for q in lines + xz + yz:
        cx, cy, _ = VELOCITIES[q]
        x = 0 if cx > 0 else size_x - 1
        y = 0 if cy > 0 else size_y - 8
        if q in lines:
            moves.append(((q, x, pl.ds(y, 8)), line_buf.at[lines.index(q)]))
        elif q in xz:
            moves.append(((q, x), xz_buf.at[xz.index(q)]))
        else:
            moves.append(((q, pl.ds(0, size_x), pl.ds(y, 8)), yz_buf.at[yz.index(q)]))
    loads = [
        pltpu.make_async_copy(old_hbm.at[piece], buf, in_sem.at[n])
        for n, (piece, buf) in enumerate(moves)
    ]
    stores = [
        pltpu.make_async_copy(buf, read_hbm.at[piece], out_sem.at[n])
        for n, (piece, buf) in enumerate(moves)
    ]
    load_back = pltpu.make_async_copy(back_hbm, back_ref, in_sem.at[12])
    load_back.start()
    for load in loads:
        load.start()
    load_back.wait()

    columns = {}
    for sign in (1, -1):
        source = gy * nz + lax.rem(gz - sign + nz, nz)
        block = [back_ref[source, e, 3:4, :] for e in range(4)]
        block = jnp.concatenate(block + [jnp.zeros((verts - 4, verts), F32)], axis=0)
        columns[sign] = jnp.transpose(block)[0:size_y]
    lane = lax.broadcasted_iota(jnp.int32, (size_y, size_z), 1)
    for load in loads:
        load.wait()
    for sign in (1, -1):
        source = lax.rem(gy - sign + ny, ny) * nz + gz
        for e, q in enumerate(Y_EDGES[sign]):
            line = 0 if sign > 0 else 7
            line_buf[lines.index(q), line : line + 1, :] = back_ref[source, e, 3:4, :]
        target = 0 if sign > 0 else size_z - 1
        for e, q in enumerate(Z_EDGES[sign]):
            column = pltpu.roll(columns[sign], (target - e) % size_z, 1)
            if q in xz:
                n = xz.index(q)
                xz_buf[n] = jnp.where(lane == target, column, xz_buf[n])
            else:
                n = yz.index(q)
                line = 0 if VELOCITIES[q][1] > 0 else 7
                for x in range(size_x):
                    old = yz_buf[n, x, line : line + 1, :]
                    new = jnp.where(lane[0:1] == target, column[x : x + 1], old)
                    yz_buf[n, x, line : line + 1, :] = new
    for store in stores:
        store.start()

    for p in range(patches):
        value = None
        for i in range(2):
            brick = inter_ref[i, p]
            base = base_ref[2 * p + i]
            rank = jnp.broadcast_to(rank_ref[i, p : p + 1, :], (8, verts))
            spot = rank + base
            block = lax.shift_right_logical(base, 7)
            other = jnp.minimum(block + 1, SLOT_CAP - 1)
            both = jnp.concatenate([back_ref[brick, block], back_ref[brick, other]], axis=0)
            picked = jnp.take_along_axis(both, spot & (verts - 1), axis=1)
            here = lax.shift_right_arithmetic(spot, 7)[0:3] == block
            picked = jnp.where(here, picked[0:3], picked[4:7])
            picked = jnp.where(rank[0:3] >= 0, picked, 0.0)
            value = picked if value is None else value + picked
        out_ref[:, p, :] = value
    for store in stores:
        store.wait()


def finish(place, intersection, bases, ranks, back, read):
    _, size_x, size_y, size_z = read.shape
    _, patches, verts = ranks.shape
    anyspace = pl.BlockSpec(memory_space=pl.ANY)
    return pl.pallas_call(
        functools.partial(finish_kernel, read.shape[1:]),
        out_shape=(
            jax.ShapeDtypeStruct(read.shape, F32),
            jax.ShapeDtypeStruct((3, patches, verts), F32),
        ),
        in_specs=[smem(), smem(), smem(), vmem(), anyspace, anyspace],
        out_specs=(anyspace, vmem()),
        scratch_shapes=[
            pltpu.VMEM(back.shape, F32),
            pltpu.VMEM((4, 8, size_z), F32),
            pltpu.VMEM((4, size_y, size_z), F32),
            pltpu.VMEM((4, size_x, 8, size_z), F32),
            pltpu.SemaphoreType.DMA((13,)),
            pltpu.SemaphoreType.DMA((12,)),
        ],
        input_output_aliases={5: 0},
        compiler_params=settings(6),
        name="finish",
    )(place, intersection, bases, ranks, back, read)


def shifted(value, axis, step):
    count = lax.axis_size(axis)
    return lax.ppermute(value, axis, [(i, (i + step) % count) for i in range(count)])


def exchanged(value):
    return lax.all_to_all(value, ("gy", "gz"), split_axis=0, concat_axis=0, tiled=True)


def body(populations, solid_flags, positions, anchors, base_cell, weights, intersection):
    extent = populations.shape[1:]
    axes = ("gx", "gy", "gz")
    bricks = lax.axis_size("gy") * lax.axis_size("gz")
    here = [lax.axis_index(axis) for axis in axes]
    place = jnp.stack(
        [here[d] * extent[d] for d in range(3)]
        + here
        + [jnp.int32(lax.axis_size(axis)) for axis in axes]
    ).astype(jnp.int32)
    lists = intersection.T
    near_out, far_out, ranks, bases = build_lists(
        lists,
        jnp.transpose(positions, (1, 0, 2)),
        jnp.transpose(anchors, (1, 0, 2)),
        jnp.transpose(base_cell, (1, 0, 2)),
        weights,
        bricks,
        lax.axis_size("gz"),
        extent,
    )
    near = exchanged(near_out)
    far = exchanged(far_out)
    total = spread_near(place, near, extent)
    post, x_face, y_plus, y_minus, z_plus, z_minus, unit = collide(
        place, far, total, populations, solid_flags
    )
    if lax.axis_size("gx") == 2:
        x_halo = shifted(x_face, "gx", 1)
    else:
        x_halo = jnp.concatenate(
            [shifted(x_face[:5], "gx", 1), shifted(x_face[5:], "gx", -1)], axis=0
        )
    y_plus = shifted(y_plus, "gy", 1)
    y_minus = shifted(y_minus, "gy", -1)
    z_plus = shifted(z_plus, "gz", 1)
    z_minus = shifted(z_minus, "gz", -1)
    sampled = sample_near(place, near, unit, extent)
    outgoing = sample_return(place, far, unit, sampled, x_halo, y_plus, y_minus, extent)
    back = exchanged(outgoing)
    read = stream(post, x_halo, y_plus, y_minus, z_plus, z_minus)
    read, velocity = finish(place, lists, bases, ranks, back, read)
    return read, jnp.transpose(velocity, (1, 0, 2))


def solution(mesh):
    return jax.shard_map(
        body,
        mesh=mesh,
        in_specs=(
            P(None, "gx", "gy", "gz"),
            P("gx", "gy", "gz"),
            P(("gx", "gy", "gz"), None, None),
            P(("gx", "gy", "gz"), None, None),
            P(("gx", "gy", "gz"), None, None),
            P(("gx", "gy", "gz"), None, None),
            P(("gx", "gy", "gz"), None),
        ),
        out_specs=(P(None, "gx", "gy", "gz"), P(("gx", "gy", "gz"), None, None)),
        check_vma=False,
    )
```

```python
import functools

import jax
import jax.numpy as jnp
from jax import lax
from jax.experimental import pallas as pl
from jax.experimental.pallas import tpu as pltpu
from jax.sharding import PartitionSpec as P

SLOT_CAP = 4
GROUPS = 7
EDGE_LANE = 80

RELAXATION = 0.8
TENSION = 0.05
TETHER = 0.5
VELOCITIES = [
    (0, 0, 0),
    (1, 0, 0),
    (-1, 0, 0),
    (0, 1, 0),
    (0, -1, 0),
    (0, 0, 1),
    (0, 0, -1),
    (1, 1, 0),
    (-1, -1, 0),
    (1, -1, 0),
    (-1, 1, 0),
    (1, 0, 1),
    (-1, 0, -1),
    (1, 0, -1),
    (-1, 0, 1),
    (0, 1, 1),
    (0, -1, -1),
    (0, 1, -1),
    (0, -1, 1),
]
LATTICE_WEIGHTS = [1.0 / 3.0] + [1.0 / 18.0] * 6 + [1.0 / 36.0] * 12


def crossing(axis, sign):
    return [q for q in range(19) if VELOCITIES[q][axis] == sign]


X_LISTS = {1: crossing(0, 1), -1: crossing(0, -1)}
Y_LISTS = {1: crossing(1, 1), -1: crossing(1, -1)}
Z_LISTS = {1: crossing(2, 1), -1: crossing(2, -1)}
Y_EDGES = {s: [q for q in Y_LISTS[s] if VELOCITIES[q][0] != 0] for s in (1, -1)}
Z_EDGES = {
    s: [q for q in Z_LISTS[s] if VELOCITIES[q][0] != 0 or VELOCITIES[q][1] != 0] for s in (1, -1)
}

BF = jnp.bfloat16
F32 = jnp.float32
MIB = 1024 * 1024
NT = (((1,), (1,)), ((), ()))
NN = (((1,), (0,)), ((), ()))


def settings(mib):
    return pltpu.CompilerParams(vmem_limit_bytes=mib * MIB)


def cost(flops, size):
    return pl.CostEstimate(flops=flops, bytes_accessed=size, transcendentals=0)


def vmem():
    return pl.BlockSpec(memory_space=pltpu.VMEM)


def smem():
    return pl.BlockSpec(memory_space=pltpu.SMEM)


def list_kernel(
    bricks_z,
    inter_ref,
    pos_ref,
    anchor_ref,
    cell_ref,
    weight_ref,
    out_ref,
    rank_ref,
    base_ref,
    payload,
    lists,
    count_ref,
    extent,
):
    patches, verts = pos_ref.shape[1:]
    bricks = out_ref.shape[0]
    pos = pos_ref[...]
    cycle_term = pltpu.roll(pos, 1, 2) + pltpu.roll(pos, verts - 1, 2) - 2.0 * pos
    forces = TENSION * cycle_term + TETHER * (anchor_ref[...] - pos)
    cells = cell_ref[...].astype(F32)
    payload[:, 0:8, :] = weight_ref[...]
    for p in range(patches):
        payload[p, 8:11, :] = forces[:, p, :]
        payload[p, 11:14, :] = cells[:, p, :] + 1.0
        payload[p, 14:16, :] = jnp.zeros((2, verts), F32)
    lists[...] = jnp.zeros(lists.shape, F32)

    @pl.loop(0, bricks)
    def _(b):
        count_ref[b] = 0

    lane = lax.broadcasted_iota(jnp.int32, (patches, verts), 1)
    row = lax.broadcasted_iota(jnp.int32, (patches, verts), 0)
    upper = (
        lax.broadcasted_iota(jnp.int32, (verts, verts), 0)
        <= lax.broadcasted_iota(jnp.int32, (verts, verts), 1)
    ).astype(F32)
    codes, sums = [], []
    for i in range(2):
        first_y = jnp.zeros((patches, verts), F32)
        first_z = jnp.zeros((patches, verts), F32)
        for p in range(patches):
            brick = inter_ref[i, p]
            first_y = jnp.where(row == p, (brick // bricks_z * extent[1]).astype(F32), first_y)
            first_z = jnp.where(row == p, (brick % bricks_z * extent[2]).astype(F32), first_z)
        live = (
            (cells[1] >= first_y)
            & (cells[1] < first_y + extent[1])
            & (cells[2] >= first_z)
            & (cells[2] < first_z + extent[2])
        )
        mask = live.astype(F32)
        total = jnp.dot(mask.astype(BF), upper.astype(BF), preferred_element_type=F32)
        rank = (total - mask).astype(jnp.int32)
        rank_ref[i] = jnp.where(live, rank, -1)
        code = jnp.where(live, (lane - rank) + lane * 256 + 65536, 0)
        step = 1
        while step < verts:
            moving = jnp.where((code & step) != 0, code, 0)
            code = (code - moving) + pltpu.roll(moving, verts - step, 1)
            step *= 2
        codes.append(code)
        sums.append(total)
    wide_lane = lax.broadcasted_iota(jnp.int32, (16, verts), 1)
    for p in range(patches):
        for i in range(2):
            brick = inter_ref[i, p]
            base = count_ref[brick]
            base_ref[2 * p + i] = base
            count_ref[brick] = base + jnp.max(sums[i][p : p + 1, :]).astype(jnp.int32)
            block = lax.shift_right_logical(base, 7)
            shift = base & (verts - 1)
            code = jnp.broadcast_to(codes[i][p : p + 1, :], (8, verts))
            code = pltpu.roll(code, shift, 1)
            code = jnp.concatenate([code, code], axis=0)
            source = lax.shift_right_logical(code, 8) & (verts - 1)
            moved = jnp.take_along_axis(payload[p], source, axis=1)
            moved = jnp.where(code >= 65536, moved, 0.0)
            lists[brick, block] += jnp.where(wide_lane >= shift, moved, 0.0)
            lists[brick, block + 1] += jnp.where(wide_lane < shift, moved, 0.0)

    @pl.loop(0, bricks)
    def _(b):
        for j in range(SLOT_CAP):
            value = lists[b, j]
            first = j // 2 * GROUPS
            for g in range(3):
                out_ref[b, first + j % 2 * 3 + g] = value[4 * g : 4 * g + 4]
            out_ref[b, first + 6, j % 2 * 2 : j % 2 * 2 + 2] = value[12:14]


def build_lists(intersection, positions, anchors, base_cell, weights, bricks, bricks_z, extent):
    _, patches, verts = positions.shape

    def kernel(*refs):
        list_kernel(bricks_z, *refs, extent)

    return pl.pallas_call(
        kernel,
        out_shape=(
            jax.ShapeDtypeStruct((bricks, 2 * GROUPS, 4, verts), F32),
            jax.ShapeDtypeStruct((2, patches, verts), jnp.int32),
            jax.ShapeDtypeStruct((2 * patches,), jnp.int32),
        ),
        in_specs=[smem(), vmem(), vmem(), vmem(), vmem()],
        out_specs=(vmem(), vmem(), smem()),
        scratch_shapes=[
            pltpu.VMEM((patches, 16, verts), F32),
            pltpu.VMEM((bricks, SLOT_CAP + 1, 16, verts), F32),
            pltpu.SMEM((bricks,), jnp.int32),
        ],
        compiler_params=settings(56),
        name="vertex_lists",
    )(intersection, positions, anchors, base_cell, weights)


def block_rows(table_ref, owner, j):
    first = j // 2 * GROUPS
    group = first + j % 2 * 3
    weight = jnp.concatenate([table_ref[owner, group], table_ref[owner, group + 1]], axis=0)
    third = table_ref[owner, group + 2]
    line = j % 2 * 2
    last = table_ref[owner, first + 6, line : line + 2]
    return weight, third[0:3], jnp.concatenate([third[3:4], last], axis=0)


def pack_far(table_ref, packed, spot_ref):
    owners, _, _, verts = table_ref.shape
    packed[...] = jnp.zeros(packed.shape, F32)
    lane = lax.broadcasted_iota(jnp.int32, (16, verts), 1)
    counts = []
    for owner in range(owners):
        for j in range(2):
            held = (table_ref[owner, GROUPS + 3 * j + 2, 3:4, :] > 0.0).astype(F32)
            counts.append(jnp.sum(held).astype(jnp.int32))
    spot = jnp.int32(0)
    for owner in range(owners):
        for j in range(2):
            count = counts[2 * owner + j]
            spot_ref[2 * owner + j] = spot

            @pl.when(count > 0)
            def _(owner=owner, j=j, spot=spot):
                weight, force, cells = block_rows(table_ref, owner, 2 + j)
                rows = jnp.concatenate(
                    [weight, force, cells, jnp.zeros((2, verts), F32)], axis=0
                )
                block = lax.shift_right_logical(spot, 7)
                shift = spot & (verts - 1)
                rows = pltpu.roll(rows, shift, 1)
                packed[block] += jnp.where(lane >= shift, rows, 0.0)
                packed[block + 1] += jnp.where(lane < shift, rows, 0.0)

            spot = spot + count
    spot_ref[2 * owners] = spot


def packed_blocks(spot, verts):
    return lax.shift_right_logical(spot + verts - 1, 7)


def packed_rows(packed, block):
    return packed[block, 0:8], packed[block, 8:11], packed[block, 11:14]


def place_rows(place_ref, rows, extent):
    weight, force, cells = rows
    local, inside = [], None
    for d in range(3):
        value = cells[d : d + 1] - (place_ref[d] + 1).astype(F32)
        ok = (value >= 0.0) & (value < float(extent[d]))
        inside = ok if inside is None else inside & ok
        local.append(value)
    weight = weight * jnp.broadcast_to(inside.astype(F32), weight.shape)
    return weight, force, local


def halves(value):
    high = value.astype(BF).astype(F32)
    return high, value - high


def spread_scratch(extent, verts):
    size_x, size_y, size_z = extent
    depth = SLOT_CAP * 2 * verts
    return [
        pltpu.VMEM((2, 2, size_x * size_y, depth), BF),
        pltpu.VMEM((2, 6 * size_z, depth), BF),
        pltpu.VMEM((2, SLOT_CAP, 16, verts), F32),
        pltpu.VMEM((2, SLOT_CAP, 8, verts), F32),
        pltpu.VMEM((2, SLOT_CAP, 8, verts), F32),
    ]


def spread_tools(place_ref, extent, verts, total, a_buf, zf_buf, w_rows, f_rows, c_rows):
    size_x, size_y, size_z = extent
    iota_y = lax.broadcasted_iota(jnp.int32, (16, verts), 0).astype(F32).astype(BF)
    zero = jnp.zeros((16, verts), BF)

    def wide(ref, slot, j, row):
        return jnp.broadcast_to(ref[slot, j, row : row + 1, :], (16, verts)).astype(BF)

    def build(blocks, slot):
        for j, rows in enumerate(blocks):
            weight, force, local = place_rows(place_ref, rows, extent)
            w_hi, w_lo = halves(weight)
            f_hi, f_lo = halves(force)
            w_rows[slot, j, 0:8] = w_hi
            w_rows[slot, j, 8:16] = w_lo
            f_rows[slot, j, 0:3] = f_hi
            f_rows[slot, j, 4:7] = f_lo
            for d in range(3):
                c_rows[slot, j, d : d + 1] = local[d]
        for j in range(len(blocks)):
            xl = wide(c_rows, slot, j, 0)
            yl = wide(c_rows, slot, j, 1)
            zl = wide(c_rows, slot, j, 2)
            at_y0 = iota_y == yl
            at_y1 = iota_y == yl + 1.0
            lines = {}
            for part in range(2):
                for dx in range(2):
                    for dz in range(2):
                        first = part * 8 + dx * 4 + dz
                        lines[part, dx, dz] = jnp.where(
                            at_y0,
                            wide(w_rows, slot, j, first),
                            jnp.where(at_y1, wide(w_rows, slot, j, first + 2), zero),
                        )
            before = None
            for x in range(size_x):
                here = xl == float(x)
                for part in range(2):
                    for dz in range(2):
                        value = jnp.where(here, lines[part, 0, dz], zero)
                        if before is not None:
                            value = jnp.where(before, lines[part, 1, dz], value)
                        column = (j * 2 + dz) * verts
                        a_buf[slot, part, x * 16 : (x + 1) * 16, column : column + verts] = value
                before = here
            force = [wide(f_rows, slot, j, part * 4 + c) for part in range(2) for c in range(3)]
            for zb in range(size_z // 16):
                for dz in range(2):
                    at_z = iota_y == zl + float(dz - 16 * zb)
                    column = (j * 2 + dz) * verts
                    for part in range(2):
                        for c in range(3):
                            line = (part * 3 + c) * size_z + zb * 16
                            zf_buf[slot, line : line + 16, column : column + verts] = jnp.where(
                                at_z, force[part * 3 + c], zero
                            )

    def product(slot, blocks=SLOT_CAP):
        lines = 3 * size_z
        depth = blocks * 2 * verts
        high = lax.dot_general(
            zf_buf[slot, :, :depth], a_buf[slot, 0, :, :depth], NT, preferred_element_type=F32
        )
        low = lax.dot_general(
            zf_buf[slot, :lines, :depth],
            a_buf[slot, 1, :, :depth],
            NT,
            preferred_element_type=F32,
        )
        total[...] += high[:lines] + high[lines:] + low

    return build, product


def pair_blocks(table_ref, step):
    return [block_rows(table_ref, 2 * step + oo, j) for oo in range(2) for j in range(2)]


def settle_kernel(pop, solid, base_ref, fluid_ref):
    keep = 1.0 - 1.0 / RELAXATION

    @pl.loop(0, solid.shape[0], unroll=2)
    def _(x):
        wall = solid[x] == 1
        fluid_ref[x] = jnp.where(wall, 0.0, 1.0)
        base_ref[0, x] = jnp.where(wall, pop[0, x], keep * pop[0, x])
        for q in range(1, 19, 2):
            one, two = pop[q, x], pop[q + 1, x]
            base_ref[q, x] = jnp.where(wall, two, keep * one)
            base_ref[q + 1, x] = jnp.where(wall, one, keep * two)


def settle(populations, solid):
    return pl.pallas_call(
        settle_kernel,
        out_shape=(
            jax.ShapeDtypeStruct(populations.shape, F32),
            jax.ShapeDtypeStruct(solid.shape, F32),
        ),
        in_specs=[vmem(), vmem()],
        out_specs=(vmem(), vmem()),
        compiler_params=settings(12),
        cost_estimate=cost(16 * MIB, 8 * MIB),
        name="settle",
    )(populations, solid)


def collide_kernel(
    place_ref,
    table_ref,
    base_ref,
    fluid_ref,
    post,
    xface_ref,
    yfp_ref,
    yfm_ref,
    zfp_ref,
    zfm_ref,
    unit_ref,
    packed,
    spot_ref,
    total,
    field,
    *scratch,
):
    _, size_x, size_y, size_z = post.shape
    owners, _, _, verts = table_ref.shape
    build, product = spread_tools(
        place_ref, (size_x, size_y, size_z), verts, total, *scratch
    )
    steps = owners // 2
    total[...] = jnp.zeros(total.shape, F32)
    pack_far(table_ref, packed, spot_ref)
    build(pair_blocks(table_ref, 0), 0)

    @pl.loop(0, steps // 2)
    def _(i):
        build(pair_blocks(table_ref, 2 * i + 1), 1)
        product(0)
        build(pair_blocks(table_ref, jnp.minimum(2 * i + 2, steps - 1)), 0)
        product(1)

    @pl.loop(0, packed_blocks(spot_ref[2 * owners], verts))
    def _(block):
        build([packed_rows(packed, block)], 0)
        product(0, 1)

    for c in range(3):
        for half in range(size_x * size_y // 128):
            field[c, half * 128 : (half + 1) * 128, :] = jnp.transpose(
                total[c * size_z : (c + 1) * size_z, half * 128 : (half + 1) * 128]
            )

    lane = lax.broadcasted_iota(jnp.int32, (size_y, size_z), 1)
    factor = 1.0 - 0.5 / RELAXATION
    rate = 1.0 / RELAXATION
    keep = 1.0 - rate

    def plane(x, z_out):
        z_out = dict(zip((1, -1), z_out))
        lines = pl.ds(pl.multiple_of(x * 16, 16), 16)
        force = [field[c, lines, :] for c in range(3)]
        fluid = fluid_ref[x]
        cells = [base_ref[q, x] for q in range(19)]
        rho = cells[0]
        for q in range(1, 19):
            rho = rho + cells[q]
        moment = []
        for c in range(3):
            value = None
            for q in range(1, 19, 2):
                if VELOCITIES[q][c] != 0:
                    term = cells[q] - cells[q + 1]
                    if VELOCITIES[q][c] < 0:
                        term = -term
                    value = term if value is None else value + term
            moment.append(value)
        rho = rho * jnp.where(fluid > 0.0, 1.0 / keep, 1.0)
        sign = jnp.where(fluid > 0.0, 1.0 / keep, -1.0)
        inverse = 1.0 / rho
        rho = rho * fluid
        vel = [(moment[c] * sign + 0.5 * force[c]) * inverse for c in range(3)]
        for c in range(3):
            high, low = halves(vel[c])
            first = pl.ds(pl.multiple_of((x * 3 + c) * 16, 16), 16)
            unit_ref[first, 0:size_z] = high.astype(BF)
            unit_ref[first, size_z : 2 * size_z] = low.astype(BF)
        speed = vel[0] * vel[0] + vel[1] * vel[1] + vel[2] * vel[2]
        u_dot_f = vel[0] * force[0] + vel[1] * force[1] + vel[2] * force[2]
        three = (3.0 * factor) * fluid
        nine = (9.0 * factor) * fluid
        rest = (rate * rho) * (1.0 - 1.5 * speed) - three * u_dot_f
        quad = (4.5 * rate) * rho
        linear = (3.0 * rate) * rho
        results = [None] * 19
        results[0] = cells[0] + LATTICE_WEIGHTS[0] * rest

        def along(vector, q):
            value = None
            for c in range(3):
                move = VELOCITIES[q][c]
                if move == 0:
                    continue
                if value is None:
                    value = vector[c] if move > 0 else -vector[c]
                else:
                    value = value + vector[c] if move > 0 else value - vector[c]
            return value

        for q in range(1, 19, 2):
            a = along(vel, q)
            b = along(force, q)
            weight = LATTICE_WEIGHTS[q]
            even = weight * (rest + a * (quad * a + nine * b))
            odd = weight * (linear * a + three * b)
            results[q] = cells[q] + (even + odd)
            results[q + 1] = cells[q + 1] + (even - odd)
        for q in range(19):
            post[q, x] = results[q]
        for sign, line, face in ((1, size_y - 1, yfp_ref), (-1, 0, yfm_ref)):
            for k, q in enumerate(Y_LISTS[sign]):
                face[k, pl.ds(x, 1), :] = results[q][line : line + 1, :]
        for sign, column in ((1, size_z - 1), (-1, 0)):
            for k, q in enumerate(Z_LISTS[sign]):
                place = k * 16 + x
                moved = pltpu.roll(results[q], (place - column + size_z) & (size_z - 1), 1)
                z_out[sign] = jnp.where(lane == place, moved, z_out[sign])
        return z_out[1], z_out[-1]

    empty = jnp.zeros((size_y, size_z), F32)
    zfp_ref[...], zfm_ref[...] = lax.fori_loop(0, size_x, plane, (empty, empty), unroll=2)
    for k, q in enumerate(X_LISTS[1]):
        xface_ref[k] = post[q, size_x - 1]
    for k, q in enumerate(X_LISTS[-1]):
        xface_ref[5 + k] = post[q, 0]


def collide(place, table, base, fluid):
    _, size_x, size_y, size_z = base.shape
    owners, _, _, verts = table.shape
    cross = size_x * size_y
    face_y = jax.ShapeDtypeStruct((5, size_x, size_z), F32)
    face_z = jax.ShapeDtypeStruct((size_y, size_z), F32)
    return pl.pallas_call(
        collide_kernel,
        out_shape=(
            jax.ShapeDtypeStruct(base.shape, F32),
            jax.ShapeDtypeStruct((10, size_y, size_z), F32),
            face_y,
            face_y,
            face_z,
            face_z,
            jax.ShapeDtypeStruct((cross * 3, 2 * size_z), BF),
            jax.ShapeDtypeStruct((2 * owners + 1, 16, verts), F32),
            jax.ShapeDtypeStruct((2 * owners + 1,), jnp.int32),
        ),
        in_specs=[smem()] + [vmem()] * 3,
        out_specs=(vmem(),) * 8 + (smem(),),
        scratch_shapes=[
            pltpu.VMEM((3 * size_z, cross), F32),
            pltpu.VMEM((3, cross, size_z), F32),
        ]
        + spread_scratch((size_x, size_y, size_z), verts),
        compiler_params=settings(24),
        cost_estimate=cost(6 * owners * 3 * size_z * cross * 4 * verts, 6 * MIB),
        name="spread_collide",
    )(place, table, base, fluid)


def sample_scratch(extent, verts):
    size_x, size_y, size_z = extent
    return [
        pltpu.VMEM((2, SLOT_CAP, 2 * size_z, 2 * verts), BF),
        pltpu.VMEM((2, 3 * size_x * size_y, 2 * verts), F32),
        pltpu.VMEM((2, SLOT_CAP, 8, verts), F32),
        pltpu.VMEM((2, SLOT_CAP, 8, verts), F32),
    ]


def sample_tools(place_ref, unit_ref, extent, verts, hot, grid_buf, w_rows, c_rows):
    size_x, size_y, size_z = extent
    iota_y = lax.broadcasted_iota(jnp.int32, (16, verts), 0).astype(F32)
    iota_b = iota_y.astype(BF)
    one = jnp.ones((16, verts), BF)
    zero_b = jnp.zeros((16, verts), BF)
    zero = jnp.zeros((16, verts), F32)

    def wide(ref, slot, j, row):
        return jnp.broadcast_to(ref[slot, j, row : row + 1, :], (16, verts))

    def prepare(blocks, slot):
        for j, rows in enumerate(blocks):
            weight, _, local = place_rows(place_ref, rows, extent)
            w_rows[slot, j] = weight
            for d in range(3):
                c_rows[slot, j, d : d + 1] = local[d]
        for j in range(len(blocks)):
            zl = wide(c_rows, slot, j, 2).astype(BF)
            for zb in range(size_z // 16):
                for dz in range(2):
                    value = jnp.where(iota_b == zl + float(dz - 16 * zb), one, zero_b)
                    for part in range(2):
                        line = part * size_z + zb * 16
                        hot[slot, j, line : line + 16, dz * verts : (dz + 1) * verts] = value

    def product(slot, j):
        grid_buf[j % 2] = lax.dot_general(unit_ref[...], hot[slot, j], NN, preferred_element_type=F32)

    def select(slot, j):
        xl = wide(c_rows, slot, j, 0)
        yl = wide(c_rows, slot, j, 1)
        at_y0 = iota_y == yl
        at_y1 = iota_y == yl + 1.0
        lines = {}
        for dx in range(2):
            for dz in range(2):
                first = dx * 4 + dz
                lines[dx, dz] = jnp.where(
                    at_y0,
                    wide(w_rows, slot, j, first),
                    jnp.where(at_y1, wide(w_rows, slot, j, first + 2), zero),
                )
        sums = [zero, zero, zero]
        before = None
        for x in range(size_x):
            here = xl == float(x)
            for dz in range(2):
                value = jnp.where(here, lines[0, dz], zero)
                if before is not None:
                    value = jnp.where(before, lines[1, dz], value)
                for c in range(3):
                    first = (x * 3 + c) * 16
                    part = grid_buf[j % 2, first : first + 16, dz * verts : (dz + 1) * verts]
                    sums[c] = sums[c] + value * part
            before = here
        return [jnp.sum(value, axis=0, keepdims=True) for value in sums]

    def work(slot, store):
        product(slot, 0)
        for j in range(SLOT_CAP):
            if j + 1 < SLOT_CAP:
                product(slot, j + 1)
            store(j, select(slot, j))

    return prepare, product, select, work


def x_plane(xr_ref, q):
    sign = VELOCITIES[q][0]
    return xr_ref[(0 if sign > 0 else 5) + X_LISTS[sign].index(q)]


def sample_kernel(extent, place_ref, spot_ref, table_ref, packed, unit_ref, out_ref, found, *scratch):
    owners, _, _, verts = table_ref.shape
    prepare, product, select, work = sample_tools(place_ref, unit_ref, extent, verts, *scratch)
    steps = owners // 2
    out_ref[...] = jnp.zeros(out_ref.shape, F32)

    def store(step):
        def put(j, values):
            for c in range(3):
                out_ref[2 * step + j // 2, j % 2, c : c + 1, :] = values[c]

        return put

    prepare(pair_blocks(table_ref, 0), 0)

    @pl.loop(0, steps // 2)
    def _(i):
        prepare(pair_blocks(table_ref, 2 * i + 1), 1)
        work(0, store(2 * i))
        prepare(pair_blocks(table_ref, jnp.minimum(2 * i + 2, steps - 1)), 0)
        work(1, store(2 * i + 1))

    @pl.loop(0, packed_blocks(spot_ref[2 * owners], verts))
    def _(block):
        prepare([packed_rows(packed, block)], 0)
        product(0, 0)
        values = select(0, 0)
        for c in range(3):
            found[block, c : c + 1, :] = values[c]

    lane = lax.broadcasted_iota(jnp.int32, (4, verts), 1)
    for owner in range(owners):
        for j in range(2):
            spot = spot_ref[2 * owner + j]

            @pl.when(spot_ref[2 * owner + j + 1] > spot)
            def _(owner=owner, j=j, spot=spot):
                block = lax.shift_right_logical(spot, 7)
                shift = spot & (verts - 1)
                back = (verts - shift) & (verts - 1)
                first = pltpu.roll(found[block, 0:4], back, 1)
                second = pltpu.roll(found[block + 1, 0:4], back, 1)
                value = jnp.where(lane < verts - shift, first, second)
                out_ref[owner, 2 + j, 0:3, :] = value[0:3]


def sample(place, spots, table, packed, unit, extent):
    owners, _, _, verts = table.shape
    size_x, size_y, size_z = extent
    return pl.pallas_call(
        functools.partial(sample_kernel, extent),
        out_shape=jax.ShapeDtypeStruct((owners, SLOT_CAP, 4, verts), F32),
        in_specs=[smem(), smem()] + [vmem()] * 3,
        out_specs=vmem(),
        scratch_shapes=[pltpu.VMEM((2 * owners + 2, 8, verts), F32)]
        + sample_scratch(extent, verts),
        compiler_params=settings(12),
        cost_estimate=cost(16 * owners * 3 * size_x * size_y * size_z * verts, MIB),
        name="sample_velocity",
    )(place, spots, table, packed, unit)


def y_message_kernel(xr_ref, yfp_ref, yfm_ref, plus_ref, minus_ref):
    size_y = xr_ref.shape[1]
    for sign, face, out in ((1, yfp_ref, plus_ref), (-1, yfm_ref, minus_ref)):
        out[0:5] = face[...]
        line = size_y - 1 if sign > 0 else 0
        for e, q in enumerate(Y_EDGES[sign]):
            out[5, e : e + 1, :] = x_plane(xr_ref, q)[line : line + 1, :]


def y_messages(x_halo, y_plus, y_minus):
    shape = jax.ShapeDtypeStruct((6,) + y_plus.shape[1:], F32)
    return pl.pallas_call(
        y_message_kernel,
        out_shape=(shape, shape),
        in_specs=[vmem()] * 3,
        out_specs=(vmem(), vmem()),
        compiler_params=settings(4),
        name="y_messages",
    )(x_halo, y_plus, y_minus)


def z_message_kernel(xr_ref, yrp_ref, yrm_ref, zfp_ref, zfm_ref, plus_ref, minus_ref):
    size_y, size_z = zfp_ref.shape
    y_halo = {1: yrp_ref, -1: yrm_ref}
    lane = lax.broadcasted_iota(jnp.int32, (size_y, size_z), 1)
    for sign, face, out in ((1, zfp_ref, plus_ref), (-1, zfm_ref, minus_ref)):
        column = size_z - 1 if sign > 0 else 0
        block = face[...]
        for e, q in enumerate(Z_EDGES[sign]):
            if VELOCITIES[q][0] != 0:
                plane = x_plane(xr_ref, q)
            else:
                y_sign = VELOCITIES[q][1]
                plane = y_halo[y_sign][Y_LISTS[y_sign].index(q)]
            spot = EDGE_LANE + e
            block = jnp.where(lane == spot, pltpu.roll(plane, (spot - column) % size_z, 1), block)
        out[...] = block


def z_messages(x_halo, y_plus, y_minus, z_plus, z_minus):
    shape = jax.ShapeDtypeStruct(z_plus.shape, F32)
    return pl.pallas_call(
        z_message_kernel,
        out_shape=(shape, shape),
        in_specs=[vmem()] * 5,
        out_specs=(vmem(), vmem()),
        compiler_params=settings(4),
        name="z_messages",
    )(x_halo, y_plus, y_minus, z_plus, z_minus)


def stream_kernel(
    post,
    xr_ref,
    yrp_ref,
    yrm_ref,
    zrp_ref,
    zrm_ref,
    read_hbm,
    read,
    out_sem,
):
    _, size_x, size_y, size_z = post.shape
    y_halo = {1: yrp_ref, -1: yrm_ref}
    z_halo = {1: zrp_ref, -1: zrm_ref}
    stores = [pltpu.make_async_copy(read.at[q], read_hbm.at[q], out_sem.at[q]) for q in range(19)]
    lane = lax.broadcasted_iota(jnp.int32, (size_y, size_z), 1)
    row = lax.broadcasted_iota(jnp.int32, (size_y, size_z), 0)

    def shift_z(plane, cz, place):
        moved = pltpu.roll(plane, cz % size_z, 1)
        target = 0 if cz > 0 else size_z - 1
        column = pltpu.roll(z_halo[cz][...], (target - place) % size_z, 1)
        return jnp.where(lane == target, column, moved)

    for q in range(19):
        cx, cy, cz = VELOCITIES[q]
        rows = None
        if cy != 0:
            rows = y_halo[cy][Y_LISTS[cy].index(q)]
            if cz != 0:
                rows = shift_z(rows, cz, EDGE_LANE + Z_EDGES[cz].index(q))
        for x in range(size_x):
            source = x - cx
            outside = source < 0 or source >= size_x
            plane = x_plane(xr_ref, q) if outside else post[q, source]
            if cz != 0:
                if outside:
                    place = EDGE_LANE + Z_EDGES[cz].index(q)
                else:
                    place = Z_LISTS[cz].index(q) * 16 + source
                plane = shift_z(plane, cz, place)
            if cy != 0:
                moved = pltpu.roll(plane, cy % size_y, 0)
                target = 0 if cy > 0 else size_y - 1
                if outside:
                    e = Y_EDGES[cy].index(q)
                    line = y_halo[cy][5, e : e + 1, :]
                else:
                    line = rows[source : source + 1, :]
                plane = jnp.where(row == target, jnp.broadcast_to(line, moved.shape), moved)
            read[q, x] = plane
        stores[q].start()
    for store in stores:
        store.wait()


def stream(post, x_halo, y_plus, y_minus, z_plus, z_minus):
    anyspace = pl.BlockSpec(memory_space=pl.ANY)
    return pl.pallas_call(
        stream_kernel,
        out_shape=jax.ShapeDtypeStruct(post.shape, F32),
        in_specs=[vmem()] * 6,
        out_specs=anyspace,
        scratch_shapes=[
            pltpu.VMEM(post.shape, F32),
            pltpu.SemaphoreType.DMA((19,)),
        ],
        compiler_params=settings(10),
        cost_estimate=cost(MIB, 16 * MIB),
        name="stream_populations",
    )(post, x_halo, y_plus, y_minus, z_plus, z_minus)


def collect_kernel(inter_ref, base_ref, rank_ref, back_ref, out_ref):
    patches, verts = rank_ref.shape[1:]
    for p in range(patches):
        value = None
        for i in range(2):
            brick = inter_ref[i, p]
            base = base_ref[2 * p + i]
            rank = jnp.broadcast_to(rank_ref[i, p : p + 1, :], (8, verts))
            spot = rank + base
            block = lax.shift_right_logical(base, 7)
            other = jnp.minimum(block + 1, SLOT_CAP - 1)
            both = jnp.concatenate([back_ref[brick, block], back_ref[brick, other]], axis=0)
            picked = jnp.take_along_axis(both, spot & (verts - 1), axis=1)
            here = lax.shift_right_arithmetic(spot, 7)[0:3] == block
            picked = jnp.where(here, picked[0:3], picked[4:7])
            picked = jnp.where(rank[0:3] >= 0, picked, 0.0)
            value = picked if value is None else value + picked
        out_ref[:, p, :] = value


def collect(intersection, bases, ranks, back):
    _, patches, verts = ranks.shape
    return pl.pallas_call(
        collect_kernel,
        out_shape=jax.ShapeDtypeStruct((3, patches, verts), F32),
        in_specs=[smem()] * 2 + [vmem()] * 2,
        out_specs=vmem(),
        compiler_params=settings(4),
        name="collect_velocity",
    )(intersection, bases, ranks, back)


def shifted(value, axis, step):
    count = lax.axis_size(axis)
    return lax.ppermute(value, axis, [(i, (i + step) % count) for i in range(count)])


def exchanged(value):
    return lax.all_to_all(value, ("gy", "gz"), split_axis=0, concat_axis=0, tiled=True)


def body(populations, solid_flags, positions, anchors, base_cell, weights, intersection):
    extent = populations.shape[1:]
    axes = ("gx", "gy", "gz")
    bricks = lax.axis_size("gy") * lax.axis_size("gz")
    here = [lax.axis_index(axis) for axis in axes]
    place = jnp.stack(
        [here[d] * extent[d] for d in range(3)]
        + here
        + [jnp.int32(lax.axis_size(axis)) for axis in axes]
    ).astype(jnp.int32)
    lists = intersection.T
    outgoing, ranks, bases = build_lists(
        lists,
        jnp.transpose(positions, (1, 0, 2)),
        jnp.transpose(anchors, (1, 0, 2)),
        jnp.transpose(base_cell, (1, 0, 2)),
        weights,
        bricks,
        lax.axis_size("gz"),
        extent,
    )
    table = exchanged(outgoing)
    base, fluid = settle(populations, solid_flags)
    post, x_face, y_plus, y_minus, z_plus, z_minus, unit, packed, spots = collide(
        place, table, base, fluid
    )
    if lax.axis_size("gx") == 2:
        x_halo = shifted(x_face, "gx", 1)
    else:
        x_halo = jnp.concatenate(
            [shifted(x_face[:5], "gx", 1), shifted(x_face[5:], "gx", -1)], axis=0
        )
    sampled = sample(place, spots, table, packed, unit, extent)
    back = exchanged(sampled)
    y_plus, y_minus = y_messages(x_halo, y_plus, y_minus)
    y_plus = shifted(y_plus, "gy", 1)
    y_minus = shifted(y_minus, "gy", -1)
    z_plus, z_minus = z_messages(x_halo, y_plus, y_minus, z_plus, z_minus)
    z_plus = shifted(z_plus, "gz", 1)
    z_minus = shifted(z_minus, "gz", -1)
    read = stream(post, x_halo, y_plus, y_minus, z_plus, z_minus)
    velocity = collect(lists, bases, ranks, back)
    return read, jnp.transpose(velocity, (1, 0, 2))


def solution(mesh):
    return jax.shard_map(
        body,
        mesh=mesh,
        in_specs=(
            P(None, "gx", "gy", "gz"),
            P("gx", "gy", "gz"),
            P(("gx", "gy", "gz"), None, None),
            P(("gx", "gy", "gz"), None, None),
            P(("gx", "gy", "gz"), None, None),
            P(("gx", "gy", "gz"), None, None),
            P(("gx", "gy", "gz"), None),
        ),
        out_specs=(P(None, "gx", "gy", "gz"), P(("gx", "gy", "gz"), None, None)),
        check_vma=False,
    )
```

```python
import functools

import jax
import jax.numpy as jnp
from jax import lax
from jax.experimental import pallas as pl
from jax.experimental.pallas import tpu as pltpu
from jax.sharding import PartitionSpec as P

SLOT_CAP = 4
GROUPS = 7
EDGE_LANE = 80

RELAXATION = 0.8
TENSION = 0.05
TETHER = 0.5
VELOCITIES = [
    (0, 0, 0),
    (1, 0, 0),
    (-1, 0, 0),
    (0, 1, 0),
    (0, -1, 0),
    (0, 0, 1),
    (0, 0, -1),
    (1, 1, 0),
    (-1, -1, 0),
    (1, -1, 0),
    (-1, 1, 0),
    (1, 0, 1),
    (-1, 0, -1),
    (1, 0, -1),
    (-1, 0, 1),
    (0, 1, 1),
    (0, -1, -1),
    (0, 1, -1),
    (0, -1, 1),
]
LATTICE_WEIGHTS = [1.0 / 3.0] + [1.0 / 18.0] * 6 + [1.0 / 36.0] * 12


def crossing(axis, sign):
    return [q for q in range(19) if VELOCITIES[q][axis] == sign]


X_LISTS = {1: crossing(0, 1), -1: crossing(0, -1)}
Y_LISTS = {1: crossing(1, 1), -1: crossing(1, -1)}
Z_LISTS = {1: crossing(2, 1), -1: crossing(2, -1)}
Y_EDGES = {s: [q for q in Y_LISTS[s] if VELOCITIES[q][0] != 0] for s in (1, -1)}
Z_EDGES = {
    s: [q for q in Z_LISTS[s] if VELOCITIES[q][0] != 0 or VELOCITIES[q][1] != 0] for s in (1, -1)
}

BF = jnp.bfloat16
F32 = jnp.float32
MIB = 1024 * 1024
NT = (((1,), (1,)), ((), ()))
NN = (((1,), (0,)), ((), ()))


def settings(mib):
    return pltpu.CompilerParams(vmem_limit_bytes=mib * MIB)


def cost(flops, size):
    return pl.CostEstimate(flops=flops, bytes_accessed=size, transcendentals=0)


def vmem():
    return pl.BlockSpec(memory_space=pltpu.VMEM)


def smem():
    return pl.BlockSpec(memory_space=pltpu.SMEM)


def list_kernel(
    bricks_z,
    inter_ref,
    pos_ref,
    anchor_ref,
    cell_ref,
    weight_ref,
    out_ref,
    rank_ref,
    base_ref,
    payload,
    lists,
    count_ref,
    extent,
):
    patches, verts = pos_ref.shape[1:]
    bricks = out_ref.shape[0]
    pos = pos_ref[...]
    cycle_term = pltpu.roll(pos, 1, 2) + pltpu.roll(pos, verts - 1, 2) - 2.0 * pos
    forces = TENSION * cycle_term + TETHER * (anchor_ref[...] - pos)
    cells = cell_ref[...].astype(F32)
    payload[:, 0:8, :] = weight_ref[...]
    for p in range(patches):
        payload[p, 8:11, :] = forces[:, p, :]
        payload[p, 11:14, :] = cells[:, p, :] + 1.0
        payload[p, 14:16, :] = jnp.zeros((2, verts), F32)
    lists[...] = jnp.zeros(lists.shape, F32)

    @pl.loop(0, bricks)
    def _(b):
        count_ref[b] = 0

    lane = lax.broadcasted_iota(jnp.int32, (patches, verts), 1)
    row = lax.broadcasted_iota(jnp.int32, (patches, verts), 0)
    upper = (
        lax.broadcasted_iota(jnp.int32, (verts, verts), 0)
        <= lax.broadcasted_iota(jnp.int32, (verts, verts), 1)
    ).astype(F32)
    codes, sums = [], []
    for i in range(2):
        first_y = jnp.zeros((patches, verts), F32)
        first_z = jnp.zeros((patches, verts), F32)
        for p in range(patches):
            brick = inter_ref[i, p]
            first_y = jnp.where(row == p, (brick // bricks_z * extent[1]).astype(F32), first_y)
            first_z = jnp.where(row == p, (brick % bricks_z * extent[2]).astype(F32), first_z)
        live = (
            (cells[1] >= first_y)
            & (cells[1] < first_y + extent[1])
            & (cells[2] >= first_z)
            & (cells[2] < first_z + extent[2])
        )
        mask = live.astype(F32)
        total = jnp.dot(mask.astype(BF), upper.astype(BF), preferred_element_type=F32)
        rank = (total - mask).astype(jnp.int32)
        rank_ref[i] = jnp.where(live, rank, -1)
        code = jnp.where(live, (lane - rank) + lane * 256 + 65536, 0)
        step = 1
        while step < verts:
            moving = jnp.where((code & step) != 0, code, 0)
            code = (code - moving) + pltpu.roll(moving, verts - step, 1)
            step *= 2
        codes.append(code)
        sums.append(total)
    wide_lane = lax.broadcasted_iota(jnp.int32, (16, verts), 1)
    for p in range(patches):
        for i in range(2):
            brick = inter_ref[i, p]
            base = count_ref[brick]
            base_ref[2 * p + i] = base
            count_ref[brick] = base + jnp.max(sums[i][p : p + 1, :]).astype(jnp.int32)
            block = lax.shift_right_logical(base, 7)
            shift = base & (verts - 1)
            code = jnp.broadcast_to(codes[i][p : p + 1, :], (8, verts))
            code = pltpu.roll(code, shift, 1)
            code = jnp.concatenate([code, code], axis=0)
            source = lax.shift_right_logical(code, 8) & (verts - 1)
            moved = jnp.take_along_axis(payload[p], source, axis=1)
            moved = jnp.where(code >= 65536, moved, 0.0)
            lists[brick, block] += jnp.where(wide_lane >= shift, moved, 0.0)
            lists[brick, block + 1] += jnp.where(wide_lane < shift, moved, 0.0)

    @pl.loop(0, bricks)
    def _(b):
        for j in range(SLOT_CAP):
            value = lists[b, j]
            first = j // 2 * GROUPS
            for g in range(3):
                out_ref[b, first + j % 2 * 3 + g] = value[4 * g : 4 * g + 4]
            out_ref[b, first + 6, j % 2 * 2 : j % 2 * 2 + 2] = value[12:14]


def build_lists(intersection, positions, anchors, base_cell, weights, bricks, bricks_z, extent):
    _, patches, verts = positions.shape

    def kernel(*refs):
        list_kernel(bricks_z, *refs, extent)

    return pl.pallas_call(
        kernel,
        out_shape=(
            jax.ShapeDtypeStruct((bricks, 2 * GROUPS, 4, verts), F32),
            jax.ShapeDtypeStruct((2, patches, verts), jnp.int32),
            jax.ShapeDtypeStruct((2 * patches,), jnp.int32),
        ),
        in_specs=[smem(), vmem(), vmem(), vmem(), vmem()],
        out_specs=(vmem(), vmem(), smem()),
        scratch_shapes=[
            pltpu.VMEM((patches, 16, verts), F32),
            pltpu.VMEM((bricks, SLOT_CAP + 1, 16, verts), F32),
            pltpu.SMEM((bricks,), jnp.int32),
        ],
        compiler_params=settings(56),
        name="vertex_lists",
    )(intersection, positions, anchors, base_cell, weights)


def block_rows(table_ref, owner, j):
    first = j // 2 * GROUPS
    group = first + j % 2 * 3
    weight = jnp.concatenate([table_ref[owner, group], table_ref[owner, group + 1]], axis=0)
    third = table_ref[owner, group + 2]
    line = j % 2 * 2
    last = table_ref[owner, first + 6, line : line + 2]
    return weight, third[0:3], jnp.concatenate([third[3:4], last], axis=0)


def pack_far(table_ref, packed, spot_ref):
    owners, _, _, verts = table_ref.shape
    packed[...] = jnp.zeros(packed.shape, F32)
    lane = lax.broadcasted_iota(jnp.int32, (16, verts), 1)
    counts = []
    for owner in range(owners):
        for j in range(2):
            held = (table_ref[owner, GROUPS + 3 * j + 2, 3:4, :] > 0.0).astype(F32)
            counts.append(jnp.sum(held).astype(jnp.int32))
    spot = jnp.int32(0)
    for owner in range(owners):
        for j in range(2):
            count = counts[2 * owner + j]
            spot_ref[2 * owner + j] = spot

            @pl.when(count > 0)
            def _(owner=owner, j=j, spot=spot):
                weight, force, cells = block_rows(table_ref, owner, 2 + j)
                rows = jnp.concatenate(
                    [weight, force, cells, jnp.zeros((2, verts), F32)], axis=0
                )
                block = lax.shift_right_logical(spot, 7)
                shift = spot & (verts - 1)
                rows = pltpu.roll(rows, shift, 1)
                packed[block] += jnp.where(lane >= shift, rows, 0.0)
                packed[block + 1] += jnp.where(lane < shift, rows, 0.0)

            spot = spot + count
    spot_ref[2 * owners] = spot


def packed_blocks(spot, verts):
    return lax.shift_right_logical(spot + verts - 1, 7)


def packed_rows(packed, block):
    return packed[block, 0:8], packed[block, 8:11], packed[block, 11:14]


def place_rows(place_ref, rows, extent):
    weight, force, cells = rows
    local, inside = [], None
    for d in range(3):
        value = cells[d : d + 1] - (place_ref[d] + 1).astype(F32)
        ok = (value >= 0.0) & (value < float(extent[d]))
        inside = ok if inside is None else inside & ok
        local.append(value)
    weight = weight * jnp.broadcast_to(inside.astype(F32), weight.shape)
    return weight, force, local


def halves(value):
    high = value.astype(BF).astype(F32)
    return high, value - high


def spread_scratch(extent, verts):
    size_x, size_y, size_z = extent
    depth = SLOT_CAP * 2 * verts
    return [
        pltpu.VMEM((2, 2, size_x * size_y, depth), BF),
        pltpu.VMEM((2, 6 * size_z, depth), BF),
        pltpu.VMEM((2, SLOT_CAP, 16, verts), F32),
        pltpu.VMEM((2, SLOT_CAP, 8, verts), F32),
        pltpu.VMEM((2, SLOT_CAP, 8, verts), F32),
    ]


def spread_tools(place_ref, extent, verts, total, a_buf, zf_buf, w_rows, f_rows, c_rows):
    size_x, size_y, size_z = extent
    iota_y = lax.broadcasted_iota(jnp.int32, (16, verts), 0).astype(F32).astype(BF)
    zero = jnp.zeros((16, verts), BF)

    def wide(ref, slot, j, row):
        return jnp.broadcast_to(ref[slot, j, row : row + 1, :], (16, verts)).astype(BF)

    def build(blocks, slot):
        for j, rows in enumerate(blocks):
            weight, force, local = place_rows(place_ref, rows, extent)
            w_hi, w_lo = halves(weight)
            f_hi, f_lo = halves(force)
            w_rows[slot, j, 0:8] = w_hi
            w_rows[slot, j, 8:16] = w_lo
            f_rows[slot, j, 0:3] = f_hi
            f_rows[slot, j, 4:7] = f_lo
            for d in range(3):
                c_rows[slot, j, d : d + 1] = local[d]
        for j in range(len(blocks)):
            xl = wide(c_rows, slot, j, 0)
            yl = wide(c_rows, slot, j, 1)
            zl = wide(c_rows, slot, j, 2)
            at_y0 = iota_y == yl
            at_y1 = iota_y == yl + 1.0
            lines = {}
            for part in range(2):
                for dx in range(2):
                    for dz in range(2):
                        first = part * 8 + dx * 4 + dz
                        lines[part, dx, dz] = jnp.where(
                            at_y0,
                            wide(w_rows, slot, j, first),
                            jnp.where(at_y1, wide(w_rows, slot, j, first + 2), zero),
                        )
            before = None
            for x in range(size_x):
                here = xl == float(x)
                for part in range(2):
                    for dz in range(2):
                        value = jnp.where(here, lines[part, 0, dz], zero)
                        if before is not None:
                            value = jnp.where(before, lines[part, 1, dz], value)
                        column = (j * 2 + dz) * verts
                        a_buf[slot, part, x * 16 : (x + 1) * 16, column : column + verts] = value
                before = here
            force = [wide(f_rows, slot, j, part * 4 + c) for part in range(2) for c in range(3)]
            for zb in range(size_z // 16):
                for dz in range(2):
                    at_z = iota_y == zl + float(dz - 16 * zb)
                    column = (j * 2 + dz) * verts
                    for part in range(2):
                        for c in range(3):
                            line = (part * 3 + c) * size_z + zb * 16
                            zf_buf[slot, line : line + 16, column : column + verts] = jnp.where(
                                at_z, force[part * 3 + c], zero
                            )

    def product(slot, blocks=SLOT_CAP):
        lines = 3 * size_z
        depth = blocks * 2 * verts
        high = lax.dot_general(
            zf_buf[slot, :, :depth], a_buf[slot, 0, :, :depth], NT, preferred_element_type=F32
        )
        low = lax.dot_general(
            zf_buf[slot, :lines, :depth],
            a_buf[slot, 1, :, :depth],
            NT,
            preferred_element_type=F32,
        )
        total[...] += high[:lines] + high[lines:] + low

    return build, product


def pair_blocks(table_ref, step):
    return [block_rows(table_ref, 2 * step + oo, j) for oo in range(2) for j in range(2)]


def spread_kernel(extent, place_ref, table_ref, total, packed, spot_ref, *scratch):
    owners, _, _, verts = table_ref.shape
    build, product = spread_tools(place_ref, extent, verts, total, *scratch)
    steps = owners // 2
    total[...] = jnp.zeros(total.shape, F32)
    pack_far(table_ref, packed, spot_ref)
    build(pair_blocks(table_ref, 0), 0)

    @pl.loop(0, steps // 2)
    def _(i):
        build(pair_blocks(table_ref, 2 * i + 1), 1)
        product(0)
        build(pair_blocks(table_ref, jnp.minimum(2 * i + 2, steps - 1)), 0)
        product(1)

    @pl.loop(0, packed_blocks(spot_ref[2 * owners], verts))
    def _(block):
        build([packed_rows(packed, block)], 0)
        product(0, 1)


def spread(place, table, extent):
    owners, _, _, verts = table.shape
    size_x, size_y, size_z = extent
    cross = size_x * size_y
    return pl.pallas_call(
        functools.partial(spread_kernel, extent),
        out_shape=(
            jax.ShapeDtypeStruct((3 * size_z, cross), F32),
            jax.ShapeDtypeStruct((2 * owners + 1, 16, verts), F32),
            jax.ShapeDtypeStruct((2 * owners + 1,), jnp.int32),
        ),
        in_specs=[smem(), vmem()],
        out_specs=(vmem(), vmem(), smem()),
        scratch_shapes=spread_scratch(extent, verts),
        compiler_params=settings(16),
        cost_estimate=cost(6 * owners * 3 * size_z * cross * 4 * verts, MIB),
        name="spread",
    )(place, table)


def collide_kernel(
    total,
    pop,
    solid,
    post,
    xface_ref,
    yfp_ref,
    yfm_ref,
    zfp_ref,
    zfm_ref,
    unit_ref,
    field,
):
    _, size_x, size_y, size_z = post.shape

    for c in range(3):
        for half in range(size_x * size_y // 128):
            field[c, half * 128 : (half + 1) * 128, :] = jnp.transpose(
                total[c * size_z : (c + 1) * size_z, half * 128 : (half + 1) * 128]
            )

    lane = lax.broadcasted_iota(jnp.int32, (size_y, size_z), 1)
    factor = 1.0 - 0.5 / RELAXATION
    rate = 1.0 / RELAXATION
    keep = 1.0 - rate

    def plane(x, z_out):
        z_out = dict(zip((1, -1), z_out))
        lines = pl.ds(pl.multiple_of(x * 16, 16), 16)
        force = [field[c, lines, :] for c in range(3)]
        cells = [pop[q, x] for q in range(19)]
        wall = solid[x] == 1
        rho = cells[0]
        for q in range(1, 19):
            rho = rho + cells[q]
        moment = []
        for c in range(3):
            value = None
            for q in range(1, 19, 2):
                if VELOCITIES[q][c] != 0:
                    term = cells[q] - cells[q + 1]
                    if VELOCITIES[q][c] < 0:
                        term = -term
                    value = term if value is None else value + term
            moment.append(value)
        inverse = 1.0 / rho
        vel = [(moment[c] + 0.5 * force[c]) * inverse for c in range(3)]
        for c in range(3):
            high, low = halves(vel[c])
            first = pl.ds(pl.multiple_of((x * 3 + c) * 16, 16), 16)
            unit_ref[first, 0:size_z] = high.astype(BF)
            unit_ref[first, size_z : 2 * size_z] = low.astype(BF)
        speed = vel[0] * vel[0] + vel[1] * vel[1] + vel[2] * vel[2]
        u_dot_f = vel[0] * force[0] + vel[1] * force[1] + vel[2] * force[2]
        three = 3.0 * factor
        nine = 9.0 * factor
        rest = (rate * rho) * (1.0 - 1.5 * speed) - three * u_dot_f
        quad = (4.5 * rate) * rho
        linear = (3.0 * rate) * rho
        results = [None] * 19
        results[0] = jnp.where(wall, cells[0], keep * cells[0] + LATTICE_WEIGHTS[0] * rest)

        def along(vector, q):
            value = None
            for c in range(3):
                move = VELOCITIES[q][c]
                if move == 0:
                    continue
                if value is None:
                    value = vector[c] if move > 0 else -vector[c]
                else:
                    value = value + vector[c] if move > 0 else value - vector[c]
            return value

        for q in range(1, 19, 2):
            a = along(vel, q)
            b = along(force, q)
            weight = LATTICE_WEIGHTS[q]
            even = weight * (rest + a * (quad * a + nine * b))
            odd = weight * (linear * a + three * b)
            results[q] = jnp.where(wall, cells[q + 1], keep * cells[q] + (even + odd))
            results[q + 1] = jnp.where(wall, cells[q], keep * cells[q + 1] + (even - odd))
        for q in range(19):
            post[q, x] = results[q]
        for sign, line, face in ((1, size_y - 1, yfp_ref), (-1, 0, yfm_ref)):
            for k, q in enumerate(Y_LISTS[sign]):
                face[k, pl.ds(x, 1), :] = results[q][line : line + 1, :]
        for sign, column in ((1, size_z - 1), (-1, 0)):
            for k, q in enumerate(Z_LISTS[sign]):
                place = k * 16 + x
                moved = pltpu.roll(results[q], (place - column + size_z) & (size_z - 1), 1)
                z_out[sign] = jnp.where(lane == place, moved, z_out[sign])
        return z_out[1], z_out[-1]

    empty = jnp.zeros((size_y, size_z), F32)
    zfp_ref[...], zfm_ref[...] = lax.fori_loop(0, size_x, plane, (empty, empty), unroll=2)
    for k, q in enumerate(X_LISTS[1]):
        xface_ref[k] = post[q, size_x - 1]
    for k, q in enumerate(X_LISTS[-1]):
        xface_ref[5 + k] = post[q, 0]


def collide(total, populations, solid):
    _, size_x, size_y, size_z = populations.shape
    cross = size_x * size_y
    face_y = jax.ShapeDtypeStruct((5, size_x, size_z), F32)
    face_z = jax.ShapeDtypeStruct((size_y, size_z), F32)
    return pl.pallas_call(
        collide_kernel,
        out_shape=(
            jax.ShapeDtypeStruct(populations.shape, F32),
            jax.ShapeDtypeStruct((10, size_y, size_z), F32),
            face_y,
            face_y,
            face_z,
            face_z,
            jax.ShapeDtypeStruct((cross * 3, 2 * size_z), BF),
        ),
        in_specs=[vmem()] * 3,
        out_specs=(vmem(),) * 7,
        scratch_shapes=[pltpu.VMEM((3, cross, size_z), F32)],
        compiler_params=settings(12),
        cost_estimate=cost(16 * MIB, 8 * MIB),
        name="collide",
    )(total, populations, solid)


def sample_scratch(extent, verts):
    size_x, size_y, size_z = extent
    return [
        pltpu.VMEM((2, SLOT_CAP, 2 * size_z, 2 * verts), BF),
        pltpu.VMEM((2, 3 * size_x * size_y, 2 * verts), F32),
        pltpu.VMEM((2, SLOT_CAP, 8, verts), F32),
        pltpu.VMEM((2, SLOT_CAP, 8, verts), F32),
    ]


def sample_tools(place_ref, unit_ref, extent, verts, hot, grid_buf, w_rows, c_rows):
    size_x, size_y, size_z = extent
    iota_y = lax.broadcasted_iota(jnp.int32, (16, verts), 0).astype(F32)
    iota_b = iota_y.astype(BF)
    one = jnp.ones((16, verts), BF)
    zero_b = jnp.zeros((16, verts), BF)
    zero = jnp.zeros((16, verts), F32)

    def wide(ref, slot, j, row):
        return jnp.broadcast_to(ref[slot, j, row : row + 1, :], (16, verts))

    def prepare(blocks, slot):
        for j, rows in enumerate(blocks):
            weight, _, local = place_rows(place_ref, rows, extent)
            w_rows[slot, j] = weight
            for d in range(3):
                c_rows[slot, j, d : d + 1] = local[d]
        for j in range(len(blocks)):
            zl = wide(c_rows, slot, j, 2).astype(BF)
            for zb in range(size_z // 16):
                for dz in range(2):
                    value = jnp.where(iota_b == zl + float(dz - 16 * zb), one, zero_b)
                    for part in range(2):
                        line = part * size_z + zb * 16
                        hot[slot, j, line : line + 16, dz * verts : (dz + 1) * verts] = value

    def product(slot, j):
        grid_buf[j % 2] = lax.dot_general(unit_ref[...], hot[slot, j], NN, preferred_element_type=F32)

    def select(slot, j):
        xl = wide(c_rows, slot, j, 0)
        yl = wide(c_rows, slot, j, 1)
        at_y0 = iota_y == yl
        at_y1 = iota_y == yl + 1.0
        lines = {}
        for dx in range(2):
            for dz in range(2):
                first = dx * 4 + dz
                lines[dx, dz] = jnp.where(
                    at_y0,
                    wide(w_rows, slot, j, first),
                    jnp.where(at_y1, wide(w_rows, slot, j, first + 2), zero),
                )
        sums = [zero, zero, zero]
        before = None
        for x in range(size_x):
            here = xl == float(x)
            for dz in range(2):
                value = jnp.where(here, lines[0, dz], zero)
                if before is not None:
                    value = jnp.where(before, lines[1, dz], value)
                for c in range(3):
                    first = (x * 3 + c) * 16
                    part = grid_buf[j % 2, first : first + 16, dz * verts : (dz + 1) * verts]
                    sums[c] = sums[c] + value * part
            before = here
        return [jnp.sum(value, axis=0, keepdims=True) for value in sums]

    def work(slot, store):
        product(slot, 0)
        for j in range(SLOT_CAP):
            if j + 1 < SLOT_CAP:
                product(slot, j + 1)
            store(j, select(slot, j))

    return prepare, product, select, work


def x_plane(xr_ref, q):
    sign = VELOCITIES[q][0]
    return xr_ref[(0 if sign > 0 else 5) + X_LISTS[sign].index(q)]


def sample_steps(table_ref, first, last, prepare, work, out_ref):
    def store(step):
        def put(j, values):
            for c in range(3):
                line = j % 2
                out_ref[2 * (step - first) + j // 2, c, line : line + 1, :] = values[c]

        return put

    prepare(pair_blocks(table_ref, first), 0)

    @pl.loop(0, (last - first) // 2)
    def _(i):
        step = first + 2 * i
        prepare(pair_blocks(table_ref, step + 1), 1)
        work(0, store(step))
        prepare(pair_blocks(table_ref, jnp.minimum(step + 2, last - 1)), 0)
        work(1, store(step + 1))


def sample_part_kernel(extent, first, last, place_ref, table_ref, unit_ref, *refs):
    out_ref, scratch = refs[-5], refs[-4:]
    verts = table_ref.shape[3]
    prepare, _, _, work = sample_tools(place_ref, unit_ref, extent, verts, *scratch)
    sample_steps(table_ref, first, last, prepare, work, out_ref)


def sample_part(place, table, unit, order, first, last, extent):
    owners, _, _, verts = table.shape
    size_x, size_y, size_z = extent
    return pl.pallas_call(
        functools.partial(sample_part_kernel, extent, first, last),
        out_shape=jax.ShapeDtypeStruct((2 * (last - first), 3, 2, verts), F32),
        in_specs=[smem(), vmem(), vmem()] + [pl.BlockSpec(memory_space=pl.ANY)] * len(order),
        out_specs=vmem(),
        scratch_shapes=sample_scratch(extent, verts),
        compiler_params=settings(12),
        cost_estimate=cost(
            32 * (last - first) * 3 * size_x * size_y * size_z * verts, MIB
        ),
        name="sample_part",
    )(place, table, unit, *order)


def sample_kernel(
    extent, place_ref, spot_ref, table_ref, packed, unit_ref, one_ref, two_ref, *refs
):
    out_ref, found, scratch = refs[-6], refs[-5], refs[-4:]
    owners, _, _, verts = table_ref.shape
    prepare, product, select, work = sample_tools(place_ref, unit_ref, extent, verts, *scratch)
    middle = one_ref.shape[0]
    done = middle + two_ref.shape[0]
    for c in range(3):
        out_ref[0:middle, c, 0:2] = one_ref[:, c]
        out_ref[middle:done, c, 0:2] = two_ref[:, c]
        out_ref[:, c, 2:4] = jnp.zeros((owners, 2, verts), F32)
    rest = out_ref.at[pl.ds(done, owners - done)]
    sample_steps(table_ref, done // 2, owners // 2, prepare, work, rest)

    @pl.loop(0, packed_blocks(spot_ref[2 * owners], verts))
    def _(block):
        prepare([packed_rows(packed, block)], 0)
        product(0, 0)
        values = select(0, 0)
        for c in range(3):
            found[block, c : c + 1, :] = values[c]

    lane = lax.broadcasted_iota(jnp.int32, (4, verts), 1)
    for owner in range(owners):
        for j in range(2):
            spot = spot_ref[2 * owner + j]

            @pl.when(spot_ref[2 * owner + j + 1] > spot)
            def _(owner=owner, j=j, spot=spot):
                block = lax.shift_right_logical(spot, 7)
                shift = spot & (verts - 1)
                back = (verts - shift) & (verts - 1)
                first = pltpu.roll(found[block, 0:4], back, 1)
                second = pltpu.roll(found[block + 1, 0:4], back, 1)
                value = jnp.where(lane < verts - shift, first, second)
                for c in range(3):
                    out_ref[owner, c, 2 + j : 3 + j, :] = value[c : c + 1]


def sample(place, spots, table, packed, unit, parts, order, extent):
    owners, _, _, verts = table.shape
    size_x, size_y, size_z = extent
    return pl.pallas_call(
        functools.partial(sample_kernel, extent),
        out_shape=jax.ShapeDtypeStruct((owners, 3, SLOT_CAP, verts), F32),
        in_specs=[smem(), smem()]
        + [vmem()] * 5
        + [pl.BlockSpec(memory_space=pl.ANY)] * len(order),
        out_specs=vmem(),
        scratch_shapes=[pltpu.VMEM((2 * owners + 2, 8, verts), F32)]
        + sample_scratch(extent, verts),
        compiler_params=settings(12),
        cost_estimate=cost(8 * owners * 3 * size_x * size_y * size_z * verts, MIB),
        name="sample_velocity",
    )(place, spots, table, packed, unit, *parts, *order)


def y_message_kernel(xr_ref, yfp_ref, yfm_ref, plus_ref, minus_ref):
    size_y = xr_ref.shape[1]
    for sign, face, out in ((1, yfp_ref, plus_ref), (-1, yfm_ref, minus_ref)):
        out[0:5] = face[...]
        line = size_y - 1 if sign > 0 else 0
        for e, q in enumerate(Y_EDGES[sign]):
            out[5, e : e + 1, :] = x_plane(xr_ref, q)[line : line + 1, :]


def y_messages(x_halo, y_plus, y_minus):
    shape = jax.ShapeDtypeStruct((6,) + y_plus.shape[1:], F32)
    return pl.pallas_call(
        y_message_kernel,
        out_shape=(shape, shape),
        in_specs=[vmem()] * 3,
        out_specs=(vmem(), vmem()),
        compiler_params=settings(4),
        name="y_messages",
    )(x_halo, y_plus, y_minus)


def z_message_kernel(xr_ref, yrp_ref, yrm_ref, zfp_ref, zfm_ref, plus_ref, minus_ref):
    size_y, size_z = zfp_ref.shape
    y_halo = {1: yrp_ref, -1: yrm_ref}
    lane = lax.broadcasted_iota(jnp.int32, (size_y, size_z), 1)
    for sign, face, out in ((1, zfp_ref, plus_ref), (-1, zfm_ref, minus_ref)):
        column = size_z - 1 if sign > 0 else 0
        block = face[...]
        for e, q in enumerate(Z_EDGES[sign]):
            if VELOCITIES[q][0] != 0:
                plane = x_plane(xr_ref, q)
            else:
                y_sign = VELOCITIES[q][1]
                plane = y_halo[y_sign][Y_LISTS[y_sign].index(q)]
            spot = EDGE_LANE + e
            block = jnp.where(lane == spot, pltpu.roll(plane, (spot - column) % size_z, 1), block)
        out[...] = block


def z_messages(x_halo, y_plus, y_minus, z_plus, z_minus):
    shape = jax.ShapeDtypeStruct(z_plus.shape, F32)
    return pl.pallas_call(
        z_message_kernel,
        out_shape=(shape, shape),
        in_specs=[vmem()] * 5,
        out_specs=(vmem(), vmem()),
        compiler_params=settings(4),
        name="z_messages",
    )(x_halo, y_plus, y_minus, z_plus, z_minus)


def stream_kernel(
    post,
    xr_ref,
    yrp_ref,
    yrm_ref,
    zrp_ref,
    zrm_ref,
    read_hbm,
    read,
    out_sem,
):
    _, size_x, size_y, size_z = post.shape
    y_halo = {1: yrp_ref, -1: yrm_ref}
    z_halo = {1: zrp_ref, -1: zrm_ref}
    stores = [pltpu.make_async_copy(read.at[q], read_hbm.at[q], out_sem.at[q]) for q in range(19)]
    lane = lax.broadcasted_iota(jnp.int32, (size_y, size_z), 1)
    row = lax.broadcasted_iota(jnp.int32, (size_y, size_z), 0)

    def shift_z(plane, cz, place):
        moved = pltpu.roll(plane, cz % size_z, 1)
        target = 0 if cz > 0 else size_z - 1
        column = pltpu.roll(z_halo[cz][...], (target - place) % size_z, 1)
        return jnp.where(lane == target, column, moved)

    for q in range(19):
        cx, cy, cz = VELOCITIES[q]
        rows = None
        if cy != 0:
            rows = y_halo[cy][Y_LISTS[cy].index(q)]
            if cz != 0:
                rows = shift_z(rows, cz, EDGE_LANE + Z_EDGES[cz].index(q))
        for x in range(size_x):
            source = x - cx
            outside = source < 0 or source >= size_x
            plane = x_plane(xr_ref, q) if outside else post[q, source]
            if cz != 0:
                if outside:
                    place = EDGE_LANE + Z_EDGES[cz].index(q)
                else:
                    place = Z_LISTS[cz].index(q) * 16 + source
                plane = shift_z(plane, cz, place)
            if cy != 0:
                moved = pltpu.roll(plane, cy % size_y, 0)
                target = 0 if cy > 0 else size_y - 1
                if outside:
                    e = Y_EDGES[cy].index(q)
                    line = y_halo[cy][5, e : e + 1, :]
                else:
                    line = rows[source : source + 1, :]
                plane = jnp.where(row == target, jnp.broadcast_to(line, moved.shape), moved)
            read[q, x] = plane
        stores[q].start()
    for store in stores:
        store.wait()


def stream(post, x_halo, y_plus, y_minus, z_plus, z_minus):
    anyspace = pl.BlockSpec(memory_space=pl.ANY)
    return pl.pallas_call(
        stream_kernel,
        out_shape=jax.ShapeDtypeStruct(post.shape, F32),
        in_specs=[vmem()] * 6,
        out_specs=anyspace,
        scratch_shapes=[
            pltpu.VMEM(post.shape, F32),
            pltpu.SemaphoreType.DMA((19,)),
        ],
        compiler_params=settings(10),
        cost_estimate=cost(MIB, 16 * MIB),
        name="stream_populations",
    )(post, x_halo, y_plus, y_minus, z_plus, z_minus)


def collect_kernel(inter_ref, base_ref, rank_ref, back_ref, out_ref):
    patches, verts = rank_ref.shape[1:]
    line = lax.broadcasted_iota(jnp.int32, (16, verts), 0) & (SLOT_CAP - 1)
    for p in range(patches):
        value = None
        for i in range(2):
            brick = inter_ref[i, p]
            base = base_ref[2 * p + i]
            rank = jnp.broadcast_to(rank_ref[i, p : p + 1, :], (8, verts))
            spot = jnp.concatenate([rank + base] * 2, axis=0)
            rows = [back_ref[brick, c] for c in range(3)] + [jnp.zeros((4, verts), F32)]
            picked = jnp.concatenate(rows, axis=0)
            picked = jnp.take_along_axis(picked, spot & (verts - 1), axis=1)
            here = lax.shift_right_logical(spot, 7) == line
            picked = jnp.where(here & (jnp.concatenate([rank] * 2, axis=0) >= 0), picked, 0.0)
            value = picked if value is None else value + picked
        value = value + pltpu.roll(value, 15, 0)
        value = value + pltpu.roll(value, 14, 0)
        value = jnp.concatenate([value[4 * c : 4 * c + 1] for c in range(3)], axis=0)
        out_ref[:, p, :] = value


def collect(intersection, bases, ranks, back):
    _, patches, verts = ranks.shape
    return pl.pallas_call(
        collect_kernel,
        out_shape=jax.ShapeDtypeStruct((3, patches, verts), F32),
        in_specs=[smem()] * 2 + [vmem()] * 2,
        out_specs=vmem(),
        compiler_params=settings(4),
        name="collect_velocity",
    )(intersection, bases, ranks, back)


def shifted(value, axis, step):
    count = lax.axis_size(axis)
    return lax.ppermute(value, axis, [(i, (i + step) % count) for i in range(count)])


def exchanged(value):
    return lax.all_to_all(value, ("gy", "gz"), split_axis=0, concat_axis=0, tiled=True)


def body(populations, solid_flags, positions, anchors, base_cell, weights, intersection):
    extent = populations.shape[1:]
    axes = ("gx", "gy", "gz")
    bricks = lax.axis_size("gy") * lax.axis_size("gz")
    here = [lax.axis_index(axis) for axis in axes]
    place = jnp.stack(
        [here[d] * extent[d] for d in range(3)]
        + here
        + [jnp.int32(lax.axis_size(axis)) for axis in axes]
    ).astype(jnp.int32)
    lists = intersection.T
    outgoing, ranks, bases = build_lists(
        lists,
        jnp.transpose(positions, (1, 0, 2)),
        jnp.transpose(anchors, (1, 0, 2)),
        jnp.transpose(base_cell, (1, 0, 2)),
        weights,
        bricks,
        lax.axis_size("gz"),
        extent,
    )
    table = exchanged(outgoing)
    total, packed, spots = spread(place, table, extent)
    post, x_face, y_plus, y_minus, z_plus, z_minus, unit = collide(
        total, populations, solid_flags
    )
    if lax.axis_size("gx") == 2:
        x_halo = shifted(x_face, "gx", 1)
    else:
        x_halo = jnp.concatenate(
            [shifted(x_face[:5], "gx", 1), shifted(x_face[5:], "gx", -1)], axis=0
        )
    steps = table.shape[0] // 2
    one = sample_part(place, table, unit, (), 0, steps // 4, extent)
    y_plus, y_minus = y_messages(x_halo, y_plus, y_minus)
    y_plus = shifted(y_plus, "gy", 1)
    y_minus = shifted(y_minus, "gy", -1)
    two = sample_part(place, table, unit, (x_halo,), steps // 4, steps // 4 * 3, extent)
    order = (y_plus, y_minus)
    sampled = sample(place, spots, table, packed, unit, (one, two), order, extent)
    back = exchanged(sampled)
    z_plus, z_minus = z_messages(x_halo, y_plus, y_minus, z_plus, z_minus)
    z_plus = shifted(z_plus, "gz", 1)
    z_minus = shifted(z_minus, "gz", -1)
    read = stream(post, x_halo, y_plus, y_minus, z_plus, z_minus)
    velocity = collect(lists, bases, ranks, back)
    return read, jnp.transpose(velocity, (1, 0, 2))


def solution(mesh):
    return jax.shard_map(
        body,
        mesh=mesh,
        in_specs=(
            P(None, "gx", "gy", "gz"),
            P("gx", "gy", "gz"),
            P(("gx", "gy", "gz"), None, None),
            P(("gx", "gy", "gz"), None, None),
            P(("gx", "gy", "gz"), None, None),
            P(("gx", "gy", "gz"), None, None),
            P(("gx", "gy", "gz"), None),
        ),
        out_specs=(P(None, "gx", "gy", "gz"), P(("gx", "gy", "gz"), None, None)),
        check_vma=False,
    )
```

```python
import functools

import jax
import jax.numpy as jnp
from jax import lax
from jax.experimental import pallas as pl
from jax.experimental.pallas import tpu as pltpu
from jax.sharding import PartitionSpec as P

SLOT_CAP = 4
GROUPS = 7
EDGE_LANE = 80

RELAXATION = 0.8
TENSION = 0.05
TETHER = 0.5
VELOCITIES = [
    (0, 0, 0),
    (1, 0, 0),
    (-1, 0, 0),
    (0, 1, 0),
    (0, -1, 0),
    (0, 0, 1),
    (0, 0, -1),
    (1, 1, 0),
    (-1, -1, 0),
    (1, -1, 0),
    (-1, 1, 0),
    (1, 0, 1),
    (-1, 0, -1),
    (1, 0, -1),
    (-1, 0, 1),
    (0, 1, 1),
    (0, -1, -1),
    (0, 1, -1),
    (0, -1, 1),
]
LATTICE_WEIGHTS = [1.0 / 3.0] + [1.0 / 18.0] * 6 + [1.0 / 36.0] * 12


def crossing(axis, sign):
    return [q for q in range(19) if VELOCITIES[q][axis] == sign]


X_LISTS = {1: crossing(0, 1), -1: crossing(0, -1)}
Y_LISTS = {1: crossing(1, 1), -1: crossing(1, -1)}
Z_LISTS = {1: crossing(2, 1), -1: crossing(2, -1)}
Y_EDGES = {s: [q for q in Y_LISTS[s] if VELOCITIES[q][0] != 0] for s in (1, -1)}
Z_EDGES = {
    s: [q for q in Z_LISTS[s] if VELOCITIES[q][0] != 0 or VELOCITIES[q][1] != 0] for s in (1, -1)
}

BF = jnp.bfloat16
F32 = jnp.float32
MIB = 1024 * 1024
NT = (((1,), (1,)), ((), ()))
NN = (((1,), (0,)), ((), ()))


def settings(mib):
    return pltpu.CompilerParams(vmem_limit_bytes=mib * MIB)


def cost(flops, size):
    return pl.CostEstimate(flops=flops, bytes_accessed=size, transcendentals=0)


def vmem():
    return pl.BlockSpec(memory_space=pltpu.VMEM)


def smem():
    return pl.BlockSpec(memory_space=pltpu.SMEM)


def list_kernel(
    bricks_z,
    inter_ref,
    pos_ref,
    anchor_ref,
    cell_ref,
    weight_ref,
    out_ref,
    rank_ref,
    base_ref,
    payload,
    lists,
    count_ref,
    extent,
):
    patches, verts = pos_ref.shape[1:]
    bricks = out_ref.shape[0]
    pos = pos_ref[...]
    cycle_term = pltpu.roll(pos, 1, 2) + pltpu.roll(pos, verts - 1, 2) - 2.0 * pos
    forces = TENSION * cycle_term + TETHER * (anchor_ref[...] - pos)
    cells = cell_ref[...].astype(F32)
    payload[:, 0:8, :] = weight_ref[...]
    for p in range(patches):
        payload[p, 8:11, :] = forces[:, p, :]
        payload[p, 11:14, :] = cells[:, p, :] + 1.0
        payload[p, 14:16, :] = jnp.zeros((2, verts), F32)
    lists[...] = jnp.zeros(lists.shape, F32)

    @pl.loop(0, bricks)
    def _(b):
        count_ref[b] = 0

    lane = lax.broadcasted_iota(jnp.int32, (patches, verts), 1)
    row = lax.broadcasted_iota(jnp.int32, (patches, verts), 0)
    upper = (
        lax.broadcasted_iota(jnp.int32, (verts, verts), 0)
        <= lax.broadcasted_iota(jnp.int32, (verts, verts), 1)
    ).astype(F32)
    codes, sums = [], []
    for i in range(2):
        first_y = jnp.zeros((patches, verts), F32)
        first_z = jnp.zeros((patches, verts), F32)
        for p in range(patches):
            brick = inter_ref[i, p]
            first_y = jnp.where(row == p, (brick // bricks_z * extent[1]).astype(F32), first_y)
            first_z = jnp.where(row == p, (brick % bricks_z * extent[2]).astype(F32), first_z)
        live = (
            (cells[1] >= first_y)
            & (cells[1] < first_y + extent[1])
            & (cells[2] >= first_z)
            & (cells[2] < first_z + extent[2])
        )
        mask = live.astype(F32)
        total = jnp.dot(mask.astype(BF), upper.astype(BF), preferred_element_type=F32)
        rank = (total - mask).astype(jnp.int32)
        rank_ref[i] = jnp.where(live, rank, -1)
        code = jnp.where(live, (lane - rank) + lane * 256 + 65536, 0)
        step = 1
        while step < verts:
            moving = jnp.where((code & step) != 0, code, 0)
            code = (code - moving) + pltpu.roll(moving, verts - step, 1)
            step *= 2
        codes.append(code)
        sums.append(total)
    wide_lane = lax.broadcasted_iota(jnp.int32, (16, verts), 1)
    for p in range(patches):
        for i in range(2):
            brick = inter_ref[i, p]
            base = count_ref[brick]
            base_ref[2 * p + i] = base
            count_ref[brick] = base + jnp.max(sums[i][p : p + 1, :]).astype(jnp.int32)
            block = lax.shift_right_logical(base, 7)
            shift = base & (verts - 1)
            code = jnp.broadcast_to(codes[i][p : p + 1, :], (8, verts))
            code = pltpu.roll(code, shift, 1)
            code = jnp.concatenate([code, code], axis=0)
            source = lax.shift_right_logical(code, 8) & (verts - 1)
            moved = jnp.take_along_axis(payload[p], source, axis=1)
            moved = jnp.where(code >= 65536, moved, 0.0)
            lists[brick, block] += jnp.where(wide_lane >= shift, moved, 0.0)
            lists[brick, block + 1] += jnp.where(wide_lane < shift, moved, 0.0)

    @pl.loop(0, bricks)
    def _(b):
        for j in range(SLOT_CAP):
            value = lists[b, j]
            first = j // 2 * GROUPS
            for g in range(3):
                out_ref[b, first + j % 2 * 3 + g] = value[4 * g : 4 * g + 4]
            out_ref[b, first + 6, j % 2 * 2 : j % 2 * 2 + 2] = value[12:14]


def build_lists(intersection, positions, anchors, base_cell, weights, bricks, bricks_z, extent):
    _, patches, verts = positions.shape

    def kernel(*refs):
        list_kernel(bricks_z, *refs, extent)

    return pl.pallas_call(
        kernel,
        out_shape=(
            jax.ShapeDtypeStruct((bricks, 2 * GROUPS, 4, verts), F32),
            jax.ShapeDtypeStruct((2, patches, verts), jnp.int32),
            jax.ShapeDtypeStruct((2 * patches,), jnp.int32),
        ),
        in_specs=[smem(), vmem(), vmem(), vmem(), vmem()],
        out_specs=(vmem(), vmem(), smem()),
        scratch_shapes=[
            pltpu.VMEM((patches, 16, verts), F32),
            pltpu.VMEM((bricks, SLOT_CAP + 1, 16, verts), F32),
            pltpu.SMEM((bricks,), jnp.int32),
        ],
        compiler_params=settings(56),
        name="vertex_lists",
    )(intersection, positions, anchors, base_cell, weights)


def block_rows(table_ref, owner, j):
    first = j // 2 * GROUPS
    group = first + j % 2 * 3
    weight = jnp.concatenate([table_ref[owner, group], table_ref[owner, group + 1]], axis=0)
    third = table_ref[owner, group + 2]
    line = j % 2 * 2
    last = table_ref[owner, first + 6, line : line + 2]
    return weight, third[0:3], jnp.concatenate([third[3:4], last], axis=0)


def pack_far(table_ref, packed, spot_ref, owner, spot):
    verts = table_ref.shape[3]
    lane = lax.broadcasted_iota(jnp.int32, (16, verts), 1)
    for j in range(2):
        weight, force, cells = block_rows(table_ref, owner, 2 + j)
        held = (cells[0:1] > 0.0).astype(F32)
        rows = jnp.concatenate([weight, force, cells, jnp.zeros((2, verts), F32)], axis=0)
        spot_ref[2 * owner + j] = spot
        block = lax.shift_right_logical(spot, 7)
        shift = spot & (verts - 1)
        rows = pltpu.roll(rows, shift, 1)
        packed[block] += jnp.where(lane >= shift, rows, 0.0)
        packed[block + 1] += jnp.where(lane < shift, rows, 0.0)
        spot = spot + jnp.sum(held).astype(jnp.int32)
    return spot


def packed_blocks(spot, verts):
    return lax.shift_right_logical(spot + verts - 1, 7)


def packed_rows(packed, block):
    return packed[block, 0:8], packed[block, 8:11], packed[block, 11:14]


def place_rows(place_ref, rows, extent):
    weight, force, cells = rows
    local, inside = [], None
    for d in range(3):
        value = cells[d : d + 1] - (place_ref[d] + 1).astype(F32)
        ok = (value >= 0.0) & (value < float(extent[d]))
        inside = ok if inside is None else inside & ok
        local.append(value)
    weight = weight * jnp.broadcast_to(inside.astype(F32), weight.shape)
    return weight, force, local


def halves(value):
    high = value.astype(BF).astype(F32)
    return high, value - high


def spread_scratch(extent, verts):
    size_x, size_y, size_z = extent
    depth = SLOT_CAP * 2 * verts
    return [
        pltpu.VMEM((2, 2, size_x * size_y, depth), BF),
        pltpu.VMEM((2, 6 * size_z, depth), BF),
        pltpu.VMEM((2, SLOT_CAP, 16, verts), F32),
        pltpu.VMEM((2, SLOT_CAP, 8, verts), F32),
        pltpu.VMEM((2, SLOT_CAP, 8, verts), F32),
    ]


def spread_tools(place_ref, extent, verts, total, a_buf, zf_buf, w_rows, f_rows, c_rows):
    size_x, size_y, size_z = extent
    iota_y = lax.broadcasted_iota(jnp.int32, (16, verts), 0).astype(F32).astype(BF)
    zero = jnp.zeros((16, verts), BF)

    def wide(ref, slot, j, row):
        return jnp.broadcast_to(ref[slot, j, row : row + 1, :], (16, verts)).astype(BF)

    def build(blocks, slot):
        for j, rows in enumerate(blocks):
            weight, force, local = place_rows(place_ref, rows, extent)
            w_hi, w_lo = halves(weight)
            f_hi, f_lo = halves(force)
            w_rows[slot, j, 0:8] = w_hi
            w_rows[slot, j, 8:16] = w_lo
            f_rows[slot, j, 0:3] = f_hi
            f_rows[slot, j, 4:7] = f_lo
            for d in range(3):
                c_rows[slot, j, d : d + 1] = local[d]
        for j in range(len(blocks)):
            xl = wide(c_rows, slot, j, 0)
            yl = wide(c_rows, slot, j, 1)
            zl = wide(c_rows, slot, j, 2)
            at_y0 = iota_y == yl
            at_y1 = iota_y == yl + 1.0
            lines = {}
            for part in range(2):
                for dx in range(2):
                    for dz in range(2):
                        first = part * 8 + dx * 4 + dz
                        lines[part, dx, dz] = jnp.where(
                            at_y0,
                            wide(w_rows, slot, j, first),
                            jnp.where(at_y1, wide(w_rows, slot, j, first + 2), zero),
                        )
            before = None
            for x in range(size_x):
                here = xl == float(x)
                for part in range(2):
                    for dz in range(2):
                        value = jnp.where(here, lines[part, 0, dz], zero)
                        if before is not None:
                            value = jnp.where(before, lines[part, 1, dz], value)
                        column = (j * 2 + dz) * verts
                        a_buf[slot, part, x * 16 : (x + 1) * 16, column : column + verts] = value
                before = here
            force = [wide(f_rows, slot, j, part * 4 + c) for part in range(2) for c in range(3)]
            for zb in range(size_z // 16):
                for dz in range(2):
                    at_z = iota_y == zl + float(dz - 16 * zb)
                    column = (j * 2 + dz) * verts
                    for part in range(2):
                        for c in range(3):
                            line = (part * 3 + c) * size_z + zb * 16
                            zf_buf[slot, line : line + 16, column : column + verts] = jnp.where(
                                at_z, force[part * 3 + c], zero
                            )

    def product(slot, blocks=SLOT_CAP):
        lines = 3 * size_z
        depth = blocks * 2 * verts
        high = lax.dot_general(
            zf_buf[slot, :, :depth], a_buf[slot, 0, :, :depth], NT, preferred_element_type=F32
        )
        low = lax.dot_general(
            zf_buf[slot, :lines, :depth],
            a_buf[slot, 1, :, :depth],
            NT,
            preferred_element_type=F32,
        )
        total[...] += high[:lines] + high[lines:] + low

    return build, product


def pair_blocks(table_ref, step):
    return [block_rows(table_ref, 2 * step + oo, j) for oo in range(2) for j in range(2)]


def spread_kernel(extent, place_ref, table_ref, total, packed, spot_ref, *scratch):
    owners, _, _, verts = table_ref.shape
    build, product = spread_tools(place_ref, extent, verts, total, *scratch)
    steps = owners // 2
    total[...] = jnp.zeros(total.shape, F32)
    packed[...] = jnp.zeros(packed.shape, F32)
    build(pair_blocks(table_ref, 0), 0)

    def near(i, spot):
        build(pair_blocks(table_ref, 2 * i + 1), 1)
        product(0)
        for owner in range(2):
            spot = pack_far(table_ref, packed, spot_ref, 4 * i + owner, spot)
        build(pair_blocks(table_ref, jnp.minimum(2 * i + 2, steps - 1)), 0)
        product(1)
        for owner in range(2, 4):
            spot = pack_far(table_ref, packed, spot_ref, 4 * i + owner, spot)
        return spot

    spot_ref[2 * owners] = lax.fori_loop(0, steps // 2, near, jnp.int32(0))

    @pl.loop(0, packed_blocks(spot_ref[2 * owners], verts))
    def _(block):
        build([packed_rows(packed, block)], 0)
        product(0, 1)


def spread(place, table, extent):
    owners, _, _, verts = table.shape
    size_x, size_y, size_z = extent
    cross = size_x * size_y
    return pl.pallas_call(
        functools.partial(spread_kernel, extent),
        out_shape=(
            jax.ShapeDtypeStruct((3 * size_z, cross), F32),
            jax.ShapeDtypeStruct((2 * owners + 2, 16, verts), F32),
            jax.ShapeDtypeStruct((2 * owners + 1,), jnp.int32),
        ),
        in_specs=[smem(), vmem()],
        out_specs=(vmem(), vmem(), smem()),
        scratch_shapes=spread_scratch(extent, verts),
        compiler_params=settings(16),
        cost_estimate=cost(6 * owners * 3 * size_z * cross * 4 * verts, MIB),
        name="spread",
    )(place, table)


def along(vector, q):
    value = None
    for c in range(3):
        move = VELOCITIES[q][c]
        if move == 0:
            continue
        if value is None:
            value = vector[c] if move > 0 else -vector[c]
        else:
            value = value + vector[c] if move > 0 else value - vector[c]
    return value


def collide_plane(x, force, pop, solid):
    factor = 1.0 - 0.5 / RELAXATION
    rate = 1.0 / RELAXATION
    keep = 1.0 - rate
    cells = [pop[q, x] for q in range(19)]
    wall = solid[x] == 1
    rho = cells[0]
    for q in range(1, 19):
        rho = rho + cells[q]
    moment = []
    for c in range(3):
        value = None
        for q in range(1, 19, 2):
            if VELOCITIES[q][c] != 0:
                term = cells[q] - cells[q + 1]
                if VELOCITIES[q][c] < 0:
                    term = -term
                value = term if value is None else value + term
        moment.append(value)
    inverse = 1.0 / rho
    vel = [(moment[c] + 0.5 * force[c]) * inverse for c in range(3)]
    speed = vel[0] * vel[0] + vel[1] * vel[1] + vel[2] * vel[2]
    u_dot_f = vel[0] * force[0] + vel[1] * force[1] + vel[2] * force[2]
    three = 3.0 * factor
    nine = 9.0 * factor
    rest = (rate * rho) * (1.0 - 1.5 * speed) - three * u_dot_f
    quad = (4.5 * rate) * rho
    linear = (3.0 * rate) * rho
    results = [None] * 19
    results[0] = jnp.where(wall, cells[0], keep * cells[0] + LATTICE_WEIGHTS[0] * rest)

    for q in range(1, 19, 2):
        a = along(vel, q)
        b = along(force, q)
        weight = LATTICE_WEIGHTS[q]
        even = weight * (rest + a * (quad * a + nine * b))
        odd = weight * (linear * a + three * b)
        results[q] = jnp.where(wall, cells[q + 1], keep * cells[q] + (even + odd))
        results[q + 1] = jnp.where(wall, cells[q], keep * cells[q + 1] + (even - odd))
    return results, vel


def face_kernel(total, pop, solid, xface_ref, field):
    size_x, size_y, size_z = solid.shape
    for c in range(3):
        for half in range(size_x * size_y // 128):
            field[c, half * 128 : (half + 1) * 128, :] = jnp.transpose(
                total[c * size_z : (c + 1) * size_z, half * 128 : (half + 1) * 128]
            )
    for x, first, sign in ((size_x - 1, 0, 1), (0, 5, -1)):
        force = [field[c, x * size_y : (x + 1) * size_y, :] for c in range(3)]
        results, _ = collide_plane(x, force, pop, solid)
        for k, q in enumerate(X_LISTS[sign]):
            xface_ref[first + k] = results[q]


def x_faces(total, populations, solid):
    _, size_x, size_y, size_z = populations.shape
    return pl.pallas_call(
        face_kernel,
        out_shape=(
            jax.ShapeDtypeStruct((10, size_y, size_z), F32),
            jax.ShapeDtypeStruct((3, size_x * size_y, size_z), F32),
        ),
        in_specs=[vmem()] * 3,
        out_specs=(vmem(),) * 2,
        compiler_params=settings(12),
        cost_estimate=cost(2 * MIB, MIB),
        name="x_faces",
    )(total, populations, solid)


def collide_kernel(field, pop, solid, post, yfp_ref, yfm_ref, zfp_ref, zfm_ref, unit_ref):
    _, size_x, size_y, size_z = post.shape
    lane = lax.broadcasted_iota(jnp.int32, (size_y, size_z), 1)

    def plane(x, z_out):
        z_out = dict(zip((1, -1), z_out))
        lines = pl.ds(pl.multiple_of(x * 16, 16), 16)
        force = [field[c, lines, :] for c in range(3)]
        results, vel = collide_plane(x, force, pop, solid)
        for c in range(3):
            high, low = halves(vel[c])
            first = pl.ds(pl.multiple_of((x * 3 + c) * 16, 16), 16)
            unit_ref[first, 0:size_z] = high.astype(BF)
            unit_ref[first, size_z : 2 * size_z] = low.astype(BF)
        for q in range(19):
            post[q, x] = results[q]
        for sign, line, face in ((1, size_y - 1, yfp_ref), (-1, 0, yfm_ref)):
            for k, q in enumerate(Y_LISTS[sign]):
                face[k, pl.ds(x, 1), :] = results[q][line : line + 1, :]
        for sign, column in ((1, size_z - 1), (-1, 0)):
            for k, q in enumerate(Z_LISTS[sign]):
                place = k * 16 + x
                moved = pltpu.roll(results[q], (place - column + size_z) & (size_z - 1), 1)
                z_out[sign] = jnp.where(lane == place, moved, z_out[sign])
        return z_out[1], z_out[-1]

    empty = jnp.zeros((size_y, size_z), F32)
    zfp_ref[...], zfm_ref[...] = lax.fori_loop(0, size_x, plane, (empty, empty), unroll=2)


def collide(field, populations, solid):
    _, size_x, size_y, size_z = populations.shape
    face_y = jax.ShapeDtypeStruct((5, size_x, size_z), F32)
    face_z = jax.ShapeDtypeStruct((size_y, size_z), F32)
    return pl.pallas_call(
        collide_kernel,
        out_shape=(
            jax.ShapeDtypeStruct(populations.shape, F32),
            face_y,
            face_y,
            face_z,
            face_z,
            jax.ShapeDtypeStruct((size_x * size_y * 3, 2 * size_z), BF),
        ),
        in_specs=[vmem()] * 3,
        out_specs=(vmem(),) * 6,
        compiler_params=settings(12),
        cost_estimate=cost(16 * MIB, 8 * MIB),
        name="collide",
    )(field, populations, solid)


def sample_scratch(extent, verts):
    size_x, size_y, size_z = extent
    return [
        pltpu.VMEM((2, SLOT_CAP, 2 * size_z, 2 * verts), BF),
        pltpu.VMEM((2, 3 * size_x * size_y, 2 * verts), F32),
        pltpu.VMEM((2, SLOT_CAP, 8, verts), F32),
        pltpu.VMEM((2, SLOT_CAP, 8, verts), F32),
    ]


def sample_tools(place_ref, unit_ref, extent, verts, hot, grid_buf, w_rows, c_rows):
    size_x, size_y, size_z = extent
    iota_y = lax.broadcasted_iota(jnp.int32, (16, verts), 0).astype(F32)
    iota_b = iota_y.astype(BF)
    one = jnp.ones((16, verts), BF)
    zero_b = jnp.zeros((16, verts), BF)
    zero = jnp.zeros((16, verts), F32)

    def wide(ref, slot, j, row):
        return jnp.broadcast_to(ref[slot, j, row : row + 1, :], (16, verts))

    def prepare(blocks, slot):
        for j, rows in enumerate(blocks):
            weight, _, local = place_rows(place_ref, rows, extent)
            w_rows[slot, j] = weight
            for d in range(3):
                c_rows[slot, j, d : d + 1] = local[d]
        for j in range(len(blocks)):
            zl = wide(c_rows, slot, j, 2).astype(BF)
            for zb in range(size_z // 16):
                for dz in range(2):
                    value = jnp.where(iota_b == zl + float(dz - 16 * zb), one, zero_b)
                    for part in range(2):
                        line = part * size_z + zb * 16
                        hot[slot, j, line : line + 16, dz * verts : (dz + 1) * verts] = value

    def product(slot, j):
        grid_buf[j % 2] = lax.dot_general(unit_ref[...], hot[slot, j], NN, preferred_element_type=F32)

    def select(slot, j):
        xl = wide(c_rows, slot, j, 0)
        yl = wide(c_rows, slot, j, 1)
        at_y0 = iota_y == yl
        at_y1 = iota_y == yl + 1.0
        lines = {}
        for dx in range(2):
            for dz in range(2):
                first = dx * 4 + dz
                lines[dx, dz] = jnp.where(
                    at_y0,
                    wide(w_rows, slot, j, first),
                    jnp.where(at_y1, wide(w_rows, slot, j, first + 2), zero),
                )
        sums = [zero, zero, zero]
        before = None
        for x in range(size_x):
            here = xl == float(x)
            for dz in range(2):
                value = jnp.where(here, lines[0, dz], zero)
                if before is not None:
                    value = jnp.where(before, lines[1, dz], value)
                for c in range(3):
                    first = (x * 3 + c) * 16
                    part = grid_buf[j % 2, first : first + 16, dz * verts : (dz + 1) * verts]
                    sums[c] = sums[c] + value * part
            before = here
        return [jnp.sum(value, axis=0, keepdims=True) for value in sums]

    def work(slot, store):
        product(slot, 0)
        for j in range(SLOT_CAP):
            if j + 1 < SLOT_CAP:
                product(slot, j + 1)
            store(j, select(slot, j))

    return prepare, product, select, work


def x_plane(xr_ref, q):
    sign = VELOCITIES[q][0]
    return xr_ref[(0 if sign > 0 else 5) + X_LISTS[sign].index(q)]


def sample_steps(table_ref, first, last, prepare, work, put):
    def store(step):
        return lambda j, values: put(2 * step + j // 2, j % 2, values)

    prepare(pair_blocks(table_ref, first), 0)

    @pl.loop(0, (last - first) // 2)
    def _(i):
        step = first + 2 * i
        prepare(pair_blocks(table_ref, step + 1), 1)
        work(0, store(step))
        prepare(pair_blocks(table_ref, jnp.minimum(step + 2, last - 1)), 0)
        work(1, store(step + 1))


def sample_part_kernel(extent, first, last, place_ref, table_ref, unit_ref, *refs):
    out_ref, scratch = refs[-5], refs[-4:]
    verts = table_ref.shape[3]
    prepare, _, _, work = sample_tools(place_ref, unit_ref, extent, verts, *scratch)

    def put(owner, line, values):
        for c in range(3):
            out_ref[owner - 2 * first, c, line : line + 1, :] = values[c]

    sample_steps(table_ref, first, last, prepare, work, put)


def sample_part(place, table, unit, order, first, last, extent):
    owners, _, _, verts = table.shape
    size_x, size_y, size_z = extent
    return pl.pallas_call(
        functools.partial(sample_part_kernel, extent, first, last),
        out_shape=jax.ShapeDtypeStruct((2 * (last - first), 3, 2, verts), F32),
        in_specs=[smem(), vmem(), vmem()] + [pl.BlockSpec(memory_space=pl.ANY)] * len(order),
        out_specs=vmem(),
        scratch_shapes=sample_scratch(extent, verts),
        compiler_params=settings(12),
        cost_estimate=cost(
            32 * (last - first) * 3 * size_x * size_y * size_z * verts, MIB
        ),
        name="sample_part",
    )(place, table, unit, *order)


def sample_kernel(
    extent, place_ref, spot_ref, table_ref, packed, unit_ref, part_ref, *refs
):
    out_ref, found, scratch = refs[-6], refs[-5], refs[-4:]
    owners, _, _, verts = table_ref.shape
    prepare, product, select, work = sample_tools(place_ref, unit_ref, extent, verts, *scratch)
    done = part_ref.shape[0]
    for c in range(3):
        out_ref[0:done, c, 0:2] = part_ref[:, c]
        out_ref[:, c, 2:4] = jnp.zeros((owners, 2, verts), F32)

    def put(owner, line, values):
        for c in range(3):
            out_ref[owner, c, line : line + 1, :] = values[c]

    sample_steps(table_ref, done // 2, owners // 2, prepare, work, put)

    @pl.loop(0, packed_blocks(spot_ref[2 * owners], verts))
    def _(block):
        prepare([packed_rows(packed, block)], 0)
        product(0, 0)
        values = select(0, 0)
        for c in range(3):
            found[block, c : c + 1, :] = values[c]

    lane = lax.broadcasted_iota(jnp.int32, (4, verts), 1)
    for owner in range(owners):
        for j in range(2):
            spot = spot_ref[2 * owner + j]

            @pl.when(spot_ref[2 * owner + j + 1] > spot)
            def _(owner=owner, j=j, spot=spot):
                block = lax.shift_right_logical(spot, 7)
                shift = spot & (verts - 1)
                back = (verts - shift) & (verts - 1)
                first = pltpu.roll(found[block, 0:4], back, 1)
                second = pltpu.roll(found[block + 1, 0:4], back, 1)
                value = jnp.where(lane < verts - shift, first, second)
                for c in range(3):
                    out_ref[owner, c, 2 + j : 3 + j, :] = value[c : c + 1]


def sample(place, spots, table, packed, unit, part, order, extent):
    owners, _, _, verts = table.shape
    size_x, size_y, size_z = extent
    return pl.pallas_call(
        functools.partial(sample_kernel, extent),
        out_shape=jax.ShapeDtypeStruct((owners, 3, SLOT_CAP, verts), F32),
        in_specs=[smem(), smem()]
        + [vmem()] * 4
        + [pl.BlockSpec(memory_space=pl.ANY)] * len(order),
        out_specs=vmem(),
        scratch_shapes=[pltpu.VMEM((2 * owners + 2, 8, verts), F32)]
        + sample_scratch(extent, verts),
        compiler_params=settings(12),
        cost_estimate=cost(8 * owners * 3 * size_x * size_y * size_z * verts, MIB),
        name="sample_velocity",
    )(place, spots, table, packed, unit, part, *order)


def y_message_kernel(xr_ref, yfp_ref, yfm_ref, plus_ref, minus_ref):
    size_y = xr_ref.shape[1]
    for sign, face, out in ((1, yfp_ref, plus_ref), (-1, yfm_ref, minus_ref)):
        out[0:5] = face[...]
        line = size_y - 1 if sign > 0 else 0
        for e, q in enumerate(Y_EDGES[sign]):
            out[5, e : e + 1, :] = x_plane(xr_ref, q)[line : line + 1, :]


def y_messages(x_halo, y_plus, y_minus):
    shape = jax.ShapeDtypeStruct((6,) + y_plus.shape[1:], F32)
    return pl.pallas_call(
        y_message_kernel,
        out_shape=(shape, shape),
        in_specs=[vmem()] * 3,
        out_specs=(vmem(), vmem()),
        compiler_params=settings(4),
        name="y_messages",
    )(x_halo, y_plus, y_minus)


def z_message_kernel(xr_ref, yrp_ref, yrm_ref, zfp_ref, zfm_ref, plus_ref, minus_ref):
    size_y, size_z = zfp_ref.shape
    y_halo = {1: yrp_ref, -1: yrm_ref}
    lane = lax.broadcasted_iota(jnp.int32, (size_y, size_z), 1)
    for sign, face, out in ((1, zfp_ref, plus_ref), (-1, zfm_ref, minus_ref)):
        column = size_z - 1 if sign > 0 else 0
        block = face[...]
        for e, q in enumerate(Z_EDGES[sign]):
            if VELOCITIES[q][0] != 0:
                plane = x_plane(xr_ref, q)
            else:
                y_sign = VELOCITIES[q][1]
                plane = y_halo[y_sign][Y_LISTS[y_sign].index(q)]
            spot = EDGE_LANE + e
            block = jnp.where(lane == spot, pltpu.roll(plane, (spot - column) % size_z, 1), block)
        out[...] = block


def z_messages(x_halo, y_plus, y_minus, z_plus, z_minus):
    shape = jax.ShapeDtypeStruct(z_plus.shape, F32)
    return pl.pallas_call(
        z_message_kernel,
        out_shape=(shape, shape),
        in_specs=[vmem()] * 5,
        out_specs=(vmem(), vmem()),
        compiler_params=settings(4),
        name="z_messages",
    )(x_halo, y_plus, y_minus, z_plus, z_minus)


def stream_kernel(
    post,
    xr_ref,
    yrp_ref,
    yrm_ref,
    zrp_ref,
    zrm_ref,
    read_hbm,
    read,
    out_sem,
):
    _, size_x, size_y, size_z = post.shape
    y_halo = {1: yrp_ref, -1: yrm_ref}
    z_halo = {1: zrp_ref, -1: zrm_ref}
    stores = [pltpu.make_async_copy(read.at[q], read_hbm.at[q], out_sem.at[q]) for q in range(19)]
    lane = lax.broadcasted_iota(jnp.int32, (size_y, size_z), 1)
    row = lax.broadcasted_iota(jnp.int32, (size_y, size_z), 0)

    def shift_z(plane, cz, place):
        moved = pltpu.roll(plane, cz % size_z, 1)
        target = 0 if cz > 0 else size_z - 1
        column = pltpu.roll(z_halo[cz][...], (target - place) % size_z, 1)
        return jnp.where(lane == target, column, moved)

    for q in range(19):
        cx, cy, cz = VELOCITIES[q]
        rows = None
        if cy != 0:
            rows = y_halo[cy][Y_LISTS[cy].index(q)]
            if cz != 0:
                rows = shift_z(rows, cz, EDGE_LANE + Z_EDGES[cz].index(q))
        for x in range(size_x):
            source = x - cx
            outside = source < 0 or source >= size_x
            plane = x_plane(xr_ref, q) if outside else post[q, source]
            if cz != 0:
                if outside:
                    place = EDGE_LANE + Z_EDGES[cz].index(q)
                else:
                    place = Z_LISTS[cz].index(q) * 16 + source
                plane = shift_z(plane, cz, place)
            if cy != 0:
                moved = pltpu.roll(plane, cy % size_y, 0)
                target = 0 if cy > 0 else size_y - 1
                if outside:
                    e = Y_EDGES[cy].index(q)
                    line = y_halo[cy][5, e : e + 1, :]
                else:
                    line = rows[source : source + 1, :]
                plane = jnp.where(row == target, jnp.broadcast_to(line, moved.shape), moved)
            read[q, x] = plane
        stores[q].start()
    for store in stores:
        store.wait()


def stream(post, x_halo, y_plus, y_minus, z_plus, z_minus):
    anyspace = pl.BlockSpec(memory_space=pl.ANY)
    return pl.pallas_call(
        stream_kernel,
        out_shape=jax.ShapeDtypeStruct(post.shape, F32),
        in_specs=[vmem()] * 6,
        out_specs=anyspace,
        scratch_shapes=[
            pltpu.VMEM(post.shape, F32),
            pltpu.SemaphoreType.DMA((19,)),
        ],
        compiler_params=settings(10),
        cost_estimate=cost(MIB, 16 * MIB),
        name="stream_populations",
    )(post, x_halo, y_plus, y_minus, z_plus, z_minus)


def collect_kernel(inter_ref, base_ref, rank_ref, back_ref, out_ref):
    patches, verts = rank_ref.shape[1:]
    line = lax.broadcasted_iota(jnp.int32, (16, verts), 0) & (SLOT_CAP - 1)
    for p in range(patches):
        value = None
        for i in range(2):
            brick = inter_ref[i, p]
            base = base_ref[2 * p + i]
            rank = jnp.broadcast_to(rank_ref[i, p : p + 1, :], (8, verts))
            spot = jnp.concatenate([rank + base] * 2, axis=0)
            rows = [back_ref[brick, c] for c in range(3)] + [jnp.zeros((4, verts), F32)]
            picked = jnp.concatenate(rows, axis=0)
            picked = jnp.take_along_axis(picked, spot & (verts - 1), axis=1)
            here = lax.shift_right_logical(spot, 7) == line
            picked = jnp.where(here & (jnp.concatenate([rank] * 2, axis=0) >= 0), picked, 0.0)
            value = picked if value is None else value + picked
        value = value + pltpu.roll(value, 15, 0)
        value = value + pltpu.roll(value, 14, 0)
        value = jnp.concatenate([value[4 * c : 4 * c + 1] for c in range(3)], axis=0)
        out_ref[:, p, :] = value


def collect(intersection, bases, ranks, back):
    _, patches, verts = ranks.shape
    return pl.pallas_call(
        collect_kernel,
        out_shape=jax.ShapeDtypeStruct((3, patches, verts), F32),
        in_specs=[smem()] * 2 + [vmem()] * 2,
        out_specs=vmem(),
        compiler_params=settings(4),
        name="collect_velocity",
    )(intersection, bases, ranks, back)


def shifted(value, axis, step):
    count = lax.axis_size(axis)
    return lax.ppermute(value, axis, [(i, (i + step) % count) for i in range(count)])


def exchanged(value):
    return lax.all_to_all(value, ("gy", "gz"), split_axis=0, concat_axis=0, tiled=True)


def body(populations, solid_flags, positions, anchors, base_cell, weights, intersection):
    extent = populations.shape[1:]
    axes = ("gx", "gy", "gz")
    bricks = lax.axis_size("gy") * lax.axis_size("gz")
    here = [lax.axis_index(axis) for axis in axes]
    place = jnp.stack(
        [here[d] * extent[d] for d in range(3)]
        + here
        + [jnp.int32(lax.axis_size(axis)) for axis in axes]
    ).astype(jnp.int32)
    lists = intersection.T
    outgoing, ranks, bases = build_lists(
        lists,
        jnp.transpose(positions, (1, 0, 2)),
        jnp.transpose(anchors, (1, 0, 2)),
        jnp.transpose(base_cell, (1, 0, 2)),
        weights,
        bricks,
        lax.axis_size("gz"),
        extent,
    )
    table = exchanged(outgoing)
    total, packed, spots = spread(place, table, extent)
    x_face, field = x_faces(total, populations, solid_flags)
    post, y_plus, y_minus, z_plus, z_minus, unit = collide(field, populations, solid_flags)
    if lax.axis_size("gx") == 2:
        x_halo = shifted(x_face, "gx", 1)
    else:
        x_halo = jnp.concatenate(
            [shifted(x_face[:5], "gx", 1), shifted(x_face[5:], "gx", -1)], axis=0
        )
    y_plus, y_minus = y_messages(x_halo, y_plus, y_minus)
    y_plus = shifted(y_plus, "gy", 1)
    y_minus = shifted(y_minus, "gy", -1)
    steps = table.shape[0] // 2
    part = sample_part(place, table, unit, (x_halo,), 0, steps // 4 * 3, extent)
    order = (y_plus, y_minus)
    sampled = sample(place, spots, table, packed, unit, part, order, extent)
    back = exchanged(sampled)
    z_plus, z_minus = z_messages(x_halo, y_plus, y_minus, z_plus, z_minus)
    z_plus = shifted(z_plus, "gz", 1)
    z_minus = shifted(z_minus, "gz", -1)
    read = stream(post, x_halo, y_plus, y_minus, z_plus, z_minus)
    velocity = collect(lists, bases, ranks, back)
    return read, jnp.transpose(velocity, (1, 0, 2))


def solution(mesh):
    return jax.shard_map(
        body,
        mesh=mesh,
        in_specs=(
            P(None, "gx", "gy", "gz"),
            P("gx", "gy", "gz"),
            P(("gx", "gy", "gz"), None, None),
            P(("gx", "gy", "gz"), None, None),
            P(("gx", "gy", "gz"), None, None),
            P(("gx", "gy", "gz"), None, None),
            P(("gx", "gy", "gz"), None),
        ),
        out_specs=(P(None, "gx", "gy", "gz"), P(("gx", "gy", "gz"), None, None)),
        check_vma=False,
    )
```

```python
import functools

import jax
import jax.numpy as jnp
from jax import lax
from jax.experimental import pallas as pl
from jax.experimental.pallas import tpu as pltpu
from jax.sharding import PartitionSpec as P

SLOT_CAP = 4
GROUPS = 7
EDGE_LANE = 80

RELAXATION = 0.8
TENSION = 0.05
TETHER = 0.5
VELOCITIES = [
    (0, 0, 0),
    (1, 0, 0),
    (-1, 0, 0),
    (0, 1, 0),
    (0, -1, 0),
    (0, 0, 1),
    (0, 0, -1),
    (1, 1, 0),
    (-1, -1, 0),
    (1, -1, 0),
    (-1, 1, 0),
    (1, 0, 1),
    (-1, 0, -1),
    (1, 0, -1),
    (-1, 0, 1),
    (0, 1, 1),
    (0, -1, -1),
    (0, 1, -1),
    (0, -1, 1),
]
LATTICE_WEIGHTS = [1.0 / 3.0] + [1.0 / 18.0] * 6 + [1.0 / 36.0] * 12


def crossing(axis, sign):
    return [q for q in range(19) if VELOCITIES[q][axis] == sign]


X_LISTS = {1: crossing(0, 1), -1: crossing(0, -1)}
Y_LISTS = {1: crossing(1, 1), -1: crossing(1, -1)}
Z_LISTS = {1: crossing(2, 1), -1: crossing(2, -1)}
Y_EDGES = {s: [q for q in Y_LISTS[s] if VELOCITIES[q][0] != 0] for s in (1, -1)}
Z_EDGES = {
    s: [q for q in Z_LISTS[s] if VELOCITIES[q][0] != 0 or VELOCITIES[q][1] != 0] for s in (1, -1)
}

BF = jnp.bfloat16
F32 = jnp.float32
MIB = 1024 * 1024
NT = (((1,), (1,)), ((), ()))
NN = (((1,), (0,)), ((), ()))


def settings(mib):
    return pltpu.CompilerParams(vmem_limit_bytes=mib * MIB)


def cost(flops, size):
    return pl.CostEstimate(flops=flops, bytes_accessed=size, transcendentals=0)


def vmem():
    return pl.BlockSpec(memory_space=pltpu.VMEM)


def smem():
    return pl.BlockSpec(memory_space=pltpu.SMEM)


def list_kernel(
    bricks_z,
    inter_ref,
    pos_ref,
    anchor_ref,
    cell_ref,
    weight_ref,
    out_ref,
    rank_ref,
    base_ref,
    payload,
    lists,
    count_ref,
    extent,
):
    patches, verts = pos_ref.shape[1:]
    bricks = out_ref.shape[0]
    pos = pos_ref[...]
    cycle_term = pltpu.roll(pos, 1, 2) + pltpu.roll(pos, verts - 1, 2) - 2.0 * pos
    forces = TENSION * cycle_term + TETHER * (anchor_ref[...] - pos)
    cells = cell_ref[...].astype(F32)
    payload[:, 0:8, :] = weight_ref[...]
    for p in range(patches):
        payload[p, 8:11, :] = forces[:, p, :]
        payload[p, 11:14, :] = cells[:, p, :] + 1.0
        payload[p, 14:16, :] = jnp.zeros((2, verts), F32)
    lists[...] = jnp.zeros(lists.shape, F32)

    @pl.loop(0, bricks)
    def _(b):
        count_ref[b] = 0

    lane = lax.broadcasted_iota(jnp.int32, (patches, verts), 1)
    row = lax.broadcasted_iota(jnp.int32, (patches, verts), 0)
    upper = (
        lax.broadcasted_iota(jnp.int32, (verts, verts), 0)
        <= lax.broadcasted_iota(jnp.int32, (verts, verts), 1)
    ).astype(F32)
    codes, sums = [], []
    for i in range(2):
        first_y = jnp.zeros((patches, verts), F32)
        first_z = jnp.zeros((patches, verts), F32)
        for p in range(patches):
            brick = inter_ref[i, p]
            first_y = jnp.where(row == p, (brick // bricks_z * extent[1]).astype(F32), first_y)
            first_z = jnp.where(row == p, (brick % bricks_z * extent[2]).astype(F32), first_z)
        live = (
            (cells[1] >= first_y)
            & (cells[1] < first_y + extent[1])
            & (cells[2] >= first_z)
            & (cells[2] < first_z + extent[2])
        )
        mask = live.astype(F32)
        total = jnp.dot(mask.astype(BF), upper.astype(BF), preferred_element_type=F32)
        rank = (total - mask).astype(jnp.int32)
        rank_ref[i] = jnp.where(live, rank, -1)
        code = jnp.where(live, (lane - rank) + lane * 256 + 65536, 0)
        step = 1
        while step < verts:
            moving = jnp.where((code & step) != 0, code, 0)
            code = (code - moving) + pltpu.roll(moving, verts - step, 1)
            step *= 2
        codes.append(code)
        sums.append(total)
    wide_lane = lax.broadcasted_iota(jnp.int32, (16, verts), 1)
    for p in range(patches):
        for i in range(2):
            brick = inter_ref[i, p]
            base = count_ref[brick]
            base_ref[2 * p + i] = base
            count_ref[brick] = base + jnp.max(sums[i][p : p + 1, :]).astype(jnp.int32)
            block = lax.shift_right_logical(base, 7)
            shift = base & (verts - 1)
            code = jnp.broadcast_to(codes[i][p : p + 1, :], (8, verts))
            code = pltpu.roll(code, shift, 1)
            code = jnp.concatenate([code, code], axis=0)
            source = lax.shift_right_logical(code, 8) & (verts - 1)
            moved = jnp.take_along_axis(payload[p], source, axis=1)
            moved = jnp.where(code >= 65536, moved, 0.0)
            lists[brick, block] += jnp.where(wide_lane >= shift, moved, 0.0)
            lists[brick, block + 1] += jnp.where(wide_lane < shift, moved, 0.0)

    @pl.loop(0, bricks)
    def _(b):
        for j in range(SLOT_CAP):
            value = lists[b, j]
            first = j // 2 * GROUPS
            for g in range(3):
                out_ref[b, first + j % 2 * 3 + g] = value[4 * g : 4 * g + 4]
            out_ref[b, first + 6, j % 2 * 2 : j % 2 * 2 + 2] = value[12:14]


def build_lists(intersection, positions, anchors, base_cell, weights, bricks, bricks_z, extent):
    _, patches, verts = positions.shape

    def kernel(*refs):
        list_kernel(bricks_z, *refs, extent)

    return pl.pallas_call(
        kernel,
        out_shape=(
            jax.ShapeDtypeStruct((bricks, 2 * GROUPS, 4, verts), F32),
            jax.ShapeDtypeStruct((2, patches, verts), jnp.int32),
            jax.ShapeDtypeStruct((2 * patches,), jnp.int32),
        ),
        in_specs=[smem(), vmem(), vmem(), vmem(), vmem()],
        out_specs=(vmem(), vmem(), smem()),
        scratch_shapes=[
            pltpu.VMEM((patches, 16, verts), F32),
            pltpu.VMEM((bricks, SLOT_CAP + 1, 16, verts), F32),
            pltpu.SMEM((bricks,), jnp.int32),
        ],
        compiler_params=settings(56),
        name="vertex_lists",
    )(intersection, positions, anchors, base_cell, weights)


def block_rows(table_ref, owner, j):
    first = j // 2 * GROUPS
    group = first + j % 2 * 3
    weight = jnp.concatenate([table_ref[owner, group], table_ref[owner, group + 1]], axis=0)
    third = table_ref[owner, group + 2]
    line = j % 2 * 2
    last = table_ref[owner, first + 6, line : line + 2]
    return weight, third[0:3], jnp.concatenate([third[3:4], last], axis=0)


def pack_far(table_ref, packed, spot_ref, owner, spot):
    verts = table_ref.shape[3]
    lane = lax.broadcasted_iota(jnp.int32, (16, verts), 1)
    for j in range(2):
        weight, force, cells = block_rows(table_ref, owner, 2 + j)
        held = (cells[0:1] > 0.0).astype(F32)
        rows = jnp.concatenate([weight, force, cells, jnp.zeros((2, verts), F32)], axis=0)
        spot_ref[2 * owner + j] = spot
        block = lax.shift_right_logical(spot, 7)
        shift = spot & (verts - 1)
        rows = pltpu.roll(rows, shift, 1)
        packed[block] += jnp.where(lane >= shift, rows, 0.0)
        packed[block + 1] += jnp.where(lane < shift, rows, 0.0)
        spot = spot + jnp.sum(held).astype(jnp.int32)
    return spot


def packed_blocks(spot, verts):
    return lax.shift_right_logical(spot + verts - 1, 7)


def packed_rows(packed, block):
    return packed[block, 0:8], packed[block, 8:11], packed[block, 11:14]


def place_rows(place_ref, rows, extent):
    weight, force, cells = rows
    local, inside = [], None
    for d in range(3):
        value = cells[d : d + 1] - (place_ref[d] + 1).astype(F32)
        ok = (value >= 0.0) & (value < float(extent[d]))
        inside = ok if inside is None else inside & ok
        local.append(value)
    weight = weight * jnp.broadcast_to(inside.astype(F32), weight.shape)
    return weight, force, local


def halves(value):
    high = value.astype(BF).astype(F32)
    return high, value - high


def spread_scratch(extent, verts):
    size_x, size_y, size_z = extent
    depth = SLOT_CAP * 2 * verts
    return [
        pltpu.VMEM((2, 2, size_x * size_y, depth), BF),
        pltpu.VMEM((2, 6 * size_z, depth), BF),
        pltpu.VMEM((2, SLOT_CAP, 16, verts), F32),
        pltpu.VMEM((2, SLOT_CAP, 8, verts), F32),
        pltpu.VMEM((2, SLOT_CAP, 8, verts), F32),
    ]


def spread_tools(place_ref, extent, verts, total, a_buf, zf_buf, w_rows, f_rows, c_rows):
    size_x, size_y, size_z = extent
    iota_y = lax.broadcasted_iota(jnp.int32, (16, verts), 0).astype(F32).astype(BF)
    zero = jnp.zeros((16, verts), BF)

    def wide(ref, slot, j, row):
        return jnp.broadcast_to(ref[slot, j, row : row + 1, :], (16, verts)).astype(BF)

    def build(blocks, slot):
        for j, rows in enumerate(blocks):
            weight, force, local = place_rows(place_ref, rows, extent)
            w_hi, w_lo = halves(weight)
            f_hi, f_lo = halves(force)
            w_rows[slot, j, 0:8] = w_hi
            w_rows[slot, j, 8:16] = w_lo
            f_rows[slot, j, 0:3] = f_hi
            f_rows[slot, j, 4:7] = f_lo
            for d in range(3):
                c_rows[slot, j, d : d + 1] = local[d]
        for j in range(len(blocks)):
            xl = wide(c_rows, slot, j, 0)
            yl = wide(c_rows, slot, j, 1)
            zl = wide(c_rows, slot, j, 2)
            at_y0 = iota_y == yl
            at_y1 = iota_y == yl + 1.0
            lines = {}
            for part in range(2):
                for dx in range(2):
                    for dz in range(2):
                        first = part * 8 + dx * 4 + dz
                        lines[part, dx, dz] = jnp.where(
                            at_y0,
                            wide(w_rows, slot, j, first),
                            jnp.where(at_y1, wide(w_rows, slot, j, first + 2), zero),
                        )
            before = None
            for x in range(size_x):
                here = xl == float(x)
                for part in range(2):
                    for dz in range(2):
                        value = jnp.where(here, lines[part, 0, dz], zero)
                        if before is not None:
                            value = jnp.where(before, lines[part, 1, dz], value)
                        column = (j * 2 + dz) * verts
                        a_buf[slot, part, x * 16 : (x + 1) * 16, column : column + verts] = value
                before = here
            force = [wide(f_rows, slot, j, part * 4 + c) for part in range(2) for c in range(3)]
            for zb in range(size_z // 16):
                for dz in range(2):
                    at_z = iota_y == zl + float(dz - 16 * zb)
                    column = (j * 2 + dz) * verts
                    for part in range(2):
                        for c in range(3):
                            line = (part * 3 + c) * size_z + zb * 16
                            zf_buf[slot, line : line + 16, column : column + verts] = jnp.where(
                                at_z, force[part * 3 + c], zero
                            )

    def product(slot, blocks=SLOT_CAP):
        lines = 3 * size_z
        depth = blocks * 2 * verts
        high = lax.dot_general(
            zf_buf[slot, :, :depth], a_buf[slot, 0, :, :depth], NT, preferred_element_type=F32
        )
        low = lax.dot_general(
            zf_buf[slot, :lines, :depth],
            a_buf[slot, 1, :, :depth],
            NT,
            preferred_element_type=F32,
        )
        total[...] += high[:lines] + high[lines:] + low

    return build, product


def pair_blocks(table_ref, step):
    return [block_rows(table_ref, 2 * step + oo, j) for oo in range(2) for j in range(2)]


def spread_kernel(extent, place_ref, table_ref, total, packed, spot_ref, *scratch):
    owners, _, _, verts = table_ref.shape
    build, product = spread_tools(place_ref, extent, verts, total, *scratch)
    steps = owners // 2
    total[...] = jnp.zeros(total.shape, F32)
    packed[...] = jnp.zeros(packed.shape, F32)
    build(pair_blocks(table_ref, 0), 0)

    def near(i, spot):
        build(pair_blocks(table_ref, 2 * i + 1), 1)
        product(0)
        for owner in range(2):
            spot = pack_far(table_ref, packed, spot_ref, 4 * i + owner, spot)
        build(pair_blocks(table_ref, jnp.minimum(2 * i + 2, steps - 1)), 0)
        product(1)
        for owner in range(2, 4):
            spot = pack_far(table_ref, packed, spot_ref, 4 * i + owner, spot)
        return spot

    spot_ref[2 * owners] = lax.fori_loop(0, steps // 2, near, jnp.int32(0))

    @pl.loop(0, packed_blocks(spot_ref[2 * owners], verts))
    def _(block):
        build([packed_rows(packed, block)], 0)
        product(0, 1)


def spread(place, table, extent):
    owners, _, _, verts = table.shape
    size_x, size_y, size_z = extent
    cross = size_x * size_y
    return pl.pallas_call(
        functools.partial(spread_kernel, extent),
        out_shape=(
            jax.ShapeDtypeStruct((3 * size_z, cross), F32),
            jax.ShapeDtypeStruct((2 * owners + 2, 16, verts), F32),
            jax.ShapeDtypeStruct((2 * owners + 1,), jnp.int32),
        ),
        in_specs=[smem(), vmem()],
        out_specs=(vmem(), vmem(), smem()),
        scratch_shapes=spread_scratch(extent, verts),
        compiler_params=settings(16),
        cost_estimate=cost(18 * owners * 3 * size_z * cross * 4 * verts, MIB),
        name="spread",
    )(place, table)


def along(vector, q):
    value = None
    for c in range(3):
        move = VELOCITIES[q][c]
        if move == 0:
            continue
        if value is None:
            value = vector[c] if move > 0 else -vector[c]
        else:
            value = value + vector[c] if move > 0 else value - vector[c]
    return value


def collide_plane(x, force, pop, solid):
    factor = 1.0 - 0.5 / RELAXATION
    rate = 1.0 / RELAXATION
    keep = 1.0 - rate
    cells = [pop[q, x] for q in range(19)]
    wall = solid[x] == 1
    rho = cells[0]
    for q in range(1, 19):
        rho = rho + cells[q]
    moment = []
    for c in range(3):
        value = None
        for q in range(1, 19, 2):
            if VELOCITIES[q][c] != 0:
                term = cells[q] - cells[q + 1]
                if VELOCITIES[q][c] < 0:
                    term = -term
                value = term if value is None else value + term
        moment.append(value)
    inverse = 1.0 / rho
    vel = [(moment[c] + 0.5 * force[c]) * inverse for c in range(3)]
    speed = vel[0] * vel[0] + vel[1] * vel[1] + vel[2] * vel[2]
    u_dot_f = vel[0] * force[0] + vel[1] * force[1] + vel[2] * force[2]
    three = 3.0 * factor
    nine = 9.0 * factor
    rest = (rate * rho) * (1.0 - 1.5 * speed) - three * u_dot_f
    quad = (4.5 * rate) * rho
    linear = (3.0 * rate) * rho
    results = [None] * 19
    results[0] = jnp.where(wall, cells[0], keep * cells[0] + LATTICE_WEIGHTS[0] * rest)

    for q in range(1, 19, 2):
        a = along(vel, q)
        b = along(force, q)
        weight = LATTICE_WEIGHTS[q]
        even = weight * (rest + a * (quad * a + nine * b))
        odd = weight * (linear * a + three * b)
        results[q] = jnp.where(wall, cells[q + 1], keep * cells[q] + (even + odd))
        results[q + 1] = jnp.where(wall, cells[q], keep * cells[q + 1] + (even - odd))
    return results, vel


def face_kernel(total, pop, solid, xface_ref, field):
    size_x, size_y, size_z = solid.shape
    for c in range(3):
        for half in range(size_x * size_y // 128):
            field[c, half * 128 : (half + 1) * 128, :] = jnp.transpose(
                total[c * size_z : (c + 1) * size_z, half * 128 : (half + 1) * 128]
            )
    for x, first, sign in ((size_x - 1, 0, 1), (0, 5, -1)):
        force = [field[c, x * size_y : (x + 1) * size_y, :] for c in range(3)]
        results, _ = collide_plane(x, force, pop, solid)
        for k, q in enumerate(X_LISTS[sign]):
            xface_ref[first + k] = results[q]


def x_faces(total, populations, solid):
    _, size_x, size_y, size_z = populations.shape
    return pl.pallas_call(
        face_kernel,
        out_shape=(
            jax.ShapeDtypeStruct((10, size_y, size_z), F32),
            jax.ShapeDtypeStruct((3, size_x * size_y, size_z), F32),
        ),
        in_specs=[vmem()] * 3,
        out_specs=(vmem(),) * 2,
        compiler_params=settings(12),
        cost_estimate=cost(2 * MIB, MIB),
        name="x_faces",
    )(total, populations, solid)


def collide_kernel(field, pop, solid, post, yfp_ref, yfm_ref, zfp_ref, zfm_ref, unit_ref):
    _, size_x, size_y, size_z = post.shape
    lane = lax.broadcasted_iota(jnp.int32, (size_y, size_z), 1)

    def plane(x, z_out):
        z_out = dict(zip((1, -1), z_out))
        lines = pl.ds(pl.multiple_of(x * 16, 16), 16)
        force = [field[c, lines, :] for c in range(3)]
        results, vel = collide_plane(x, force, pop, solid)
        for c in range(3):
            high, low = halves(vel[c])
            first = pl.ds(pl.multiple_of((x * 3 + c) * 16, 16), 16)
            unit_ref[first, 0:size_z] = high.astype(BF)
            unit_ref[first, size_z : 2 * size_z] = low.astype(BF)
        for q in range(19):
            post[q, x] = results[q]
        for sign, line, face in ((1, size_y - 1, yfp_ref), (-1, 0, yfm_ref)):
            for k, q in enumerate(Y_LISTS[sign]):
                face[k, pl.ds(x, 1), :] = results[q][line : line + 1, :]
        for sign, column in ((1, size_z - 1), (-1, 0)):
            for k, q in enumerate(Z_LISTS[sign]):
                place = k * 16 + x
                moved = pltpu.roll(results[q], (place - column + size_z) & (size_z - 1), 1)
                z_out[sign] = jnp.where(lane == place, moved, z_out[sign])
        return z_out[1], z_out[-1]

    empty = jnp.zeros((size_y, size_z), F32)
    zfp_ref[...], zfm_ref[...] = lax.fori_loop(0, size_x, plane, (empty, empty), unroll=2)


def collide(field, populations, solid):
    _, size_x, size_y, size_z = populations.shape
    face_y = jax.ShapeDtypeStruct((5, size_x, size_z), F32)
    face_z = jax.ShapeDtypeStruct((size_y, size_z), F32)
    return pl.pallas_call(
        collide_kernel,
        out_shape=(
            jax.ShapeDtypeStruct(populations.shape, F32),
            face_y,
            face_y,
            face_z,
            face_z,
            jax.ShapeDtypeStruct((size_x * size_y * 3, 2 * size_z), BF),
        ),
        in_specs=[vmem()] * 3,
        out_specs=(vmem(),) * 6,
        compiler_params=settings(12),
        cost_estimate=cost(16 * MIB, 8 * MIB),
        name="collide",
    )(field, populations, solid)


def sample_scratch(extent, verts):
    size_x, size_y, size_z = extent
    return [
        pltpu.VMEM((2, SLOT_CAP, 2 * size_z, 2 * verts), BF),
        pltpu.VMEM((2, 3 * size_x * size_y, 2 * verts), F32),
        pltpu.VMEM((2, SLOT_CAP, 8, verts), F32),
        pltpu.VMEM((2, SLOT_CAP, 8, verts), F32),
    ]


def sample_tools(place_ref, unit_ref, extent, verts, hot, grid_buf, w_rows, c_rows):
    size_x, size_y, size_z = extent
    iota_y = lax.broadcasted_iota(jnp.int32, (16, verts), 0).astype(F32)
    iota_b = iota_y.astype(BF)
    one = jnp.ones((16, verts), BF)
    zero_b = jnp.zeros((16, verts), BF)
    zero = jnp.zeros((16, verts), F32)

    def wide(ref, slot, j, row):
        return jnp.broadcast_to(ref[slot, j, row : row + 1, :], (16, verts))

    def prepare(blocks, slot):
        for j, rows in enumerate(blocks):
            weight, _, local = place_rows(place_ref, rows, extent)
            w_rows[slot, j] = weight
            for d in range(3):
                c_rows[slot, j, d : d + 1] = local[d]
        for j in range(len(blocks)):
            zl = wide(c_rows, slot, j, 2).astype(BF)
            for zb in range(size_z // 16):
                for dz in range(2):
                    value = jnp.where(iota_b == zl + float(dz - 16 * zb), one, zero_b)
                    for part in range(2):
                        line = part * size_z + zb * 16
                        hot[slot, j, line : line + 16, dz * verts : (dz + 1) * verts] = value

    def product(slot, j):
        grid_buf[j % 2] = lax.dot_general(unit_ref[...], hot[slot, j], NN, preferred_element_type=F32)

    def select(slot, j):
        xl = wide(c_rows, slot, j, 0)
        yl = wide(c_rows, slot, j, 1)
        at_y0 = iota_y == yl
        at_y1 = iota_y == yl + 1.0
        lines = {}
        for dx in range(2):
            for dz in range(2):
                first = dx * 4 + dz
                lines[dx, dz] = jnp.where(
                    at_y0,
                    wide(w_rows, slot, j, first),
                    jnp.where(at_y1, wide(w_rows, slot, j, first + 2), zero),
                )
        sums = [zero, zero, zero]
        before = None
        for x in range(size_x):
            here = xl == float(x)
            for dz in range(2):
                value = jnp.where(here, lines[0, dz], zero)
                if before is not None:
                    value = jnp.where(before, lines[1, dz], value)
                for c in range(3):
                    first = (x * 3 + c) * 16
                    part = grid_buf[j % 2, first : first + 16, dz * verts : (dz + 1) * verts]
                    sums[c] = sums[c] + value * part
            before = here
        return [jnp.sum(value, axis=0, keepdims=True) for value in sums]

    def work(slot, store):
        product(slot, 0)
        for j in range(SLOT_CAP):
            if j + 1 < SLOT_CAP:
                product(slot, j + 1)
            store(j, select(slot, j))

    return prepare, product, select, work


def x_plane(xr_ref, q):
    sign = VELOCITIES[q][0]
    return xr_ref[(0 if sign > 0 else 5) + X_LISTS[sign].index(q)]


def sample_steps(table_ref, first, last, prepare, work, put):
    def store(step):
        return lambda j, values: put(2 * step + j // 2, j % 2, values)

    prepare(pair_blocks(table_ref, first), 0)

    @pl.loop(0, (last - first) // 2)
    def _(i):
        step = first + 2 * i
        prepare(pair_blocks(table_ref, step + 1), 1)
        work(0, store(step))
        prepare(pair_blocks(table_ref, jnp.minimum(step + 2, last - 1)), 0)
        work(1, store(step + 1))


def sample_part_kernel(extent, first, last, place_ref, table_ref, unit_ref, *refs):
    out_ref, scratch = refs[-5], refs[-4:]
    verts = table_ref.shape[3]
    prepare, _, _, work = sample_tools(place_ref, unit_ref, extent, verts, *scratch)

    def put(owner, line, values):
        for c in range(3):
            out_ref[owner - 2 * first, c, line : line + 1, :] = values[c]

    sample_steps(table_ref, first, last, prepare, work, put)


def sample_part(place, table, unit, order, first, last, extent):
    owners, _, _, verts = table.shape
    size_x, size_y, size_z = extent
    return pl.pallas_call(
        functools.partial(sample_part_kernel, extent, first, last),
        out_shape=jax.ShapeDtypeStruct((2 * (last - first), 3, 2, verts), F32),
        in_specs=[smem(), vmem(), vmem()] + [pl.BlockSpec(memory_space=pl.ANY)] * len(order),
        out_specs=vmem(),
        scratch_shapes=sample_scratch(extent, verts),
        compiler_params=settings(12),
        cost_estimate=cost(
            32 * (last - first) * 3 * size_x * size_y * size_z * verts, MIB
        ),
        name="sample_part",
    )(place, table, unit, *order)


def sample_kernel(
    extent, place_ref, spot_ref, table_ref, packed, unit_ref, part_ref, *refs
):
    out_ref, found, scratch = refs[-6], refs[-5], refs[-4:]
    owners, _, _, verts = table_ref.shape
    prepare, product, select, work = sample_tools(place_ref, unit_ref, extent, verts, *scratch)
    done = part_ref.shape[0]
    for c in range(3):
        out_ref[0:done, c, 0:2] = part_ref[:, c]
        out_ref[:, c, 2:4] = jnp.zeros((owners, 2, verts), F32)

    def put(owner, line, values):
        for c in range(3):
            out_ref[owner, c, line : line + 1, :] = values[c]

    sample_steps(table_ref, done // 2, owners // 2, prepare, work, put)

    @pl.loop(0, packed_blocks(spot_ref[2 * owners], verts))
    def _(block):
        prepare([packed_rows(packed, block)], 0)
        product(0, 0)
        values = select(0, 0)
        for c in range(3):
            found[block, c : c + 1, :] = values[c]

    lane = lax.broadcasted_iota(jnp.int32, (4, verts), 1)
    for owner in range(owners):
        for j in range(2):
            spot = spot_ref[2 * owner + j]

            @pl.when(spot_ref[2 * owner + j + 1] > spot)
            def _(owner=owner, j=j, spot=spot):
                block = lax.shift_right_logical(spot, 7)
                shift = spot & (verts - 1)
                back = (verts - shift) & (verts - 1)
                first = pltpu.roll(found[block, 0:4], back, 1)
                second = pltpu.roll(found[block + 1, 0:4], back, 1)
                value = jnp.where(lane < verts - shift, first, second)
                for c in range(3):
                    out_ref[owner, c, 2 + j : 3 + j, :] = value[c : c + 1]


def sample(place, spots, table, packed, unit, part, order, extent):
    owners, _, _, verts = table.shape
    size_x, size_y, size_z = extent
    return pl.pallas_call(
        functools.partial(sample_kernel, extent),
        out_shape=jax.ShapeDtypeStruct((owners, 3, SLOT_CAP, verts), F32),
        in_specs=[smem(), smem()]
        + [vmem()] * 4
        + [pl.BlockSpec(memory_space=pl.ANY)] * len(order),
        out_specs=vmem(),
        scratch_shapes=[pltpu.VMEM((2 * owners + 2, 8, verts), F32)]
        + sample_scratch(extent, verts),
        compiler_params=settings(12),
        cost_estimate=cost(8 * owners * 3 * size_x * size_y * size_z * verts, MIB),
        name="sample_velocity",
    )(place, spots, table, packed, unit, part, *order)


def y_message_kernel(xr_ref, yfp_ref, yfm_ref, plus_ref, minus_ref):
    size_y = xr_ref.shape[1]
    for sign, face, out in ((1, yfp_ref, plus_ref), (-1, yfm_ref, minus_ref)):
        out[0:5] = face[...]
        line = size_y - 1 if sign > 0 else 0
        for e, q in enumerate(Y_EDGES[sign]):
            out[5, e : e + 1, :] = x_plane(xr_ref, q)[line : line + 1, :]


def y_messages(x_halo, y_plus, y_minus):
    shape = jax.ShapeDtypeStruct((6,) + y_plus.shape[1:], F32)
    return pl.pallas_call(
        y_message_kernel,
        out_shape=(shape, shape),
        in_specs=[vmem()] * 3,
        out_specs=(vmem(), vmem()),
        compiler_params=settings(4),
        name="y_messages",
    )(x_halo, y_plus, y_minus)


def z_message_kernel(xr_ref, yrp_ref, yrm_ref, zfp_ref, zfm_ref, plus_ref, minus_ref):
    size_y, size_z = zfp_ref.shape
    y_halo = {1: yrp_ref, -1: yrm_ref}
    lane = lax.broadcasted_iota(jnp.int32, (size_y, size_z), 1)
    for sign, face, out in ((1, zfp_ref, plus_ref), (-1, zfm_ref, minus_ref)):
        column = size_z - 1 if sign > 0 else 0
        block = face[...]
        for e, q in enumerate(Z_EDGES[sign]):
            if VELOCITIES[q][0] != 0:
                plane = x_plane(xr_ref, q)
            else:
                y_sign = VELOCITIES[q][1]
                plane = y_halo[y_sign][Y_LISTS[y_sign].index(q)]
            spot = EDGE_LANE + e
            block = jnp.where(lane == spot, pltpu.roll(plane, (spot - column) % size_z, 1), block)
        out[...] = block


def z_messages(x_halo, y_plus, y_minus, z_plus, z_minus):
    shape = jax.ShapeDtypeStruct(z_plus.shape, F32)
    return pl.pallas_call(
        z_message_kernel,
        out_shape=(shape, shape),
        in_specs=[vmem()] * 5,
        out_specs=(vmem(), vmem()),
        compiler_params=settings(4),
        name="z_messages",
    )(x_halo, y_plus, y_minus, z_plus, z_minus)


def stream_kernel(
    post,
    xr_ref,
    yrp_ref,
    yrm_ref,
    zrp_ref,
    zrm_ref,
    read_hbm,
    read,
    out_sem,
):
    _, size_x, size_y, size_z = post.shape
    y_halo = {1: yrp_ref, -1: yrm_ref}
    z_halo = {1: zrp_ref, -1: zrm_ref}
    stores = [pltpu.make_async_copy(read.at[q], read_hbm.at[q], out_sem.at[q]) for q in range(19)]
    lane = lax.broadcasted_iota(jnp.int32, (size_y, size_z), 1)
    row = lax.broadcasted_iota(jnp.int32, (size_y, size_z), 0)

    def shift_z(plane, cz, place):
        moved = pltpu.roll(plane, cz % size_z, 1)
        target = 0 if cz > 0 else size_z - 1
        column = pltpu.roll(z_halo[cz][...], (target - place) % size_z, 1)
        return jnp.where(lane == target, column, moved)

    for q in range(19):
        cx, cy, cz = VELOCITIES[q]
        rows = None
        if cy != 0:
            rows = y_halo[cy][Y_LISTS[cy].index(q)]
            if cz != 0:
                rows = shift_z(rows, cz, EDGE_LANE + Z_EDGES[cz].index(q))
        for x in range(size_x):
            source = x - cx
            outside = source < 0 or source >= size_x
            plane = x_plane(xr_ref, q) if outside else post[q, source]
            if cz != 0:
                if outside:
                    place = EDGE_LANE + Z_EDGES[cz].index(q)
                else:
                    place = Z_LISTS[cz].index(q) * 16 + source
                plane = shift_z(plane, cz, place)
            if cy != 0:
                moved = pltpu.roll(plane, cy % size_y, 0)
                target = 0 if cy > 0 else size_y - 1
                if outside:
                    e = Y_EDGES[cy].index(q)
                    line = y_halo[cy][5, e : e + 1, :]
                else:
                    line = rows[source : source + 1, :]
                plane = jnp.where(row == target, jnp.broadcast_to(line, moved.shape), moved)
            read[q, x] = plane
        stores[q].start()
    for store in stores:
        store.wait()


def stream(post, x_halo, y_plus, y_minus, z_plus, z_minus):
    anyspace = pl.BlockSpec(memory_space=pl.ANY)
    return pl.pallas_call(
        stream_kernel,
        out_shape=jax.ShapeDtypeStruct(post.shape, F32),
        in_specs=[vmem()] * 6,
        out_specs=anyspace,
        scratch_shapes=[
            pltpu.VMEM(post.shape, F32),
            pltpu.SemaphoreType.DMA((19,)),
        ],
        compiler_params=settings(10),
        cost_estimate=cost(MIB, 16 * MIB),
        name="stream_populations",
    )(post, x_halo, y_plus, y_minus, z_plus, z_minus)


def collect_kernel(inter_ref, base_ref, rank_ref, back_ref, out_ref):
    patches, verts = rank_ref.shape[1:]
    line = lax.broadcasted_iota(jnp.int32, (16, verts), 0) & (SLOT_CAP - 1)
    for p in range(patches):
        value = None
        for i in range(2):
            brick = inter_ref[i, p]
            base = base_ref[2 * p + i]
            rank = jnp.broadcast_to(rank_ref[i, p : p + 1, :], (8, verts))
            spot = jnp.concatenate([rank + base] * 2, axis=0)
            rows = [back_ref[brick, c] for c in range(3)] + [jnp.zeros((4, verts), F32)]
            picked = jnp.concatenate(rows, axis=0)
            picked = jnp.take_along_axis(picked, spot & (verts - 1), axis=1)
            here = lax.shift_right_logical(spot, 7) == line
            picked = jnp.where(here & (jnp.concatenate([rank] * 2, axis=0) >= 0), picked, 0.0)
            value = picked if value is None else value + picked
        value = value + pltpu.roll(value, 15, 0)
        value = value + pltpu.roll(value, 14, 0)
        value = jnp.concatenate([value[4 * c : 4 * c + 1] for c in range(3)], axis=0)
        out_ref[:, p, :] = value


def collect(intersection, bases, ranks, back):
    _, patches, verts = ranks.shape
    return pl.pallas_call(
        collect_kernel,
        out_shape=jax.ShapeDtypeStruct((3, patches, verts), F32),
        in_specs=[smem()] * 2 + [vmem()] * 2,
        out_specs=vmem(),
        compiler_params=settings(4),
        name="collect_velocity",
    )(intersection, bases, ranks, back)


def shifted(value, axis, step):
    count = lax.axis_size(axis)
    return lax.ppermute(value, axis, [(i, (i + step) % count) for i in range(count)])


def exchanged(value):
    return lax.all_to_all(value, ("gy", "gz"), split_axis=0, concat_axis=0, tiled=True)


def body(populations, solid_flags, positions, anchors, base_cell, weights, intersection):
    extent = populations.shape[1:]
    axes = ("gx", "gy", "gz")
    bricks = lax.axis_size("gy") * lax.axis_size("gz")
    here = [lax.axis_index(axis) for axis in axes]
    place = jnp.stack(
        [here[d] * extent[d] for d in range(3)]
        + here
        + [jnp.int32(lax.axis_size(axis)) for axis in axes]
    ).astype(jnp.int32)
    lists = intersection.T
    outgoing, ranks, bases = build_lists(
        lists,
        jnp.transpose(positions, (1, 0, 2)),
        jnp.transpose(anchors, (1, 0, 2)),
        jnp.transpose(base_cell, (1, 0, 2)),
        weights,
        bricks,
        lax.axis_size("gz"),
        extent,
    )
    table = exchanged(outgoing)
    total, packed, spots = spread(place, table, extent)
    x_face, field = x_faces(total, populations, solid_flags)
    post, y_plus, y_minus, z_plus, z_minus, unit = collide(field, populations, solid_flags)
    if lax.axis_size("gx") == 2:
        x_halo = shifted(x_face, "gx", 1)
    else:
        x_halo = jnp.concatenate(
            [shifted(x_face[:5], "gx", 1), shifted(x_face[5:], "gx", -1)], axis=0
        )
    y_plus, y_minus = y_messages(x_halo, y_plus, y_minus)
    y_plus = shifted(y_plus, "gy", 1)
    y_minus = shifted(y_minus, "gy", -1)
    steps = table.shape[0] // 2
    part = sample_part(place, table, unit, (x_halo,), 0, steps // 4 * 3, extent)
    order = (y_plus, y_minus)
    sampled = sample(place, spots, table, packed, unit, part, order, extent)
    back = exchanged(sampled)
    z_plus, z_minus = z_messages(x_halo, y_plus, y_minus, z_plus, z_minus)
    z_plus = shifted(z_plus, "gz", 1)
    z_minus = shifted(z_minus, "gz", -1)
    read = stream(post, x_halo, y_plus, y_minus, z_plus, z_minus)
    velocity = collect(lists, bases, ranks, back)
    return read, jnp.transpose(velocity, (1, 0, 2))


def solution(mesh):
    return jax.shard_map(
        body,
        mesh=mesh,
        in_specs=(
            P(None, "gx", "gy", "gz"),
            P("gx", "gy", "gz"),
            P(("gx", "gy", "gz"), None, None),
            P(("gx", "gy", "gz"), None, None),
            P(("gx", "gy", "gz"), None, None),
            P(("gx", "gy", "gz"), None, None),
            P(("gx", "gy", "gz"), None),
        ),
        out_specs=(P(None, "gx", "gy", "gz"), P(("gx", "gy", "gz"), None, None)),
        check_vma=False,
    )
```

```python
import functools

import jax
import jax.numpy as jnp
from jax import lax
from jax.experimental import pallas as pl
from jax.experimental.pallas import tpu as pltpu
from jax.sharding import PartitionSpec as P

SLOT_CAP = 4
GROUPS = 7
EDGE_LANE = 80

RELAXATION = 0.8
TENSION = 0.05
TETHER = 0.5
VELOCITIES = [
    (0, 0, 0),
    (1, 0, 0),
    (-1, 0, 0),
    (0, 1, 0),
    (0, -1, 0),
    (0, 0, 1),
    (0, 0, -1),
    (1, 1, 0),
    (-1, -1, 0),
    (1, -1, 0),
    (-1, 1, 0),
    (1, 0, 1),
    (-1, 0, -1),
    (1, 0, -1),
    (-1, 0, 1),
    (0, 1, 1),
    (0, -1, -1),
    (0, 1, -1),
    (0, -1, 1),
]
LATTICE_WEIGHTS = [1.0 / 3.0] + [1.0 / 18.0] * 6 + [1.0 / 36.0] * 12


def crossing(axis, sign):
    return [q for q in range(19) if VELOCITIES[q][axis] == sign]


X_LISTS = {1: crossing(0, 1), -1: crossing(0, -1)}
Y_LISTS = {1: crossing(1, 1), -1: crossing(1, -1)}
Z_LISTS = {1: crossing(2, 1), -1: crossing(2, -1)}
Y_EDGES = {s: [q for q in Y_LISTS[s] if VELOCITIES[q][0] != 0] for s in (1, -1)}
Z_EDGES = {
    s: [q for q in Z_LISTS[s] if VELOCITIES[q][0] != 0 or VELOCITIES[q][1] != 0] for s in (1, -1)
}

BF = jnp.bfloat16
F32 = jnp.float32
MIB = 1024 * 1024
NT = (((1,), (1,)), ((), ()))
NN = (((1,), (0,)), ((), ()))


def settings(mib):
    return pltpu.CompilerParams(vmem_limit_bytes=mib * MIB)


def cost(flops, size):
    return pl.CostEstimate(flops=flops, bytes_accessed=size, transcendentals=0)


def vmem():
    return pl.BlockSpec(memory_space=pltpu.VMEM)


def smem():
    return pl.BlockSpec(memory_space=pltpu.SMEM)


def list_kernel(
    bricks_z,
    inter_ref,
    pos_ref,
    anchor_ref,
    cell_ref,
    weight_ref,
    out_ref,
    rank_ref,
    base_ref,
    payload,
    lists,
    count_ref,
    extent,
):
    patches, verts = pos_ref.shape[1:]
    bricks = out_ref.shape[0]
    pos = pos_ref[...]
    cycle_term = pltpu.roll(pos, 1, 2) + pltpu.roll(pos, verts - 1, 2) - 2.0 * pos
    forces = TENSION * cycle_term + TETHER * (anchor_ref[...] - pos)
    cells = cell_ref[...].astype(F32)
    payload[:, 0:8, :] = weight_ref[...]
    for p in range(patches):
        payload[p, 8:11, :] = forces[:, p, :]
        payload[p, 11:14, :] = cells[:, p, :] + 1.0
        payload[p, 14:16, :] = jnp.zeros((2, verts), F32)
    lists[...] = jnp.zeros(lists.shape, F32)

    @pl.loop(0, bricks)
    def _(b):
        count_ref[b] = 0

    lane = lax.broadcasted_iota(jnp.int32, (patches, verts), 1)
    row = lax.broadcasted_iota(jnp.int32, (patches, verts), 0)
    upper = (
        lax.broadcasted_iota(jnp.int32, (verts, verts), 0)
        <= lax.broadcasted_iota(jnp.int32, (verts, verts), 1)
    ).astype(F32)
    codes, sums = [], []
    for i in range(2):
        first_y = jnp.zeros((patches, verts), F32)
        first_z = jnp.zeros((patches, verts), F32)
        for p in range(patches):
            brick = inter_ref[i, p]
            first_y = jnp.where(row == p, (brick // bricks_z * extent[1]).astype(F32), first_y)
            first_z = jnp.where(row == p, (brick % bricks_z * extent[2]).astype(F32), first_z)
        live = (
            (cells[1] >= first_y)
            & (cells[1] < first_y + extent[1])
            & (cells[2] >= first_z)
            & (cells[2] < first_z + extent[2])
        )
        mask = live.astype(F32)
        total = jnp.dot(mask.astype(BF), upper.astype(BF), preferred_element_type=F32)
        rank = (total - mask).astype(jnp.int32)
        rank_ref[i] = jnp.where(live, rank, -1)
        code = jnp.where(live, (lane - rank) + lane * 256 + 65536, 0)
        step = 1
        while step < verts:
            moving = jnp.where((code & step) != 0, code, 0)
            code = (code - moving) + pltpu.roll(moving, verts - step, 1)
            step *= 2
        codes.append(code)
        sums.append(total)
    wide_lane = lax.broadcasted_iota(jnp.int32, (16, verts), 1)
    for p in range(patches):
        for i in range(2):
            brick = inter_ref[i, p]
            base = count_ref[brick]
            base_ref[2 * p + i] = base
            count_ref[brick] = base + jnp.max(sums[i][p : p + 1, :]).astype(jnp.int32)
            block = lax.shift_right_logical(base, 7)
            shift = base & (verts - 1)
            code = jnp.broadcast_to(codes[i][p : p + 1, :], (8, verts))
            code = pltpu.roll(code, shift, 1)
            code = jnp.concatenate([code, code], axis=0)
            source = lax.shift_right_logical(code, 8) & (verts - 1)
            moved = jnp.take_along_axis(payload[p], source, axis=1)
            moved = jnp.where(code >= 65536, moved, 0.0)
            lists[brick, block] += jnp.where(wide_lane >= shift, moved, 0.0)
            lists[brick, block + 1] += jnp.where(wide_lane < shift, moved, 0.0)

    @pl.loop(0, bricks)
    def _(b):
        for j in range(SLOT_CAP):
            value = lists[b, j]
            first = j // 2 * GROUPS
            for g in range(3):
                out_ref[b, first + j % 2 * 3 + g] = value[4 * g : 4 * g + 4]
            out_ref[b, first + 6, j % 2 * 2 : j % 2 * 2 + 2] = value[12:14]


def build_lists(intersection, positions, anchors, base_cell, weights, bricks, bricks_z, extent):
    _, patches, verts = positions.shape

    def kernel(*refs):
        list_kernel(bricks_z, *refs, extent)

    return pl.pallas_call(
        kernel,
        out_shape=(
            jax.ShapeDtypeStruct((bricks, 2 * GROUPS, 4, verts), F32),
            jax.ShapeDtypeStruct((2, patches, verts), jnp.int32),
            jax.ShapeDtypeStruct((2 * patches,), jnp.int32),
        ),
        in_specs=[smem(), vmem(), vmem(), vmem(), vmem()],
        out_specs=(vmem(), vmem(), smem()),
        scratch_shapes=[
            pltpu.VMEM((patches, 16, verts), F32),
            pltpu.VMEM((bricks, SLOT_CAP + 1, 16, verts), F32),
            pltpu.SMEM((bricks,), jnp.int32),
        ],
        compiler_params=settings(56),
        name="vertex_lists",
    )(intersection, positions, anchors, base_cell, weights)


def block_rows(table_ref, owner, j):
    first = j // 2 * GROUPS
    group = first + j % 2 * 3
    weight = jnp.concatenate([table_ref[owner, group], table_ref[owner, group + 1]], axis=0)
    third = table_ref[owner, group + 2]
    line = j % 2 * 2
    last = table_ref[owner, first + 6, line : line + 2]
    return weight, third[0:3], jnp.concatenate([third[3:4], last], axis=0)


def pack_far(table_ref, packed, spot_ref, owner, spot):
    verts = table_ref.shape[3]
    lane = lax.broadcasted_iota(jnp.int32, (16, verts), 1)
    for j in range(2):
        weight, force, cells = block_rows(table_ref, owner, 2 + j)
        held = (cells[0:1] > 0.0).astype(F32)
        rows = jnp.concatenate([weight, force, cells, jnp.zeros((2, verts), F32)], axis=0)
        spot_ref[2 * owner + j] = spot
        block = lax.shift_right_logical(spot, 7)
        shift = spot & (verts - 1)
        rows = pltpu.roll(rows, shift, 1)
        packed[block] += jnp.where(lane >= shift, rows, 0.0)
        packed[block + 1] += jnp.where(lane < shift, rows, 0.0)
        spot = spot + jnp.sum(held).astype(jnp.int32)
    return spot


def packed_blocks(spot, verts):
    return lax.shift_right_logical(spot + verts - 1, 7)


def packed_rows(packed, block):
    return packed[block, 0:8], packed[block, 8:11], packed[block, 11:14]


def place_rows(place_ref, rows, extent):
    weight, force, cells = rows
    local, inside = [], None
    for d in range(3):
        value = cells[d : d + 1] - (place_ref[d] + 1).astype(F32)
        ok = (value >= 0.0) & (value < float(extent[d]))
        inside = ok if inside is None else inside & ok
        local.append(value)
    weight = weight * jnp.broadcast_to(inside.astype(F32), weight.shape)
    return weight, force, local


def halves(value):
    high = value.astype(BF).astype(F32)
    return high, value - high


def spread_scratch(extent, verts):
    size_x, size_y, size_z = extent
    depth = SLOT_CAP * 2 * verts
    return [
        pltpu.VMEM((2, 2, size_x * size_y, depth), BF),
        pltpu.VMEM((2, 6 * size_z, depth), BF),
        pltpu.VMEM((2, SLOT_CAP, 16, verts), F32),
        pltpu.VMEM((2, SLOT_CAP, 8, verts), F32),
        pltpu.VMEM((2, SLOT_CAP, 8, verts), F32),
    ]


def spread_tools(place_ref, extent, verts, total, a_buf, zf_buf, w_rows, f_rows, c_rows):
    size_x, size_y, size_z = extent
    iota_y = lax.broadcasted_iota(jnp.int32, (16, verts), 0).astype(F32).astype(BF)
    zero = jnp.zeros((16, verts), BF)

    def wide(ref, slot, j, row):
        return jnp.broadcast_to(ref[slot, j, row : row + 1, :], (16, verts)).astype(BF)

    def build(blocks, slot):
        for j, rows in enumerate(blocks):
            weight, force, local = place_rows(place_ref, rows, extent)
            w_hi, w_lo = halves(weight)
            f_hi, f_lo = halves(force)
            w_rows[slot, j, 0:8] = w_hi
            w_rows[slot, j, 8:16] = w_lo
            f_rows[slot, j, 0:3] = f_hi
            f_rows[slot, j, 4:7] = f_lo
            for d in range(3):
                c_rows[slot, j, d : d + 1] = local[d]
        for j in range(len(blocks)):
            xl = wide(c_rows, slot, j, 0)
            yl = wide(c_rows, slot, j, 1)
            zl = wide(c_rows, slot, j, 2)
            at_y0 = iota_y == yl
            at_y1 = iota_y == yl + 1.0
            lines = {}
            for part in range(2):
                for dx in range(2):
                    for dz in range(2):
                        first = part * 8 + dx * 4 + dz
                        lines[part, dx, dz] = jnp.where(
                            at_y0,
                            wide(w_rows, slot, j, first),
                            jnp.where(at_y1, wide(w_rows, slot, j, first + 2), zero),
                        )
            before = None
            for x in range(size_x):
                here = xl == float(x)
                for part in range(2):
                    for dz in range(2):
                        value = jnp.where(here, lines[part, 0, dz], zero)
                        if before is not None:
                            value = jnp.where(before, lines[part, 1, dz], value)
                        column = (j * 2 + dz) * verts
                        a_buf[slot, part, x * 16 : (x + 1) * 16, column : column + verts] = value
                before = here
            force = [wide(f_rows, slot, j, part * 4 + c) for part in range(2) for c in range(3)]
            for zb in range(size_z // 16):
                for dz in range(2):
                    at_z = iota_y == zl + float(dz - 16 * zb)
                    column = (j * 2 + dz) * verts
                    for part in range(2):
                        for c in range(3):
                            line = (part * 3 + c) * size_z + zb * 16
                            zf_buf[slot, line : line + 16, column : column + verts] = jnp.where(
                                at_z, force[part * 3 + c], zero
                            )

    def product(slot, blocks=SLOT_CAP):
        lines = 3 * size_z
        depth = blocks * 2 * verts
        high = lax.dot_general(
            zf_buf[slot, :, :depth], a_buf[slot, 0, :, :depth], NT, preferred_element_type=F32
        )
        low = lax.dot_general(
            zf_buf[slot, :lines, :depth],
            a_buf[slot, 1, :, :depth],
            NT,
            preferred_element_type=F32,
        )
        total[...] += high[:lines] + high[lines:] + low

    return build, product


def pair_blocks(table_ref, step):
    return [block_rows(table_ref, 2 * step + oo, j) for oo in range(2) for j in range(2)]


def spread_kernel(
    extent,
    place_ref,
    table_ref,
    pop_any,
    total,
    packed,
    spot_ref,
    pop,
    sem,
    *scratch,
):
    load = pltpu.make_async_copy(pop_any, pop, sem)
    load.start()
    owners, _, _, verts = table_ref.shape
    build, product = spread_tools(place_ref, extent, verts, total, *scratch)
    steps = owners // 2
    total[...] = jnp.zeros(total.shape, F32)
    packed[...] = jnp.zeros(packed.shape, F32)
    build(pair_blocks(table_ref, 0), 0)

    def near(i, spot):
        build(pair_blocks(table_ref, 2 * i + 1), 1)
        product(0)
        for owner in range(2):
            spot = pack_far(table_ref, packed, spot_ref, 4 * i + owner, spot)
        build(pair_blocks(table_ref, jnp.minimum(2 * i + 2, steps - 1)), 0)
        product(1)
        for owner in range(2, 4):
            spot = pack_far(table_ref, packed, spot_ref, 4 * i + owner, spot)
        return spot

    spot_ref[2 * owners] = lax.fori_loop(0, steps // 2, near, jnp.int32(0))

    @pl.loop(0, packed_blocks(spot_ref[2 * owners], verts))
    def _(block):
        build([packed_rows(packed, block)], 0)
        product(0, 1)

    load.wait()


def spread(place, table, populations):
    owners, _, _, verts = table.shape
    extent = populations.shape[1:]
    size_x, size_y, size_z = extent
    anyspace = pl.BlockSpec(memory_space=pl.ANY)
    cross = size_x * size_y
    return pl.pallas_call(
        functools.partial(spread_kernel, extent),
        out_shape=(
            jax.ShapeDtypeStruct((3 * size_z, cross), F32),
            jax.ShapeDtypeStruct((2 * owners + 2, 16, verts), F32),
            jax.ShapeDtypeStruct((2 * owners + 1,), jnp.int32),
            jax.ShapeDtypeStruct(populations.shape, F32),
        ),
        in_specs=[smem(), vmem(), anyspace],
        out_specs=(vmem(), vmem(), smem(), vmem()),
        scratch_shapes=[pltpu.SemaphoreType.DMA] + spread_scratch(extent, verts),
        compiler_params=settings(48),
        cost_estimate=cost(18 * owners * 3 * size_z * cross * 4 * verts, MIB),
        name="spread",
    )(place, table, populations)


def along(vector, q):
    value = None
    for c in range(3):
        move = VELOCITIES[q][c]
        if move == 0:
            continue
        if value is None:
            value = vector[c] if move > 0 else -vector[c]
        else:
            value = value + vector[c] if move > 0 else value - vector[c]
    return value


def collide_plane(x, force, pop, solid):
    factor = 1.0 - 0.5 / RELAXATION
    rate = 1.0 / RELAXATION
    keep = 1.0 - rate
    cells = [pop[q, x] for q in range(19)]
    wall = solid[x] == 1
    rho = cells[0]
    for q in range(1, 19):
        rho = rho + cells[q]
    moment = []
    for c in range(3):
        value = None
        for q in range(1, 19, 2):
            if VELOCITIES[q][c] != 0:
                term = cells[q] - cells[q + 1]
                if VELOCITIES[q][c] < 0:
                    term = -term
                value = term if value is None else value + term
        moment.append(value)
    inverse = 1.0 / rho
    vel = [(moment[c] + 0.5 * force[c]) * inverse for c in range(3)]
    speed = vel[0] * vel[0] + vel[1] * vel[1] + vel[2] * vel[2]
    u_dot_f = vel[0] * force[0] + vel[1] * force[1] + vel[2] * force[2]
    three = 3.0 * factor
    nine = 9.0 * factor
    rest = (rate * rho) * (1.0 - 1.5 * speed) - three * u_dot_f
    quad = (4.5 * rate) * rho
    linear = (3.0 * rate) * rho
    results = [None] * 19
    results[0] = jnp.where(wall, cells[0], keep * cells[0] + LATTICE_WEIGHTS[0] * rest)

    for q in range(1, 19, 2):
        a = along(vel, q)
        b = along(force, q)
        weight = LATTICE_WEIGHTS[q]
        even = weight * (rest + a * (quad * a + nine * b))
        odd = weight * (linear * a + three * b)
        results[q] = jnp.where(wall, cells[q + 1], keep * cells[q] + (even + odd))
        results[q + 1] = jnp.where(wall, cells[q], keep * cells[q + 1] + (even - odd))
    return results, vel


def face_kernel(total, pop, solid, xface_ref, field):
    size_x, size_y, size_z = solid.shape
    for c in range(3):
        for half in range(size_x * size_y // 128):
            field[c, half * 128 : (half + 1) * 128, :] = jnp.transpose(
                total[c * size_z : (c + 1) * size_z, half * 128 : (half + 1) * 128]
            )
    for x, first, sign in ((size_x - 1, 0, 1), (0, 5, -1)):
        force = [field[c, x * size_y : (x + 1) * size_y, :] for c in range(3)]
        results, _ = collide_plane(x, force, pop, solid)
        for k, q in enumerate(X_LISTS[sign]):
            xface_ref[first + k] = results[q]


def x_faces(total, populations, solid):
    _, size_x, size_y, size_z = populations.shape
    return pl.pallas_call(
        face_kernel,
        out_shape=(
            jax.ShapeDtypeStruct((10, size_y, size_z), F32),
            jax.ShapeDtypeStruct((3, size_x * size_y, size_z), F32),
        ),
        in_specs=[vmem()] * 3,
        out_specs=(vmem(),) * 2,
        compiler_params=settings(12),
        cost_estimate=cost(2 * MIB, MIB),
        name="x_faces",
    )(total, populations, solid)


def collide_kernel(field, pop, solid, post, yfp_ref, yfm_ref, zfp_ref, zfm_ref, unit_ref):
    _, size_x, size_y, size_z = post.shape
    lane = lax.broadcasted_iota(jnp.int32, (size_y, size_z), 1)

    def plane(x, z_out):
        z_out = dict(zip((1, -1), z_out))
        lines = pl.ds(pl.multiple_of(x * 16, 16), 16)
        force = [field[c, lines, :] for c in range(3)]
        results, vel = collide_plane(x, force, pop, solid)
        for c in range(3):
            high, low = halves(vel[c])
            first = pl.ds(pl.multiple_of((x * 3 + c) * 16, 16), 16)
            unit_ref[first, 0:size_z] = high.astype(BF)
            unit_ref[first, size_z : 2 * size_z] = low.astype(BF)
        for q in range(19):
            post[q, x] = results[q]
        for sign, line, face in ((1, size_y - 1, yfp_ref), (-1, 0, yfm_ref)):
            for k, q in enumerate(Y_LISTS[sign]):
                face[k, pl.ds(x, 1), :] = results[q][line : line + 1, :]
        for sign, column in ((1, size_z - 1), (-1, 0)):
            for k, q in enumerate(Z_LISTS[sign]):
                place = k * 16 + x
                moved = pltpu.roll(results[q], (place - column + size_z) & (size_z - 1), 1)
                z_out[sign] = jnp.where(lane == place, moved, z_out[sign])
        return z_out[1], z_out[-1]

    empty = jnp.zeros((size_y, size_z), F32)
    zfp_ref[...], zfm_ref[...] = lax.fori_loop(0, size_x, plane, (empty, empty), unroll=2)


def collide(field, populations, solid):
    _, size_x, size_y, size_z = populations.shape
    face_y = jax.ShapeDtypeStruct((5, size_x, size_z), F32)
    face_z = jax.ShapeDtypeStruct((size_y, size_z), F32)
    return pl.pallas_call(
        collide_kernel,
        out_shape=(
            jax.ShapeDtypeStruct(populations.shape, F32),
            face_y,
            face_y,
            face_z,
            face_z,
            jax.ShapeDtypeStruct((size_x * size_y * 3, 2 * size_z), BF),
        ),
        in_specs=[vmem()] * 3,
        out_specs=(vmem(),) * 6,
        compiler_params=settings(12),
        cost_estimate=cost(16 * MIB, 8 * MIB),
        name="collide",
    )(field, populations, solid)


def sample_scratch(extent, verts):
    size_x, size_y, size_z = extent
    return [
        pltpu.VMEM((2, SLOT_CAP, 2 * size_z, 2 * verts), BF),
        pltpu.VMEM((2, 3 * size_x * size_y, 2 * verts), F32),
        pltpu.VMEM((2, SLOT_CAP, 8, verts), F32),
        pltpu.VMEM((2, SLOT_CAP, 8, verts), F32),
    ]


def sample_tools(place_ref, unit_ref, extent, verts, hot, grid_buf, w_rows, c_rows):
    size_x, size_y, size_z = extent
    iota_y = lax.broadcasted_iota(jnp.int32, (16, verts), 0).astype(F32)
    iota_b = iota_y.astype(BF)
    one = jnp.ones((16, verts), BF)
    zero_b = jnp.zeros((16, verts), BF)
    zero = jnp.zeros((16, verts), F32)

    def wide(ref, slot, j, row):
        return jnp.broadcast_to(ref[slot, j, row : row + 1, :], (16, verts))

    def prepare(blocks, slot):
        for j, rows in enumerate(blocks):
            weight, _, local = place_rows(place_ref, rows, extent)
            w_rows[slot, j] = weight
            for d in range(3):
                c_rows[slot, j, d : d + 1] = local[d]
        for j in range(len(blocks)):
            zl = wide(c_rows, slot, j, 2).astype(BF)
            for zb in range(size_z // 16):
                for dz in range(2):
                    value = jnp.where(iota_b == zl + float(dz - 16 * zb), one, zero_b)
                    for part in range(2):
                        line = part * size_z + zb * 16
                        hot[slot, j, line : line + 16, dz * verts : (dz + 1) * verts] = value

    def product(slot, j):
        grid_buf[j % 2] = lax.dot_general(unit_ref[...], hot[slot, j], NN, preferred_element_type=F32)

    def select(slot, j):
        xl = wide(c_rows, slot, j, 0)
        yl = wide(c_rows, slot, j, 1)
        at_y0 = iota_y == yl
        at_y1 = iota_y == yl + 1.0
        lines = {}
        for dx in range(2):
            for dz in range(2):
                first = dx * 4 + dz
                lines[dx, dz] = jnp.where(
                    at_y0,
                    wide(w_rows, slot, j, first),
                    jnp.where(at_y1, wide(w_rows, slot, j, first + 2), zero),
                )
        sums = [zero, zero, zero]
        before = None
        for x in range(size_x):
            here = xl == float(x)
            for dz in range(2):
                value = jnp.where(here, lines[0, dz], zero)
                if before is not None:
                    value = jnp.where(before, lines[1, dz], value)
                for c in range(3):
                    first = (x * 3 + c) * 16
                    part = grid_buf[j % 2, first : first + 16, dz * verts : (dz + 1) * verts]
                    sums[c] = sums[c] + value * part
            before = here
        return [jnp.sum(value, axis=0, keepdims=True) for value in sums]

    def work(slot, store):
        product(slot, 0)
        for j in range(SLOT_CAP):
            if j + 1 < SLOT_CAP:
                product(slot, j + 1)
            store(j, select(slot, j))

    return prepare, product, select, work


def x_plane(xr_ref, q):
    sign = VELOCITIES[q][0]
    return xr_ref[(0 if sign > 0 else 5) + X_LISTS[sign].index(q)]


def sample_steps(table_ref, first, last, prepare, work, put):
    def store(step):
        return lambda j, values: put(2 * step + j // 2, j % 2, values)

    prepare(pair_blocks(table_ref, first), 0)

    @pl.loop(0, (last - first) // 2)
    def _(i):
        step = first + 2 * i
        prepare(pair_blocks(table_ref, step + 1), 1)
        work(0, store(step))
        prepare(pair_blocks(table_ref, jnp.minimum(step + 2, last - 1)), 0)
        work(1, store(step + 1))


def sample_part_kernel(extent, first, last, place_ref, table_ref, unit_ref, *refs):
    out_ref, scratch = refs[-5], refs[-4:]
    verts = table_ref.shape[3]
    prepare, _, _, work = sample_tools(place_ref, unit_ref, extent, verts, *scratch)

    def put(owner, line, values):
        for c in range(3):
            out_ref[owner - 2 * first, c, line : line + 1, :] = values[c]

    sample_steps(table_ref, first, last, prepare, work, put)


def sample_part(place, table, unit, order, first, last, extent):
    owners, _, _, verts = table.shape
    size_x, size_y, size_z = extent
    return pl.pallas_call(
        functools.partial(sample_part_kernel, extent, first, last),
        out_shape=jax.ShapeDtypeStruct((2 * (last - first), 3, 2, verts), F32),
        in_specs=[smem(), vmem(), vmem()] + [pl.BlockSpec(memory_space=pl.ANY)] * len(order),
        out_specs=vmem(),
        scratch_shapes=sample_scratch(extent, verts),
        compiler_params=settings(12),
        cost_estimate=cost(
            32 * (last - first) * 3 * size_x * size_y * size_z * verts, MIB
        ),
        name="sample_part",
    )(place, table, unit, *order)


def sample_kernel(
    extent, place_ref, spot_ref, table_ref, packed, unit_ref, part_ref, *refs
):
    out_ref, found, scratch = refs[-6], refs[-5], refs[-4:]
    owners, _, _, verts = table_ref.shape
    prepare, product, select, work = sample_tools(place_ref, unit_ref, extent, verts, *scratch)
    done = part_ref.shape[0]
    for c in range(3):
        out_ref[0:done, c, 0:2] = part_ref[:, c]
        out_ref[:, c, 2:4] = jnp.zeros((owners, 2, verts), F32)

    def put(owner, line, values):
        for c in range(3):
            out_ref[owner, c, line : line + 1, :] = values[c]

    sample_steps(table_ref, done // 2, owners // 2, prepare, work, put)

    @pl.loop(0, packed_blocks(spot_ref[2 * owners], verts))
    def _(block):
        prepare([packed_rows(packed, block)], 0)
        product(0, 0)
        values = select(0, 0)
        for c in range(3):
            found[block, c : c + 1, :] = values[c]

    lane = lax.broadcasted_iota(jnp.int32, (4, verts), 1)
    for owner in range(owners):
        for j in range(2):
            spot = spot_ref[2 * owner + j]

            @pl.when(spot_ref[2 * owner + j + 1] > spot)
            def _(owner=owner, j=j, spot=spot):
                block = lax.shift_right_logical(spot, 7)
                shift = spot & (verts - 1)
                back = (verts - shift) & (verts - 1)
                first = pltpu.roll(found[block, 0:4], back, 1)
                second = pltpu.roll(found[block + 1, 0:4], back, 1)
                value = jnp.where(lane < verts - shift, first, second)
                for c in range(3):
                    out_ref[owner, c, 2 + j : 3 + j, :] = value[c : c + 1]


def sample(place, spots, table, packed, unit, part, order, extent):
    owners, _, _, verts = table.shape
    size_x, size_y, size_z = extent
    return pl.pallas_call(
        functools.partial(sample_kernel, extent),
        out_shape=jax.ShapeDtypeStruct((owners, 3, SLOT_CAP, verts), F32),
        in_specs=[smem(), smem()]
        + [vmem()] * 4
        + [pl.BlockSpec(memory_space=pl.ANY)] * len(order),
        out_specs=vmem(),
        scratch_shapes=[pltpu.VMEM((2 * owners + 2, 8, verts), F32)]
        + sample_scratch(extent, verts),
        compiler_params=settings(12),
        cost_estimate=cost(8 * owners * 3 * size_x * size_y * size_z * verts, MIB),
        name="sample_velocity",
    )(place, spots, table, packed, unit, part, *order)


def y_message_kernel(xr_ref, yfp_ref, yfm_ref, plus_ref, minus_ref):
    size_y = xr_ref.shape[1]
    for sign, face, out in ((1, yfp_ref, plus_ref), (-1, yfm_ref, minus_ref)):
        out[0:5] = face[...]
        line = size_y - 1 if sign > 0 else 0
        for e, q in enumerate(Y_EDGES[sign]):
            out[5, e : e + 1, :] = x_plane(xr_ref, q)[line : line + 1, :]


def y_messages(x_halo, y_plus, y_minus):
    shape = jax.ShapeDtypeStruct((6,) + y_plus.shape[1:], F32)
    return pl.pallas_call(
        y_message_kernel,
        out_shape=(shape, shape),
        in_specs=[vmem()] * 3,
        out_specs=(vmem(), vmem()),
        compiler_params=settings(4),
        name="y_messages",
    )(x_halo, y_plus, y_minus)


def z_message_kernel(xr_ref, yrp_ref, yrm_ref, zfp_ref, zfm_ref, plus_ref, minus_ref):
    size_y, size_z = zfp_ref.shape
    y_halo = {1: yrp_ref, -1: yrm_ref}
    lane = lax.broadcasted_iota(jnp.int32, (size_y, size_z), 1)
    for sign, face, out in ((1, zfp_ref, plus_ref), (-1, zfm_ref, minus_ref)):
        column = size_z - 1 if sign > 0 else 0
        block = face[...]
        for e, q in enumerate(Z_EDGES[sign]):
            if VELOCITIES[q][0] != 0:
                plane = x_plane(xr_ref, q)
            else:
                y_sign = VELOCITIES[q][1]
                plane = y_halo[y_sign][Y_LISTS[y_sign].index(q)]
            spot = EDGE_LANE + e
            block = jnp.where(lane == spot, pltpu.roll(plane, (spot - column) % size_z, 1), block)
        out[...] = block


def z_messages(x_halo, y_plus, y_minus, z_plus, z_minus):
    shape = jax.ShapeDtypeStruct(z_plus.shape, F32)
    return pl.pallas_call(
        z_message_kernel,
        out_shape=(shape, shape),
        in_specs=[vmem()] * 5,
        out_specs=(vmem(), vmem()),
        compiler_params=settings(4),
        name="z_messages",
    )(x_halo, y_plus, y_minus, z_plus, z_minus)


def stream_kernel(
    post,
    xr_ref,
    yrp_ref,
    yrm_ref,
    zrp_ref,
    zrm_ref,
    read_hbm,
    read,
    out_sem,
):
    _, size_x, size_y, size_z = post.shape
    y_halo = {1: yrp_ref, -1: yrm_ref}
    z_halo = {1: zrp_ref, -1: zrm_ref}
    stores = [pltpu.make_async_copy(read.at[q], read_hbm.at[q], out_sem.at[q]) for q in range(19)]
    lane = lax.broadcasted_iota(jnp.int32, (size_y, size_z), 1)
    row = lax.broadcasted_iota(jnp.int32, (size_y, size_z), 0)

    def shift_z(plane, cz, place):
        moved = pltpu.roll(plane, cz % size_z, 1)
        target = 0 if cz > 0 else size_z - 1
        column = pltpu.roll(z_halo[cz][...], (target - place) % size_z, 1)
        return jnp.where(lane == target, column, moved)

    for q in range(19):
        cx, cy, cz = VELOCITIES[q]
        rows = None
        if cy != 0:
            rows = y_halo[cy][Y_LISTS[cy].index(q)]
            if cz != 0:
                rows = shift_z(rows, cz, EDGE_LANE + Z_EDGES[cz].index(q))
        for x in range(size_x):
            source = x - cx
            outside = source < 0 or source >= size_x
            plane = x_plane(xr_ref, q) if outside else post[q, source]
            if cz != 0:
                if outside:
                    place = EDGE_LANE + Z_EDGES[cz].index(q)
                else:
                    place = Z_LISTS[cz].index(q) * 16 + source
                plane = shift_z(plane, cz, place)
            if cy != 0:
                moved = pltpu.roll(plane, cy % size_y, 0)
                target = 0 if cy > 0 else size_y - 1
                if outside:
                    e = Y_EDGES[cy].index(q)
                    line = y_halo[cy][5, e : e + 1, :]
                else:
                    line = rows[source : source + 1, :]
                plane = jnp.where(row == target, jnp.broadcast_to(line, moved.shape), moved)
            read[q, x] = plane
        stores[q].start()
    for store in stores:
        store.wait()


def stream(post, x_halo, y_plus, y_minus, z_plus, z_minus):
    anyspace = pl.BlockSpec(memory_space=pl.ANY)
    return pl.pallas_call(
        stream_kernel,
        out_shape=jax.ShapeDtypeStruct(post.shape, F32),
        in_specs=[vmem()] * 6,
        out_specs=anyspace,
        scratch_shapes=[
            pltpu.VMEM(post.shape, F32),
            pltpu.SemaphoreType.DMA((19,)),
        ],
        compiler_params=settings(10),
        cost_estimate=cost(MIB, 16 * MIB),
        name="stream_populations",
    )(post, x_halo, y_plus, y_minus, z_plus, z_minus)


def collect_kernel(inter_ref, base_ref, rank_ref, back_ref, out_ref):
    patches, verts = rank_ref.shape[1:]
    line = lax.broadcasted_iota(jnp.int32, (16, verts), 0) & (SLOT_CAP - 1)
    for p in range(patches):
        value = None
        for i in range(2):
            brick = inter_ref[i, p]
            base = base_ref[2 * p + i]
            rank = jnp.broadcast_to(rank_ref[i, p : p + 1, :], (8, verts))
            spot = jnp.concatenate([rank + base] * 2, axis=0)
            rows = [back_ref[brick, c] for c in range(3)] + [jnp.zeros((4, verts), F32)]
            picked = jnp.concatenate(rows, axis=0)
            picked = jnp.take_along_axis(picked, spot & (verts - 1), axis=1)
            here = lax.shift_right_logical(spot, 7) == line
            picked = jnp.where(here & (jnp.concatenate([rank] * 2, axis=0) >= 0), picked, 0.0)
            value = picked if value is None else value + picked
        value = value + pltpu.roll(value, 15, 0)
        value = value + pltpu.roll(value, 14, 0)
        value = jnp.concatenate([value[4 * c : 4 * c + 1] for c in range(3)], axis=0)
        out_ref[:, p, :] = value


def collect(intersection, bases, ranks, back):
    _, patches, verts = ranks.shape
    return pl.pallas_call(
        collect_kernel,
        out_shape=jax.ShapeDtypeStruct((3, patches, verts), F32),
        in_specs=[smem()] * 2 + [vmem()] * 2,
        out_specs=vmem(),
        compiler_params=settings(4),
        name="collect_velocity",
    )(intersection, bases, ranks, back)


def shifted(value, axis, step):
    count = lax.axis_size(axis)
    return lax.ppermute(value, axis, [(i, (i + step) % count) for i in range(count)])


def exchanged(value):
    return lax.all_to_all(value, ("gy", "gz"), split_axis=0, concat_axis=0, tiled=True)


def body(populations, solid_flags, positions, anchors, base_cell, weights, intersection):
    extent = populations.shape[1:]
    axes = ("gx", "gy", "gz")
    bricks = lax.axis_size("gy") * lax.axis_size("gz")
    here = [lax.axis_index(axis) for axis in axes]
    place = jnp.stack(
        [here[d] * extent[d] for d in range(3)]
        + here
        + [jnp.int32(lax.axis_size(axis)) for axis in axes]
    ).astype(jnp.int32)
    lists = intersection.T
    outgoing, ranks, bases = build_lists(
        lists,
        jnp.transpose(positions, (1, 0, 2)),
        jnp.transpose(anchors, (1, 0, 2)),
        jnp.transpose(base_cell, (1, 0, 2)),
        weights,
        bricks,
        lax.axis_size("gz"),
        extent,
    )
    table = exchanged(outgoing)
    total, packed, spots, populations = spread(place, table, populations)
    x_face, field = x_faces(total, populations, solid_flags)
    post, y_plus, y_minus, z_plus, z_minus, unit = collide(field, populations, solid_flags)
    if lax.axis_size("gx") == 2:
        x_halo = shifted(x_face, "gx", 1)
    else:
        x_halo = jnp.concatenate(
            [shifted(x_face[:5], "gx", 1), shifted(x_face[5:], "gx", -1)], axis=0
        )
    y_plus, y_minus = y_messages(x_halo, y_plus, y_minus)
    y_plus = shifted(y_plus, "gy", 1)
    y_minus = shifted(y_minus, "gy", -1)
    steps = table.shape[0] // 2
    part = sample_part(place, table, unit, (x_halo,), 0, steps // 4 * 3, extent)
    order = (y_plus, y_minus)
    sampled = sample(place, spots, table, packed, unit, part, order, extent)
    back = exchanged(sampled)
    z_plus, z_minus = z_messages(x_halo, y_plus, y_minus, z_plus, z_minus)
    z_plus = shifted(z_plus, "gz", 1)
    z_minus = shifted(z_minus, "gz", -1)
    read = stream(post, x_halo, y_plus, y_minus, z_plus, z_minus)
    velocity = collect(lists, bases, ranks, back)
    return read, jnp.transpose(velocity, (1, 0, 2))


def solution(mesh):
    return jax.shard_map(
        body,
        mesh=mesh,
        in_specs=(
            P(None, "gx", "gy", "gz"),
            P("gx", "gy", "gz"),
            P(("gx", "gy", "gz"), None, None),
            P(("gx", "gy", "gz"), None, None),
            P(("gx", "gy", "gz"), None, None),
            P(("gx", "gy", "gz"), None, None),
            P(("gx", "gy", "gz"), None),
        ),
        out_specs=(P(None, "gx", "gy", "gz"), P(("gx", "gy", "gz"), None, None)),
        check_vma=False,
    )
```

```python
import functools

import jax
import jax.numpy as jnp
from jax import lax
from jax.experimental import pallas as pl
from jax.experimental.pallas import tpu as pltpu
from jax.sharding import PartitionSpec as P

SLOT_CAP = 4
GROUPS = 7
EDGE_LANE = 80

RELAXATION = 0.8
TENSION = 0.05
TETHER = 0.5
VELOCITIES = [
    (0, 0, 0),
    (1, 0, 0),
    (-1, 0, 0),
    (0, 1, 0),
    (0, -1, 0),
    (0, 0, 1),
    (0, 0, -1),
    (1, 1, 0),
    (-1, -1, 0),
    (1, -1, 0),
    (-1, 1, 0),
    (1, 0, 1),
    (-1, 0, -1),
    (1, 0, -1),
    (-1, 0, 1),
    (0, 1, 1),
    (0, -1, -1),
    (0, 1, -1),
    (0, -1, 1),
]
LATTICE_WEIGHTS = [1.0 / 3.0] + [1.0 / 18.0] * 6 + [1.0 / 36.0] * 12


def crossing(axis, sign):
    return [q for q in range(19) if VELOCITIES[q][axis] == sign]


X_LISTS = {1: crossing(0, 1), -1: crossing(0, -1)}
Y_LISTS = {1: crossing(1, 1), -1: crossing(1, -1)}
Z_LISTS = {1: crossing(2, 1), -1: crossing(2, -1)}
Y_EDGES = {s: [q for q in Y_LISTS[s] if VELOCITIES[q][0] != 0] for s in (1, -1)}
Z_EDGES = {
    s: [q for q in Z_LISTS[s] if VELOCITIES[q][0] != 0 or VELOCITIES[q][1] != 0] for s in (1, -1)
}

BF = jnp.bfloat16
F32 = jnp.float32
MIB = 1024 * 1024
NT = (((1,), (1,)), ((), ()))
NN = (((1,), (0,)), ((), ()))


def settings(mib):
    return pltpu.CompilerParams(vmem_limit_bytes=int(mib * MIB))


def cost(flops, size):
    return pl.CostEstimate(flops=flops, bytes_accessed=size, transcendentals=0)


def vmem():
    return pl.BlockSpec(memory_space=pltpu.VMEM)


def smem():
    return pl.BlockSpec(memory_space=pltpu.SMEM)


def list_kernel(
    bricks_z,
    inter_ref,
    pos_ref,
    anchor_ref,
    cell_ref,
    weight_ref,
    out_ref,
    rank_ref,
    base_ref,
    payload,
    lists,
    count_ref,
    extent,
):
    patches, verts = pos_ref.shape[1:]
    bricks = out_ref.shape[0]
    pos = pos_ref[...]
    cycle_term = pltpu.roll(pos, 1, 2) + pltpu.roll(pos, verts - 1, 2) - 2.0 * pos
    forces = TENSION * cycle_term + TETHER * (anchor_ref[...] - pos)
    cells = cell_ref[...].astype(F32)
    payload[:, 0:8, :] = weight_ref[...]
    for p in range(patches):
        payload[p, 8:11, :] = forces[:, p, :]
        payload[p, 11:14, :] = cells[:, p, :] + 1.0
        payload[p, 14:16, :] = jnp.zeros((2, verts), F32)
    lists[...] = jnp.zeros(lists.shape, F32)

    @pl.loop(0, bricks)
    def _(b):
        count_ref[b] = 0

    lane = lax.broadcasted_iota(jnp.int32, (patches, verts), 1)
    row = lax.broadcasted_iota(jnp.int32, (patches, verts), 0)
    upper = (
        lax.broadcasted_iota(jnp.int32, (verts, verts), 0)
        <= lax.broadcasted_iota(jnp.int32, (verts, verts), 1)
    ).astype(F32)
    codes, sums = [], []
    for i in range(2):
        first_y = jnp.zeros((patches, verts), F32)
        first_z = jnp.zeros((patches, verts), F32)
        for p in range(patches):
            brick = inter_ref[i, p]
            first_y = jnp.where(row == p, (brick // bricks_z * extent[1]).astype(F32), first_y)
            first_z = jnp.where(row == p, (brick % bricks_z * extent[2]).astype(F32), first_z)
        live = (
            (cells[1] >= first_y)
            & (cells[1] < first_y + extent[1])
            & (cells[2] >= first_z)
            & (cells[2] < first_z + extent[2])
        )
        mask = live.astype(F32)
        total = jnp.dot(mask.astype(BF), upper.astype(BF), preferred_element_type=F32)
        rank = (total - mask).astype(jnp.int32)
        rank_ref[i] = jnp.where(live, rank, -1)
        code = jnp.where(live, (lane - rank) + lane * 256 + 65536, 0)
        step = 1
        while step < verts:
            moving = jnp.where((code & step) != 0, code, 0)
            code = (code - moving) + pltpu.roll(moving, verts - step, 1)
            step *= 2
        codes.append(code)
        sums.append(total)
    wide_lane = lax.broadcasted_iota(jnp.int32, (16, verts), 1)
    for p in range(patches):
        for i in range(2):
            brick = inter_ref[i, p]
            base = count_ref[brick]
            base_ref[2 * p + i] = base
            count_ref[brick] = base + jnp.max(sums[i][p : p + 1, :]).astype(jnp.int32)
            block = lax.shift_right_logical(base, 7)
            shift = base & (verts - 1)
            code = jnp.broadcast_to(codes[i][p : p + 1, :], (8, verts))
            code = pltpu.roll(code, shift, 1)
            code = jnp.concatenate([code, code], axis=0)
            source = lax.shift_right_logical(code, 8) & (verts - 1)
            moved = jnp.take_along_axis(payload[p], source, axis=1)
            moved = jnp.where(code >= 65536, moved, 0.0)
            lists[brick, block] += jnp.where(wide_lane >= shift, moved, 0.0)
            lists[brick, block + 1] += jnp.where(wide_lane < shift, moved, 0.0)

    @pl.loop(0, bricks)
    def _(b):
        for j in range(SLOT_CAP):
            value = lists[b, j]
            first = j // 2 * GROUPS
            for g in range(3):
                out_ref[b, first + j % 2 * 3 + g] = value[4 * g : 4 * g + 4]
            out_ref[b, first + 6, j % 2 * 2 : j % 2 * 2 + 2] = value[12:14]


def build_lists(intersection, positions, anchors, base_cell, weights, bricks, bricks_z, extent):
    _, patches, verts = positions.shape

    def kernel(*refs):
        list_kernel(bricks_z, *refs, extent)

    return pl.pallas_call(
        kernel,
        out_shape=(
            jax.ShapeDtypeStruct((bricks, 2 * GROUPS, 4, verts), F32),
            jax.ShapeDtypeStruct((2, patches, verts), jnp.int32),
            jax.ShapeDtypeStruct((2 * patches,), jnp.int32),
        ),
        in_specs=[smem(), vmem(), vmem(), vmem(), vmem()],
        out_specs=(vmem(), vmem(), smem()),
        scratch_shapes=[
            pltpu.VMEM((patches, 16, verts), F32),
            pltpu.VMEM((bricks, SLOT_CAP + 1, 16, verts), F32),
            pltpu.SMEM((bricks,), jnp.int32),
        ],
        compiler_params=settings(56),
        name="vertex_lists",
    )(intersection, positions, anchors, base_cell, weights)


def block_rows(table_ref, owner, j):
    first = j // 2 * GROUPS
    group = first + j % 2 * 3
    weight = jnp.concatenate([table_ref[owner, group], table_ref[owner, group + 1]], axis=0)
    third = table_ref[owner, group + 2]
    line = j % 2 * 2
    last = table_ref[owner, first + 6, line : line + 2]
    return weight, third[0:3], jnp.concatenate([third[3:4], last], axis=0)


def pack_far(table_ref, packed, spot_ref, owner, spot):
    verts = table_ref.shape[3]
    lane = lax.broadcasted_iota(jnp.int32, (16, verts), 1)
    for j in range(2):
        weight, force, cells = block_rows(table_ref, owner, 2 + j)
        held = (cells[0:1] > 0.0).astype(F32)
        rows = jnp.concatenate([weight, force, cells, jnp.zeros((2, verts), F32)], axis=0)
        spot_ref[2 * owner + j] = spot
        block = lax.shift_right_logical(spot, 7)
        shift = spot & (verts - 1)
        rows = pltpu.roll(rows, shift, 1)
        packed[block] += jnp.where(lane >= shift, rows, 0.0)
        packed[block + 1] += jnp.where(lane < shift, rows, 0.0)
        spot = spot + jnp.sum(held).astype(jnp.int32)
    return spot


def packed_blocks(spot, verts):
    return lax.shift_right_logical(spot + verts - 1, 7)


def packed_rows(packed, block):
    return packed[block, 0:8], packed[block, 8:11], packed[block, 11:14]


def place_rows(place_ref, rows, extent):
    weight, force, cells = rows
    local, inside = [], None
    for d in range(3):
        value = cells[d : d + 1] - (place_ref[d] + 1).astype(F32)
        ok = (value >= 0.0) & (value < float(extent[d]))
        inside = ok if inside is None else inside & ok
        local.append(value)
    weight = weight * jnp.broadcast_to(inside.astype(F32), weight.shape)
    return weight, force, local


def halves(value):
    high = value.astype(BF).astype(F32)
    return high, value - high


def spread_scratch(extent, verts):
    size_x, size_y, size_z = extent
    depth = SLOT_CAP * 2 * verts
    return [
        pltpu.VMEM((2, 2, size_x * size_y, depth), BF),
        pltpu.VMEM((2, 6 * size_z, depth), BF),
        pltpu.VMEM((2, SLOT_CAP, 16, verts), F32),
        pltpu.VMEM((2, SLOT_CAP, 8, verts), F32),
        pltpu.VMEM((2, SLOT_CAP, 8, verts), F32),
    ]


def spread_tools(place_ref, extent, verts, total, a_buf, zf_buf, w_rows, f_rows, c_rows):
    size_x, size_y, size_z = extent
    iota_y = lax.broadcasted_iota(jnp.int32, (16, verts), 0).astype(F32).astype(BF)
    zero = jnp.zeros((16, verts), BF)

    def wide(ref, slot, j, row):
        return jnp.broadcast_to(ref[slot, j, row : row + 1, :], (16, verts)).astype(BF)

    def build(blocks, slot):
        for j, rows in enumerate(blocks):
            weight, force, local = place_rows(place_ref, rows, extent)
            w_hi, w_lo = halves(weight)
            f_hi, f_lo = halves(force)
            w_rows[slot, j, 0:8] = w_hi
            w_rows[slot, j, 8:16] = w_lo
            f_rows[slot, j, 0:3] = f_hi
            f_rows[slot, j, 4:7] = f_lo
            for d in range(3):
                c_rows[slot, j, d : d + 1] = local[d]
        for j in range(len(blocks)):
            xl = wide(c_rows, slot, j, 0)
            yl = wide(c_rows, slot, j, 1)
            zl = wide(c_rows, slot, j, 2)
            at_y0 = iota_y == yl
            at_y1 = iota_y == yl + 1.0
            lines = {}
            for part in range(2):
                for dx in range(2):
                    for dz in range(2):
                        first = part * 8 + dx * 4 + dz
                        lines[part, dx, dz] = jnp.where(
                            at_y0,
                            wide(w_rows, slot, j, first),
                            jnp.where(at_y1, wide(w_rows, slot, j, first + 2), zero),
                        )
            before = None
            for x in range(size_x):
                here = xl == float(x)
                for part in range(2):
                    for dz in range(2):
                        value = jnp.where(here, lines[part, 0, dz], zero)
                        if before is not None:
                            value = jnp.where(before, lines[part, 1, dz], value)
                        column = (j * 2 + dz) * verts
                        a_buf[slot, part, x * 16 : (x + 1) * 16, column : column + verts] = value
                before = here
            force = [wide(f_rows, slot, j, part * 4 + c) for part in range(2) for c in range(3)]
            for zb in range(size_z // 16):
                for dz in range(2):
                    at_z = iota_y == zl + float(dz - 16 * zb)
                    column = (j * 2 + dz) * verts
                    for part in range(2):
                        for c in range(3):
                            line = (part * 3 + c) * size_z + zb * 16
                            zf_buf[slot, line : line + 16, column : column + verts] = jnp.where(
                                at_z, force[part * 3 + c], zero
                            )

    def product(slot, blocks=SLOT_CAP):
        lines = 3 * size_z
        depth = blocks * 2 * verts
        high = lax.dot_general(
            zf_buf[slot, :, :depth], a_buf[slot, 0, :, :depth], NT, preferred_element_type=F32
        )
        low = lax.dot_general(
            zf_buf[slot, :lines, :depth],
            a_buf[slot, 1, :, :depth],
            NT,
            preferred_element_type=F32,
        )
        total[...] += high[:lines] + high[lines:] + low

    return build, product


def pair_blocks(table_ref, step):
    return [block_rows(table_ref, 2 * step + oo, j) for oo in range(2) for j in range(2)]


def spread_kernel(
    extent,
    place_ref,
    table_ref,
    pop_any,
    total,
    packed,
    spot_ref,
    pop,
    sem,
    *scratch,
):
    load = pltpu.make_async_copy(pop_any, pop, sem)
    load.start()
    owners, _, _, verts = table_ref.shape
    build, product = spread_tools(place_ref, extent, verts, total, *scratch)
    steps = owners // 2
    total[...] = jnp.zeros(total.shape, F32)
    packed[...] = jnp.zeros(packed.shape, F32)
    build(pair_blocks(table_ref, 0), 0)

    def near(i, spot):
        build(pair_blocks(table_ref, 2 * i + 1), 1)
        product(0)
        for owner in range(2):
            spot = pack_far(table_ref, packed, spot_ref, 4 * i + owner, spot)
        build(pair_blocks(table_ref, jnp.minimum(2 * i + 2, steps - 1)), 0)
        product(1)
        for owner in range(2, 4):
            spot = pack_far(table_ref, packed, spot_ref, 4 * i + owner, spot)
        return spot

    spot_ref[2 * owners] = lax.fori_loop(0, steps // 2, near, jnp.int32(0))

    @pl.loop(0, packed_blocks(spot_ref[2 * owners], verts))
    def _(block):
        build([packed_rows(packed, block)], 0)
        product(0, 1)

    load.wait()


def spread(place, table, populations):
    owners, _, _, verts = table.shape
    extent = populations.shape[1:]
    size_x, size_y, size_z = extent
    anyspace = pl.BlockSpec(memory_space=pl.ANY)
    cross = size_x * size_y
    return pl.pallas_call(
        functools.partial(spread_kernel, extent),
        out_shape=(
            jax.ShapeDtypeStruct((3 * size_z, cross), F32),
            jax.ShapeDtypeStruct((2 * owners + 2, 16, verts), F32),
            jax.ShapeDtypeStruct((2 * owners + 1,), jnp.int32),
            jax.ShapeDtypeStruct(populations.shape, F32),
        ),
        in_specs=[smem(), vmem(), anyspace],
        out_specs=(vmem(), vmem(), smem(), vmem()),
        scratch_shapes=[pltpu.SemaphoreType.DMA] + spread_scratch(extent, verts),
        compiler_params=settings(49.5),
        cost_estimate=cost(18 * owners * 3 * size_z * cross * 4 * verts, MIB),
        name="spread",
    )(place, table, populations)


def along(vector, q):
    value = None
    for c in range(3):
        move = VELOCITIES[q][c]
        if move == 0:
            continue
        if value is None:
            value = vector[c] if move > 0 else -vector[c]
        else:
            value = value + vector[c] if move > 0 else value - vector[c]
    return value


def collide_plane(x, force, pop, solid):
    factor = 1.0 - 0.5 / RELAXATION
    rate = 1.0 / RELAXATION
    keep = 1.0 - rate
    cells = [pop[q, x] for q in range(19)]
    wall = solid[x] == 1
    rho = cells[0]
    for q in range(1, 19):
        rho = rho + cells[q]
    moment = []
    for c in range(3):
        value = None
        for q in range(1, 19, 2):
            if VELOCITIES[q][c] != 0:
                term = cells[q] - cells[q + 1]
                if VELOCITIES[q][c] < 0:
                    term = -term
                value = term if value is None else value + term
        moment.append(value)
    inverse = 1.0 / rho
    vel = [(moment[c] + 0.5 * force[c]) * inverse for c in range(3)]
    speed = vel[0] * vel[0] + vel[1] * vel[1] + vel[2] * vel[2]
    u_dot_f = vel[0] * force[0] + vel[1] * force[1] + vel[2] * force[2]
    three = 3.0 * factor
    nine = 9.0 * factor
    rest = (rate * rho) * (1.0 - 1.5 * speed) - three * u_dot_f
    quad = (4.5 * rate) * rho
    linear = (3.0 * rate) * rho
    results = [None] * 19
    results[0] = jnp.where(wall, cells[0], keep * cells[0] + LATTICE_WEIGHTS[0] * rest)

    for q in range(1, 19, 2):
        a = along(vel, q)
        b = along(force, q)
        weight = LATTICE_WEIGHTS[q]
        even = weight * (rest + a * (quad * a + nine * b))
        odd = weight * (linear * a + three * b)
        results[q] = jnp.where(wall, cells[q + 1], keep * cells[q] + (even + odd))
        results[q + 1] = jnp.where(wall, cells[q], keep * cells[q + 1] + (even - odd))
    return results, vel


def face_kernel(total, pop, solid, xface_ref, field):
    size_x, size_y, size_z = solid.shape
    for c in range(3):
        for half in range(size_x * size_y // 128):
            field[c, half * 128 : (half + 1) * 128, :] = jnp.transpose(
                total[c * size_z : (c + 1) * size_z, half * 128 : (half + 1) * 128]
            )
    for x, first, sign in ((size_x - 1, 0, 1), (0, 5, -1)):
        force = [field[c, x * size_y : (x + 1) * size_y, :] for c in range(3)]
        results, _ = collide_plane(x, force, pop, solid)
        for k, q in enumerate(X_LISTS[sign]):
            xface_ref[first + k] = results[q]


def x_faces(total, populations, solid):
    _, size_x, size_y, size_z = populations.shape
    return pl.pallas_call(
        face_kernel,
        out_shape=(
            jax.ShapeDtypeStruct((10, size_y, size_z), F32),
            jax.ShapeDtypeStruct((3, size_x * size_y, size_z), F32),
        ),
        in_specs=[vmem()] * 3,
        out_specs=(vmem(),) * 2,
        compiler_params=settings(12),
        cost_estimate=cost(2 * MIB, MIB),
        name="x_faces",
    )(total, populations, solid)


def collide_kernel(field, pop, solid, post, yfp_ref, yfm_ref, zfp_ref, zfm_ref, unit_ref):
    _, size_x, size_y, size_z = post.shape
    lane = lax.broadcasted_iota(jnp.int32, (size_y, size_z), 1)

    def plane(x, z_out):
        z_out = dict(zip((1, -1), z_out))
        lines = pl.ds(pl.multiple_of(x * 16, 16), 16)
        force = [field[c, lines, :] for c in range(3)]
        results, vel = collide_plane(x, force, pop, solid)
        for c in range(3):
            high, low = halves(vel[c])
            first = pl.ds(pl.multiple_of((x * 3 + c) * 16, 16), 16)
            unit_ref[first, 0:size_z] = high.astype(BF)
            unit_ref[first, size_z : 2 * size_z] = low.astype(BF)
        for q in range(19):
            post[q, x] = results[q]
        for sign, line, face in ((1, size_y - 1, yfp_ref), (-1, 0, yfm_ref)):
            for k, q in enumerate(Y_LISTS[sign]):
                face[k, pl.ds(x, 1), :] = results[q][line : line + 1, :]
        for sign, column in ((1, size_z - 1), (-1, 0)):
            for k, q in enumerate(Z_LISTS[sign]):
                place = k * 16 + x
                moved = pltpu.roll(results[q], (place - column + size_z) & (size_z - 1), 1)
                z_out[sign] = jnp.where(lane == place, moved, z_out[sign])
        return z_out[1], z_out[-1]

    empty = jnp.zeros((size_y, size_z), F32)
    zfp_ref[...], zfm_ref[...] = lax.fori_loop(0, size_x, plane, (empty, empty), unroll=2)


def collide(field, populations, solid):
    _, size_x, size_y, size_z = populations.shape
    face_y = jax.ShapeDtypeStruct((5, size_x, size_z), F32)
    face_z = jax.ShapeDtypeStruct((size_y, size_z), F32)
    return pl.pallas_call(
        collide_kernel,
        out_shape=(
            jax.ShapeDtypeStruct(populations.shape, F32),
            face_y,
            face_y,
            face_z,
            face_z,
            jax.ShapeDtypeStruct((size_x * size_y * 3, 2 * size_z), BF),
        ),
        in_specs=[vmem()] * 3,
        out_specs=(vmem(),) * 6,
        compiler_params=settings(12),
        cost_estimate=cost(16 * MIB, 8 * MIB),
        name="collide",
    )(field, populations, solid)


def sample_scratch(extent, verts):
    size_x, size_y, size_z = extent
    return [
        pltpu.VMEM((2, SLOT_CAP, 2 * size_z, 2 * verts), BF),
        pltpu.VMEM((2, 3 * size_x * size_y, 2 * verts), F32),
        pltpu.VMEM((2, SLOT_CAP, 8, verts), F32),
        pltpu.VMEM((2, SLOT_CAP, 8, verts), F32),
    ]


def sample_tools(place_ref, unit_ref, extent, verts, hot, grid_buf, w_rows, c_rows):
    size_x, size_y, size_z = extent
    iota_y = lax.broadcasted_iota(jnp.int32, (16, verts), 0).astype(F32)
    iota_b = iota_y.astype(BF)
    one = jnp.ones((16, verts), BF)
    zero_b = jnp.zeros((16, verts), BF)
    zero = jnp.zeros((16, verts), F32)

    def wide(ref, slot, j, row):
        return jnp.broadcast_to(ref[slot, j, row : row + 1, :], (16, verts))

    def prepare(blocks, slot):
        for j, rows in enumerate(blocks):
            weight, _, local = place_rows(place_ref, rows, extent)
            w_rows[slot, j] = weight
            for d in range(3):
                c_rows[slot, j, d : d + 1] = local[d]
        for j in range(len(blocks)):
            zl = wide(c_rows, slot, j, 2).astype(BF)
            for zb in range(size_z // 16):
                for dz in range(2):
                    value = jnp.where(iota_b == zl + float(dz - 16 * zb), one, zero_b)
                    for part in range(2):
                        line = part * size_z + zb * 16
                        hot[slot, j, line : line + 16, dz * verts : (dz + 1) * verts] = value

    def product(slot, j):
        grid_buf[j % 2] = lax.dot_general(unit_ref[...], hot[slot, j], NN, preferred_element_type=F32)

    def select(slot, j):
        xl = wide(c_rows, slot, j, 0)
        yl = wide(c_rows, slot, j, 1)
        at_y0 = iota_y == yl
        at_y1 = iota_y == yl + 1.0
        lines = {}
        for dx in range(2):
            for dz in range(2):
                first = dx * 4 + dz
                lines[dx, dz] = jnp.where(
                    at_y0,
                    wide(w_rows, slot, j, first),
                    jnp.where(at_y1, wide(w_rows, slot, j, first + 2), zero),
                )
        sums = [zero, zero, zero]
        before = None
        for x in range(size_x):
            here = xl == float(x)
            for dz in range(2):
                value = jnp.where(here, lines[0, dz], zero)
                if before is not None:
                    value = jnp.where(before, lines[1, dz], value)
                for c in range(3):
                    first = (x * 3 + c) * 16
                    part = grid_buf[j % 2, first : first + 16, dz * verts : (dz + 1) * verts]
                    sums[c] = sums[c] + value * part
            before = here
        return [jnp.sum(value, axis=0, keepdims=True) for value in sums]

    def work(slot, store):
        product(slot, 0)
        for j in range(SLOT_CAP):
            if j + 1 < SLOT_CAP:
                product(slot, j + 1)
            store(j, select(slot, j))

    return prepare, product, select, work


def x_plane(xr_ref, q):
    sign = VELOCITIES[q][0]
    return xr_ref[(0 if sign > 0 else 5) + X_LISTS[sign].index(q)]


def sample_steps(table_ref, first, last, prepare, work, put):
    def store(step):
        return lambda j, values: put(2 * step + j // 2, j % 2, values)

    prepare(pair_blocks(table_ref, first), 0)

    @pl.loop(0, (last - first) // 2)
    def _(i):
        step = first + 2 * i
        prepare(pair_blocks(table_ref, step + 1), 1)
        work(0, store(step))
        prepare(pair_blocks(table_ref, jnp.minimum(step + 2, last - 1)), 0)
        work(1, store(step + 1))


def sample_part_kernel(extent, first, last, place_ref, table_ref, unit_ref, *refs):
    out_ref, scratch = refs[-5], refs[-4:]
    verts = table_ref.shape[3]
    prepare, _, _, work = sample_tools(place_ref, unit_ref, extent, verts, *scratch)

    def put(owner, line, values):
        for c in range(3):
            out_ref[owner - 2 * first, c, line : line + 1, :] = values[c]

    sample_steps(table_ref, first, last, prepare, work, put)


def sample_part(place, table, unit, order, first, last, extent):
    owners, _, _, verts = table.shape
    size_x, size_y, size_z = extent
    return pl.pallas_call(
        functools.partial(sample_part_kernel, extent, first, last),
        out_shape=jax.ShapeDtypeStruct((2 * (last - first), 3, 2, verts), F32),
        in_specs=[smem(), vmem(), vmem()] + [pl.BlockSpec(memory_space=pl.ANY)] * len(order),
        out_specs=vmem(),
        scratch_shapes=sample_scratch(extent, verts),
        compiler_params=settings(12),
        cost_estimate=cost(
            32 * (last - first) * 3 * size_x * size_y * size_z * verts, MIB
        ),
        name="sample_part",
    )(place, table, unit, *order)


def sample_kernel(
    extent, place_ref, spot_ref, table_ref, packed, unit_ref, part_ref, *refs
):
    out_ref, found, scratch = refs[-6], refs[-5], refs[-4:]
    owners, _, _, verts = table_ref.shape
    prepare, product, select, work = sample_tools(place_ref, unit_ref, extent, verts, *scratch)
    done = part_ref.shape[0]
    for c in range(3):
        out_ref[0:done, c, 0:2] = part_ref[:, c]
        out_ref[:, c, 2:4] = jnp.zeros((owners, 2, verts), F32)

    def put(owner, line, values):
        for c in range(3):
            out_ref[owner, c, line : line + 1, :] = values[c]

    sample_steps(table_ref, done // 2, owners // 2, prepare, work, put)

    @pl.loop(0, packed_blocks(spot_ref[2 * owners], verts))
    def _(block):
        prepare([packed_rows(packed, block)], 0)
        product(0, 0)
        values = select(0, 0)
        for c in range(3):
            found[block, c : c + 1, :] = values[c]

    lane = lax.broadcasted_iota(jnp.int32, (4, verts), 1)
    for owner in range(owners):
        for j in range(2):
            spot = spot_ref[2 * owner + j]

            @pl.when(spot_ref[2 * owner + j + 1] > spot)
            def _(owner=owner, j=j, spot=spot):
                block = lax.shift_right_logical(spot, 7)
                shift = spot & (verts - 1)
                back = (verts - shift) & (verts - 1)
                first = pltpu.roll(found[block, 0:4], back, 1)
                second = pltpu.roll(found[block + 1, 0:4], back, 1)
                value = jnp.where(lane < verts - shift, first, second)
                for c in range(3):
                    out_ref[owner, c, 2 + j : 3 + j, :] = value[c : c + 1]


def sample(place, spots, table, packed, unit, part, order, extent):
    owners, _, _, verts = table.shape
    size_x, size_y, size_z = extent
    return pl.pallas_call(
        functools.partial(sample_kernel, extent),
        out_shape=jax.ShapeDtypeStruct((owners, 3, SLOT_CAP, verts), F32),
        in_specs=[smem(), smem()]
        + [vmem()] * 4
        + [pl.BlockSpec(memory_space=pl.ANY)] * len(order),
        out_specs=vmem(),
        scratch_shapes=[pltpu.VMEM((2 * owners + 2, 8, verts), F32)]
        + sample_scratch(extent, verts),
        compiler_params=settings(12),
        cost_estimate=cost(8 * owners * 3 * size_x * size_y * size_z * verts, MIB),
        name="sample_velocity",
    )(place, spots, table, packed, unit, part, *order)


def y_message_kernel(xr_ref, yfp_ref, yfm_ref, plus_ref, minus_ref):
    size_y = xr_ref.shape[1]
    for sign, face, out in ((1, yfp_ref, plus_ref), (-1, yfm_ref, minus_ref)):
        out[0:5] = face[...]
        line = size_y - 1 if sign > 0 else 0
        for e, q in enumerate(Y_EDGES[sign]):
            out[5, e : e + 1, :] = x_plane(xr_ref, q)[line : line + 1, :]


def y_messages(x_halo, y_plus, y_minus):
    shape = jax.ShapeDtypeStruct((6,) + y_plus.shape[1:], F32)
    return pl.pallas_call(
        y_message_kernel,
        out_shape=(shape, shape),
        in_specs=[vmem()] * 3,
        out_specs=(vmem(), vmem()),
        compiler_params=settings(4),
        name="y_messages",
    )(x_halo, y_plus, y_minus)


def z_message_kernel(xr_ref, yrp_ref, yrm_ref, zfp_ref, zfm_ref, plus_ref, minus_ref):
    size_y, size_z = zfp_ref.shape
    y_halo = {1: yrp_ref, -1: yrm_ref}
    lane = lax.broadcasted_iota(jnp.int32, (size_y, size_z), 1)
    for sign, face, out in ((1, zfp_ref, plus_ref), (-1, zfm_ref, minus_ref)):
        column = size_z - 1 if sign > 0 else 0
        block = face[...]
        for e, q in enumerate(Z_EDGES[sign]):
            if VELOCITIES[q][0] != 0:
                plane = x_plane(xr_ref, q)
            else:
                y_sign = VELOCITIES[q][1]
                plane = y_halo[y_sign][Y_LISTS[y_sign].index(q)]
            spot = EDGE_LANE + e
            block = jnp.where(lane == spot, pltpu.roll(plane, (spot - column) % size_z, 1), block)
        out[...] = block


def z_messages(x_halo, y_plus, y_minus, z_plus, z_minus):
    shape = jax.ShapeDtypeStruct(z_plus.shape, F32)
    return pl.pallas_call(
        z_message_kernel,
        out_shape=(shape, shape),
        in_specs=[vmem()] * 5,
        out_specs=(vmem(), vmem()),
        compiler_params=settings(4),
        name="z_messages",
    )(x_halo, y_plus, y_minus, z_plus, z_minus)


def stream_kernel(
    post,
    xr_ref,
    yrp_ref,
    yrm_ref,
    zrp_ref,
    zrm_ref,
    read_hbm,
    read,
    out_sem,
):
    _, size_x, size_y, size_z = post.shape
    y_halo = {1: yrp_ref, -1: yrm_ref}
    z_halo = {1: zrp_ref, -1: zrm_ref}
    stores = [pltpu.make_async_copy(read.at[q], read_hbm.at[q], out_sem.at[q]) for q in range(19)]
    lane = lax.broadcasted_iota(jnp.int32, (size_y, size_z), 1)
    row = lax.broadcasted_iota(jnp.int32, (size_y, size_z), 0)

    def shift_z(plane, cz, place):
        moved = pltpu.roll(plane, cz % size_z, 1)
        target = 0 if cz > 0 else size_z - 1
        column = pltpu.roll(z_halo[cz][...], (target - place) % size_z, 1)
        return jnp.where(lane == target, column, moved)

    for q in range(19):
        cx, cy, cz = VELOCITIES[q]
        rows = None
        if cy != 0:
            rows = y_halo[cy][Y_LISTS[cy].index(q)]
            if cz != 0:
                rows = shift_z(rows, cz, EDGE_LANE + Z_EDGES[cz].index(q))
        for x in range(size_x):
            source = x - cx
            outside = source < 0 or source >= size_x
            plane = x_plane(xr_ref, q) if outside else post[q, source]
            if cz != 0:
                if outside:
                    place = EDGE_LANE + Z_EDGES[cz].index(q)
                else:
                    place = Z_LISTS[cz].index(q) * 16 + source
                plane = shift_z(plane, cz, place)
            if cy != 0:
                moved = pltpu.roll(plane, cy % size_y, 0)
                target = 0 if cy > 0 else size_y - 1
                if outside:
                    e = Y_EDGES[cy].index(q)
                    line = y_halo[cy][5, e : e + 1, :]
                else:
                    line = rows[source : source + 1, :]
                plane = jnp.where(row == target, jnp.broadcast_to(line, moved.shape), moved)
            read[q, x] = plane
        stores[q].start()
    for store in stores:
        store.wait()


def stream(post, x_halo, y_plus, y_minus, z_plus, z_minus):
    anyspace = pl.BlockSpec(memory_space=pl.ANY)
    return pl.pallas_call(
        stream_kernel,
        out_shape=jax.ShapeDtypeStruct(post.shape, F32),
        in_specs=[vmem()] * 6,
        out_specs=anyspace,
        scratch_shapes=[
            pltpu.VMEM(post.shape, F32),
            pltpu.SemaphoreType.DMA((19,)),
        ],
        compiler_params=settings(10),
        cost_estimate=cost(MIB, 16 * MIB),
        name="stream_populations",
    )(post, x_halo, y_plus, y_minus, z_plus, z_minus)


def collect_kernel(inter_ref, base_ref, rank_ref, back_ref, out_ref):
    patches, verts = rank_ref.shape[1:]
    line = lax.broadcasted_iota(jnp.int32, (16, verts), 0) & (SLOT_CAP - 1)
    for p in range(patches):
        value = None
        for i in range(2):
            brick = inter_ref[i, p]
            base = base_ref[2 * p + i]
            rank = jnp.broadcast_to(rank_ref[i, p : p + 1, :], (8, verts))
            spot = jnp.concatenate([rank + base] * 2, axis=0)
            rows = [back_ref[brick, c] for c in range(3)] + [jnp.zeros((4, verts), F32)]
            picked = jnp.concatenate(rows, axis=0)
            picked = jnp.take_along_axis(picked, spot & (verts - 1), axis=1)
            here = lax.shift_right_logical(spot, 7) == line
            picked = jnp.where(here & (jnp.concatenate([rank] * 2, axis=0) >= 0), picked, 0.0)
            value = picked if value is None else value + picked
        value = value + pltpu.roll(value, 15, 0)
        value = value + pltpu.roll(value, 14, 0)
        value = jnp.concatenate([value[4 * c : 4 * c + 1] for c in range(3)], axis=0)
        out_ref[:, p, :] = value


def collect(intersection, bases, ranks, back):
    _, patches, verts = ranks.shape
    return pl.pallas_call(
        collect_kernel,
        out_shape=jax.ShapeDtypeStruct((3, patches, verts), F32),
        in_specs=[smem()] * 2 + [vmem()] * 2,
        out_specs=vmem(),
        compiler_params=settings(4),
        name="collect_velocity",
    )(intersection, bases, ranks, back)


def shifted(value, axis, step):
    count = lax.axis_size(axis)
    return lax.ppermute(value, axis, [(i, (i + step) % count) for i in range(count)])


def exchanged(value):
    return lax.all_to_all(value, ("gy", "gz"), split_axis=0, concat_axis=0, tiled=True)


def body(populations, solid_flags, positions, anchors, base_cell, weights, intersection):
    extent = populations.shape[1:]
    axes = ("gx", "gy", "gz")
    bricks = lax.axis_size("gy") * lax.axis_size("gz")
    here = [lax.axis_index(axis) for axis in axes]
    place = jnp.stack(
        [here[d] * extent[d] for d in range(3)]
        + here
        + [jnp.int32(lax.axis_size(axis)) for axis in axes]
    ).astype(jnp.int32)
    lists = intersection.T
    outgoing, ranks, bases = build_lists(
        lists,
        jnp.transpose(positions, (1, 0, 2)),
        jnp.transpose(anchors, (1, 0, 2)),
        jnp.transpose(base_cell, (1, 0, 2)),
        weights,
        bricks,
        lax.axis_size("gz"),
        extent,
    )
    table = exchanged(outgoing)
    total, packed, spots, populations = spread(place, table, populations)
    x_face, field = x_faces(total, populations, solid_flags)
    post, y_plus, y_minus, z_plus, z_minus, unit = collide(field, populations, solid_flags)
    if lax.axis_size("gx") == 2:
        x_halo = shifted(x_face, "gx", 1)
    else:
        x_halo = jnp.concatenate(
            [shifted(x_face[:5], "gx", 1), shifted(x_face[5:], "gx", -1)], axis=0
        )
    y_plus, y_minus = y_messages(x_halo, y_plus, y_minus)
    y_plus = shifted(y_plus, "gy", 1)
    y_minus = shifted(y_minus, "gy", -1)
    steps = table.shape[0] // 2
    part = sample_part(place, table, unit, (x_halo,), 0, steps // 4 * 3, extent)
    order = (y_plus, y_minus)
    sampled = sample(place, spots, table, packed, unit, part, order, extent)
    back = exchanged(sampled)
    z_plus, z_minus = z_messages(x_halo, y_plus, y_minus, z_plus, z_minus)
    z_plus = shifted(z_plus, "gz", 1)
    z_minus = shifted(z_minus, "gz", -1)
    read = stream(post, x_halo, y_plus, y_minus, z_plus, z_minus)
    velocity = collect(lists, bases, ranks, back)
    return read, jnp.transpose(velocity, (1, 0, 2))


def solution(mesh):
    return jax.shard_map(
        body,
        mesh=mesh,
        in_specs=(
            P(None, "gx", "gy", "gz"),
            P("gx", "gy", "gz"),
            P(("gx", "gy", "gz"), None, None),
            P(("gx", "gy", "gz"), None, None),
            P(("gx", "gy", "gz"), None, None),
            P(("gx", "gy", "gz"), None, None),
            P(("gx", "gy", "gz"), None),
        ),
        out_specs=(P(None, "gx", "gy", "gz"), P(("gx", "gy", "gz"), None, None)),
        check_vma=False,
    )
```

```python
import functools

import jax
import jax.numpy as jnp
from jax import lax
from jax.experimental import pallas as pl
from jax.experimental.pallas import tpu as pltpu
from jax.sharding import PartitionSpec as P

SLOT_CAP = 4
GROUPS = 7
SPREAD_OWNERS = 4
SPREAD_BLOCKS = 2 * SPREAD_OWNERS
EDGE_LANE = 80

RELAXATION = 0.8
TENSION = 0.05
TETHER = 0.5
VELOCITIES = [
    (0, 0, 0),
    (1, 0, 0),
    (-1, 0, 0),
    (0, 1, 0),
    (0, -1, 0),
    (0, 0, 1),
    (0, 0, -1),
    (1, 1, 0),
    (-1, -1, 0),
    (1, -1, 0),
    (-1, 1, 0),
    (1, 0, 1),
    (-1, 0, -1),
    (1, 0, -1),
    (-1, 0, 1),
    (0, 1, 1),
    (0, -1, -1),
    (0, 1, -1),
    (0, -1, 1),
]
LATTICE_WEIGHTS = [1.0 / 3.0] + [1.0 / 18.0] * 6 + [1.0 / 36.0] * 12


def crossing(axis, sign):
    return [q for q in range(19) if VELOCITIES[q][axis] == sign]


X_LISTS = {1: crossing(0, 1), -1: crossing(0, -1)}
Y_LISTS = {1: crossing(1, 1), -1: crossing(1, -1)}
Z_LISTS = {1: crossing(2, 1), -1: crossing(2, -1)}
Y_EDGES = {s: [q for q in Y_LISTS[s] if VELOCITIES[q][0] != 0] for s in (1, -1)}
Z_EDGES = {
    s: [q for q in Z_LISTS[s] if VELOCITIES[q][0] != 0 or VELOCITIES[q][1] != 0] for s in (1, -1)
}

BF = jnp.bfloat16
F32 = jnp.float32
MIB = 1024 * 1024
NT = (((1,), (1,)), ((), ()))
NN = (((1,), (0,)), ((), ()))


def settings(mib):
    return pltpu.CompilerParams(vmem_limit_bytes=int(mib * MIB))


def cost(flops, size):
    return pl.CostEstimate(flops=flops, bytes_accessed=size, transcendentals=0)


def vmem():
    return pl.BlockSpec(memory_space=pltpu.VMEM)


def smem():
    return pl.BlockSpec(memory_space=pltpu.SMEM)


def list_kernel(
    bricks_z,
    inter_ref,
    pos_ref,
    anchor_ref,
    cell_ref,
    weight_ref,
    out_ref,
    rank_ref,
    base_ref,
    payload,
    lists,
    count_ref,
    extent,
):
    patches, verts = pos_ref.shape[1:]
    bricks = out_ref.shape[0]
    pos = pos_ref[...]
    cycle_term = pltpu.roll(pos, 1, 2) + pltpu.roll(pos, verts - 1, 2) - 2.0 * pos
    forces = TENSION * cycle_term + TETHER * (anchor_ref[...] - pos)
    cells = cell_ref[...].astype(F32)
    payload[:, 0:8, :] = weight_ref[...]
    for p in range(patches):
        payload[p, 8:11, :] = forces[:, p, :]
        payload[p, 11:14, :] = cells[:, p, :] + 1.0
        payload[p, 14:16, :] = jnp.zeros((2, verts), F32)
    lists[...] = jnp.zeros(lists.shape, F32)

    @pl.loop(0, bricks)
    def _(b):
        count_ref[b] = 0

    lane = lax.broadcasted_iota(jnp.int32, (patches, verts), 1)
    row = lax.broadcasted_iota(jnp.int32, (patches, verts), 0)
    upper = (
        lax.broadcasted_iota(jnp.int32, (verts, verts), 0)
        <= lax.broadcasted_iota(jnp.int32, (verts, verts), 1)
    ).astype(F32)
    codes, sums = [], []
    for i in range(2):
        first_y = jnp.zeros((patches, verts), F32)
        first_z = jnp.zeros((patches, verts), F32)
        for p in range(patches):
            brick = inter_ref[i, p]
            first_y = jnp.where(row == p, (brick // bricks_z * extent[1]).astype(F32), first_y)
            first_z = jnp.where(row == p, (brick % bricks_z * extent[2]).astype(F32), first_z)
        live = (
            (cells[1] >= first_y)
            & (cells[1] < first_y + extent[1])
            & (cells[2] >= first_z)
            & (cells[2] < first_z + extent[2])
        )
        mask = live.astype(F32)
        total = jnp.dot(mask.astype(BF), upper.astype(BF), preferred_element_type=F32)
        rank = (total - mask).astype(jnp.int32)
        rank_ref[i] = jnp.where(live, rank, -1)
        code = jnp.where(live, (lane - rank) + lane * 256 + 65536, 0)
        step = 1
        while step < verts:
            moving = jnp.where((code & step) != 0, code, 0)
            code = (code - moving) + pltpu.roll(moving, verts - step, 1)
            step *= 2
        codes.append(code)
        sums.append(total)
    wide_lane = lax.broadcasted_iota(jnp.int32, (16, verts), 1)
    for p in range(patches):
        for i in range(2):
            brick = inter_ref[i, p]
            base = count_ref[brick]
            base_ref[2 * p + i] = base
            count_ref[brick] = base + jnp.max(sums[i][p : p + 1, :]).astype(jnp.int32)
            block = lax.shift_right_logical(base, 7)
            shift = base & (verts - 1)
            code = jnp.broadcast_to(codes[i][p : p + 1, :], (8, verts))
            code = pltpu.roll(code, shift, 1)
            code = jnp.concatenate([code, code], axis=0)
            source = lax.shift_right_logical(code, 8) & (verts - 1)
            moved = jnp.take_along_axis(payload[p], source, axis=1)
            moved = jnp.where(code >= 65536, moved, 0.0)
            lists[brick, block] += jnp.where(wide_lane >= shift, moved, 0.0)
            lists[brick, block + 1] += jnp.where(wide_lane < shift, moved, 0.0)

    @pl.loop(0, bricks)
    def _(b):
        for j in range(SLOT_CAP):
            value = lists[b, j]
            first = j // 2 * GROUPS
            for g in range(3):
                out_ref[b, first + j % 2 * 3 + g] = value[4 * g : 4 * g + 4]
            out_ref[b, first + 6, j % 2 * 2 : j % 2 * 2 + 2] = value[12:14]


def build_lists(intersection, positions, anchors, base_cell, weights, bricks, bricks_z, extent):
    _, patches, verts = positions.shape

    def kernel(*refs):
        list_kernel(bricks_z, *refs, extent)

    return pl.pallas_call(
        kernel,
        out_shape=(
            jax.ShapeDtypeStruct((bricks, 2 * GROUPS, 4, verts), F32),
            jax.ShapeDtypeStruct((2, patches, verts), jnp.int32),
            jax.ShapeDtypeStruct((2 * patches,), jnp.int32),
        ),
        in_specs=[smem(), vmem(), vmem(), vmem(), vmem()],
        out_specs=(vmem(), vmem(), smem()),
        scratch_shapes=[
            pltpu.VMEM((patches, 16, verts), F32),
            pltpu.VMEM((bricks, SLOT_CAP + 1, 16, verts), F32),
            pltpu.SMEM((bricks,), jnp.int32),
        ],
        compiler_params=settings(56),
        name="vertex_lists",
    )(intersection, positions, anchors, base_cell, weights)


def block_rows(table_ref, owner, j):
    first = j // 2 * GROUPS
    group = first + j % 2 * 3
    weight = jnp.concatenate([table_ref[owner, group], table_ref[owner, group + 1]], axis=0)
    third = table_ref[owner, group + 2]
    line = j % 2 * 2
    last = table_ref[owner, first + 6, line : line + 2]
    return weight, third[0:3], jnp.concatenate([third[3:4], last], axis=0)


def pack_far(table_ref, packed, spot_ref, owner, spot):
    verts = table_ref.shape[3]
    lane = lax.broadcasted_iota(jnp.int32, (16, verts), 1)
    for j in range(2):
        weight, force, cells = block_rows(table_ref, owner, 2 + j)
        held = (cells[0:1] > 0.0).astype(F32)
        rows = jnp.concatenate([weight, force, cells, jnp.zeros((2, verts), F32)], axis=0)
        spot_ref[2 * owner + j] = spot
        block = lax.shift_right_logical(spot, 7)
        shift = spot & (verts - 1)
        rows = pltpu.roll(rows, shift, 1)
        packed[block] += jnp.where(lane >= shift, rows, 0.0)
        packed[block + 1] += jnp.where(lane < shift, rows, 0.0)
        spot = spot + jnp.sum(held).astype(jnp.int32)
    return spot


def packed_blocks(spot, verts):
    return lax.shift_right_logical(spot + verts - 1, 7)


def packed_rows(packed, block):
    return packed[block, 0:8], packed[block, 8:11], packed[block, 11:14]


def place_rows(place_ref, rows, extent):
    weight, force, cells = rows
    local, inside = [], None
    for d in range(3):
        value = cells[d : d + 1] - (place_ref[d] + 1).astype(F32)
        ok = (value >= 0.0) & (value < float(extent[d]))
        inside = ok if inside is None else inside & ok
        local.append(value)
    weight = weight * jnp.broadcast_to(inside.astype(F32), weight.shape)
    return weight, force, local


def halves(value):
    high = value.astype(BF).astype(F32)
    return high, value - high


def spread_scratch(extent, verts):
    size_x, size_y, size_z = extent
    depth = SPREAD_BLOCKS * 2 * verts
    return [
        pltpu.VMEM((2, 2, size_x * size_y, depth), BF),
        pltpu.VMEM((2, 6 * size_z, depth), BF),
        pltpu.VMEM((2, SPREAD_BLOCKS, 16, verts), F32),
        pltpu.VMEM((2, SPREAD_BLOCKS, 8, verts), F32),
        pltpu.VMEM((2, SPREAD_BLOCKS, 8, verts), F32),
    ]


def spread_tools(place_ref, extent, verts, total, a_buf, zf_buf, w_rows, f_rows, c_rows):
    size_x, size_y, size_z = extent
    iota_y = lax.broadcasted_iota(jnp.int32, (16, verts), 0).astype(F32).astype(BF)
    zero = jnp.zeros((16, verts), BF)

    def wide(ref, slot, j, row):
        return jnp.broadcast_to(ref[slot, j, row : row + 1, :], (16, verts)).astype(BF)

    def build(blocks, slot):
        for j, rows in enumerate(blocks):
            weight, force, local = place_rows(place_ref, rows, extent)
            w_hi, w_lo = halves(weight)
            f_hi, f_lo = halves(force)
            w_rows[slot, j, 0:8] = w_hi
            w_rows[slot, j, 8:16] = w_lo
            f_rows[slot, j, 0:3] = f_hi
            f_rows[slot, j, 4:7] = f_lo
            for d in range(3):
                c_rows[slot, j, d : d + 1] = local[d]
        for j in range(len(blocks)):
            xl = wide(c_rows, slot, j, 0)
            yl = wide(c_rows, slot, j, 1)
            zl = wide(c_rows, slot, j, 2)
            at_y0 = iota_y == yl
            at_y1 = iota_y == yl + 1.0
            lines = {}
            for part in range(2):
                for dx in range(2):
                    for dz in range(2):
                        first = part * 8 + dx * 4 + dz
                        lines[part, dx, dz] = jnp.where(
                            at_y0,
                            wide(w_rows, slot, j, first),
                            jnp.where(at_y1, wide(w_rows, slot, j, first + 2), zero),
                        )
            before = None
            for x in range(size_x):
                here = xl == float(x)
                for part in range(2):
                    for dz in range(2):
                        value = jnp.where(here, lines[part, 0, dz], zero)
                        if before is not None:
                            value = jnp.where(before, lines[part, 1, dz], value)
                        column = (j * 2 + dz) * verts
                        a_buf[slot, part, x * 16 : (x + 1) * 16, column : column + verts] = value
                before = here
            force = [wide(f_rows, slot, j, part * 4 + c) for part in range(2) for c in range(3)]
            for zb in range(size_z // 16):
                for dz in range(2):
                    at_z = iota_y == zl + float(dz - 16 * zb)
                    column = (j * 2 + dz) * verts
                    for part in range(2):
                        for c in range(3):
                            line = (part * 3 + c) * size_z + zb * 16
                            zf_buf[slot, line : line + 16, column : column + verts] = jnp.where(
                                at_z, force[part * 3 + c], zero
                            )

    def product(slot, blocks=SPREAD_BLOCKS):
        lines = 3 * size_z
        depth = blocks * 2 * verts
        high = lax.dot_general(
            zf_buf[slot, :, :depth], a_buf[slot, 0, :, :depth], NT, preferred_element_type=F32
        )
        low = lax.dot_general(
            zf_buf[slot, :lines, :depth],
            a_buf[slot, 1, :, :depth],
            NT,
            preferred_element_type=F32,
        )
        total[...] += high[:lines] + high[lines:] + low

    return build, product


def pair_blocks(table_ref, step, owners=2):
    return [block_rows(table_ref, owners * step + o, j) for o in range(owners) for j in range(2)]


def spread_kernel(
    extent,
    place_ref,
    table_ref,
    pop_any,
    total,
    packed,
    spot_ref,
    pop,
    sem,
    *scratch,
):
    load = pltpu.make_async_copy(pop_any, pop, sem)
    load.start()
    owners, _, _, verts = table_ref.shape
    build, product = spread_tools(place_ref, extent, verts, total, *scratch)
    steps = owners // SPREAD_OWNERS
    total[...] = jnp.zeros(total.shape, F32)
    packed[...] = jnp.zeros(packed.shape, F32)

    def fill(step, slot):
        build(pair_blocks(table_ref, step, SPREAD_OWNERS), slot)

    def pack(step, spot):
        for o in range(SPREAD_OWNERS):
            spot = pack_far(table_ref, packed, spot_ref, SPREAD_OWNERS * step + o, spot)
        return spot

    fill(0, 0)

    def near(i, spot):
        fill(2 * i + 1, 1)
        product(0)
        spot = pack(2 * i, spot)
        fill(jnp.minimum(2 * i + 2, steps - 1), 0)
        product(1)
        return pack(2 * i + 1, spot)

    spot_ref[2 * owners] = lax.fori_loop(0, steps // 2, near, jnp.int32(0))

    @pl.loop(0, packed_blocks(spot_ref[2 * owners], verts))
    def _(block):
        build([packed_rows(packed, block)], 0)
        product(0, 1)

    load.wait()


def spread(place, table, populations):
    owners, _, _, verts = table.shape
    extent = populations.shape[1:]
    size_x, size_y, size_z = extent
    anyspace = pl.BlockSpec(memory_space=pl.ANY)
    cross = size_x * size_y
    return pl.pallas_call(
        functools.partial(spread_kernel, extent),
        out_shape=(
            jax.ShapeDtypeStruct((3 * size_z, cross), F32),
            jax.ShapeDtypeStruct((2 * owners + 2, 16, verts), F32),
            jax.ShapeDtypeStruct((2 * owners + 1,), jnp.int32),
            jax.ShapeDtypeStruct(populations.shape, F32),
        ),
        in_specs=[smem(), vmem(), anyspace],
        out_specs=(vmem(), vmem(), smem(), vmem()),
        scratch_shapes=[pltpu.SemaphoreType.DMA] + spread_scratch(extent, verts),
        compiler_params=settings(49.5),
        cost_estimate=cost(18 * owners * 3 * size_z * cross * 4 * verts, MIB),
        name="spread",
    )(place, table, populations)


def along(vector, q):
    value = None
    for c in range(3):
        move = VELOCITIES[q][c]
        if move == 0:
            continue
        if value is None:
            value = vector[c] if move > 0 else -vector[c]
        else:
            value = value + vector[c] if move > 0 else value - vector[c]
    return value


def collide_plane(x, force, pop, solid):
    factor = 1.0 - 0.5 / RELAXATION
    rate = 1.0 / RELAXATION
    keep = 1.0 - rate
    cells = [pop[q, x] for q in range(19)]
    wall = solid[x] == 1
    rho = cells[0]
    for q in range(1, 19):
        rho = rho + cells[q]
    moment = []
    for c in range(3):
        value = None
        for q in range(1, 19, 2):
            if VELOCITIES[q][c] != 0:
                term = cells[q] - cells[q + 1]
                if VELOCITIES[q][c] < 0:
                    term = -term
                value = term if value is None else value + term
        moment.append(value)
    inverse = 1.0 / rho
    vel = [(moment[c] + 0.5 * force[c]) * inverse for c in range(3)]
    speed = vel[0] * vel[0] + vel[1] * vel[1] + vel[2] * vel[2]
    u_dot_f = vel[0] * force[0] + vel[1] * force[1] + vel[2] * force[2]
    three = 3.0 * factor
    nine = 9.0 * factor
    rest = (rate * rho) * (1.0 - 1.5 * speed) - three * u_dot_f
    quad = (4.5 * rate) * rho
    linear = (3.0 * rate) * rho
    results = [None] * 19
    results[0] = jnp.where(wall, cells[0], keep * cells[0] + LATTICE_WEIGHTS[0] * rest)

    for q in range(1, 19, 2):
        a = along(vel, q)
        b = along(force, q)
        weight = LATTICE_WEIGHTS[q]
        even = weight * (rest + a * (quad * a + nine * b))
        odd = weight * (linear * a + three * b)
        results[q] = jnp.where(wall, cells[q + 1], keep * cells[q] + (even + odd))
        results[q + 1] = jnp.where(wall, cells[q], keep * cells[q + 1] + (even - odd))
    return results, vel


def face_kernel(total, pop, solid, xface_ref, field):
    size_x, size_y, size_z = solid.shape
    for c in range(3):
        for half in range(size_x * size_y // 128):
            field[c, half * 128 : (half + 1) * 128, :] = jnp.transpose(
                total[c * size_z : (c + 1) * size_z, half * 128 : (half + 1) * 128]
            )
    for x, first, sign in ((size_x - 1, 0, 1), (0, 5, -1)):
        force = [field[c, x * size_y : (x + 1) * size_y, :] for c in range(3)]
        results, _ = collide_plane(x, force, pop, solid)
        for k, q in enumerate(X_LISTS[sign]):
            xface_ref[first + k] = results[q]


def x_faces(total, populations, solid):
    _, size_x, size_y, size_z = populations.shape
    return pl.pallas_call(
        face_kernel,
        out_shape=(
            jax.ShapeDtypeStruct((10, size_y, size_z), F32),
            jax.ShapeDtypeStruct((3, size_x * size_y, size_z), F32),
        ),
        in_specs=[vmem()] * 3,
        out_specs=(vmem(),) * 2,
        compiler_params=settings(12),
        cost_estimate=cost(2 * MIB, MIB),
        name="x_faces",
    )(total, populations, solid)


def collide_kernel(field, pop, solid, post, yfp_ref, yfm_ref, zfp_ref, zfm_ref, unit_ref):
    _, size_x, size_y, size_z = post.shape
    lane = lax.broadcasted_iota(jnp.int32, (size_y, size_z), 1)

    def plane(x, z_out):
        z_out = dict(zip((1, -1), z_out))
        lines = pl.ds(pl.multiple_of(x * 16, 16), 16)
        force = [field[c, lines, :] for c in range(3)]
        results, vel = collide_plane(x, force, pop, solid)
        for c in range(3):
            high, low = halves(vel[c])
            first = pl.ds(pl.multiple_of((x * 3 + c) * 16, 16), 16)
            unit_ref[first, 0:size_z] = high.astype(BF)
            unit_ref[first, size_z : 2 * size_z] = low.astype(BF)
        for q in range(19):
            post[q, x] = results[q]
        for sign, line, face in ((1, size_y - 1, yfp_ref), (-1, 0, yfm_ref)):
            for k, q in enumerate(Y_LISTS[sign]):
                face[k, pl.ds(x, 1), :] = results[q][line : line + 1, :]
        for sign, column in ((1, size_z - 1), (-1, 0)):
            for k, q in enumerate(Z_LISTS[sign]):
                place = k * 16 + x
                moved = pltpu.roll(results[q], (place - column + size_z) & (size_z - 1), 1)
                z_out[sign] = jnp.where(lane == place, moved, z_out[sign])
        return z_out[1], z_out[-1]

    empty = jnp.zeros((size_y, size_z), F32)
    zfp_ref[...], zfm_ref[...] = lax.fori_loop(0, size_x, plane, (empty, empty), unroll=2)


def collide(field, populations, solid):
    _, size_x, size_y, size_z = populations.shape
    face_y = jax.ShapeDtypeStruct((5, size_x, size_z), F32)
    face_z = jax.ShapeDtypeStruct((size_y, size_z), F32)
    return pl.pallas_call(
        collide_kernel,
        out_shape=(
            jax.ShapeDtypeStruct(populations.shape, F32),
            face_y,
            face_y,
            face_z,
            face_z,
            jax.ShapeDtypeStruct((size_x * size_y * 3, 2 * size_z), BF),
        ),
        in_specs=[vmem()] * 3,
        out_specs=(vmem(),) * 6,
        compiler_params=settings(12),
        cost_estimate=cost(16 * MIB, 8 * MIB),
        name="collide",
    )(field, populations, solid)


def sample_scratch(extent, verts):
    size_x, size_y, size_z = extent
    return [
        pltpu.VMEM((2, SLOT_CAP, 2 * size_z, 2 * verts), BF),
        pltpu.VMEM((2, 3 * size_x * size_y, 2 * verts), F32),
        pltpu.VMEM((2, SLOT_CAP, 8, verts), F32),
        pltpu.VMEM((2, SLOT_CAP, 8, verts), F32),
    ]


def sample_tools(place_ref, unit_ref, extent, verts, hot, grid_buf, w_rows, c_rows):
    size_x, size_y, size_z = extent
    iota_y = lax.broadcasted_iota(jnp.int32, (16, verts), 0).astype(F32)
    iota_b = iota_y.astype(BF)
    one = jnp.ones((16, verts), BF)
    zero_b = jnp.zeros((16, verts), BF)
    zero = jnp.zeros((16, verts), F32)

    def wide(ref, slot, j, row):
        return jnp.broadcast_to(ref[slot, j, row : row + 1, :], (16, verts))

    def prepare(blocks, slot):
        for j, rows in enumerate(blocks):
            weight, _, local = place_rows(place_ref, rows, extent)
            w_rows[slot, j] = weight
            for d in range(3):
                c_rows[slot, j, d : d + 1] = local[d]
        for j in range(len(blocks)):
            zl = wide(c_rows, slot, j, 2).astype(BF)
            for zb in range(size_z // 16):
                for dz in range(2):
                    value = jnp.where(iota_b == zl + float(dz - 16 * zb), one, zero_b)
                    for part in range(2):
                        line = part * size_z + zb * 16
                        hot[slot, j, line : line + 16, dz * verts : (dz + 1) * verts] = value

    def product(slot, j):
        grid_buf[j % 2] = lax.dot_general(unit_ref[...], hot[slot, j], NN, preferred_element_type=F32)

    def select(slot, j):
        xl = wide(c_rows, slot, j, 0)
        yl = wide(c_rows, slot, j, 1)
        at_y0 = iota_y == yl
        at_y1 = iota_y == yl + 1.0
        lines = {}
        for dx in range(2):
            for dz in range(2):
                first = dx * 4 + dz
                lines[dx, dz] = jnp.where(
                    at_y0,
                    wide(w_rows, slot, j, first),
                    jnp.where(at_y1, wide(w_rows, slot, j, first + 2), zero),
                )
        sums = [zero, zero, zero]
        before = None
        for x in range(size_x):
            here = xl == float(x)
            for dz in range(2):
                value = jnp.where(here, lines[0, dz], zero)
                if before is not None:
                    value = jnp.where(before, lines[1, dz], value)
                for c in range(3):
                    first = (x * 3 + c) * 16
                    part = grid_buf[j % 2, first : first + 16, dz * verts : (dz + 1) * verts]
                    sums[c] = sums[c] + value * part
            before = here
        return [jnp.sum(value, axis=0, keepdims=True) for value in sums]

    def work(slot, store):
        product(slot, 0)
        for j in range(SLOT_CAP):
            if j + 1 < SLOT_CAP:
                product(slot, j + 1)
            store(j, select(slot, j))

    return prepare, product, select, work


def x_plane(xr_ref, q):
    sign = VELOCITIES[q][0]
    return xr_ref[(0 if sign > 0 else 5) + X_LISTS[sign].index(q)]


def sample_steps(table_ref, first, last, prepare, work, put):
    def store(step):
        return lambda j, values: put(2 * step + j // 2, j % 2, values)

    prepare(pair_blocks(table_ref, first), 0)

    @pl.loop(0, (last - first) // 2)
    def _(i):
        step = first + 2 * i
        prepare(pair_blocks(table_ref, step + 1), 1)
        work(0, store(step))
        prepare(pair_blocks(table_ref, jnp.minimum(step + 2, last - 1)), 0)
        work(1, store(step + 1))


def sample_part_kernel(extent, first, last, place_ref, table_ref, unit_ref, *refs):
    out_ref, scratch = refs[-5], refs[-4:]
    verts = table_ref.shape[3]
    prepare, _, _, work = sample_tools(place_ref, unit_ref, extent, verts, *scratch)

    def put(owner, line, values):
        for c in range(3):
            out_ref[owner - 2 * first, c, line : line + 1, :] = values[c]

    sample_steps(table_ref, first, last, prepare, work, put)


def sample_part(place, table, unit, order, first, last, extent):
    owners, _, _, verts = table.shape
    size_x, size_y, size_z = extent
    return pl.pallas_call(
        functools.partial(sample_part_kernel, extent, first, last),
        out_shape=jax.ShapeDtypeStruct((2 * (last - first), 3, 2, verts), F32),
        in_specs=[smem(), vmem(), vmem()] + [pl.BlockSpec(memory_space=pl.ANY)] * len(order),
        out_specs=vmem(),
        scratch_shapes=sample_scratch(extent, verts),
        compiler_params=settings(12),
        cost_estimate=cost(
            32 * (last - first) * 3 * size_x * size_y * size_z * verts, MIB
        ),
        name="sample_part",
    )(place, table, unit, *order)


def sample_kernel(
    extent, place_ref, spot_ref, table_ref, packed, unit_ref, part_ref, *refs
):
    out_ref, found, scratch = refs[-6], refs[-5], refs[-4:]
    owners, _, _, verts = table_ref.shape
    prepare, product, select, work = sample_tools(place_ref, unit_ref, extent, verts, *scratch)
    done = part_ref.shape[0]
    for c in range(3):
        out_ref[0:done, c, 0:2] = part_ref[:, c]
        out_ref[:, c, 2:4] = jnp.zeros((owners, 2, verts), F32)

    def put(owner, line, values):
        for c in range(3):
            out_ref[owner, c, line : line + 1, :] = values[c]

    sample_steps(table_ref, done // 2, owners // 2, prepare, work, put)

    @pl.loop(0, packed_blocks(spot_ref[2 * owners], verts))
    def _(block):
        prepare([packed_rows(packed, block)], 0)
        product(0, 0)
        values = select(0, 0)
        for c in range(3):
            found[block, c : c + 1, :] = values[c]

    lane = lax.broadcasted_iota(jnp.int32, (4, verts), 1)
    for owner in range(owners):
        for j in range(2):
            spot = spot_ref[2 * owner + j]

            @pl.when(spot_ref[2 * owner + j + 1] > spot)
            def _(owner=owner, j=j, spot=spot):
                block = lax.shift_right_logical(spot, 7)
                shift = spot & (verts - 1)
                back = (verts - shift) & (verts - 1)
                first = pltpu.roll(found[block, 0:4], back, 1)
                second = pltpu.roll(found[block + 1, 0:4], back, 1)
                value = jnp.where(lane < verts - shift, first, second)
                for c in range(3):
                    out_ref[owner, c, 2 + j : 3 + j, :] = value[c : c + 1]


def sample(place, spots, table, packed, unit, part, order, extent):
    owners, _, _, verts = table.shape
    size_x, size_y, size_z = extent
    return pl.pallas_call(
        functools.partial(sample_kernel, extent),
        out_shape=jax.ShapeDtypeStruct((owners, 3, SLOT_CAP, verts), F32),
        in_specs=[smem(), smem()]
        + [vmem()] * 4
        + [pl.BlockSpec(memory_space=pl.ANY)] * len(order),
        out_specs=vmem(),
        scratch_shapes=[pltpu.VMEM((2 * owners + 2, 8, verts), F32)]
        + sample_scratch(extent, verts),
        compiler_params=settings(12),
        cost_estimate=cost(8 * owners * 3 * size_x * size_y * size_z * verts, MIB),
        name="sample_velocity",
    )(place, spots, table, packed, unit, part, *order)


def y_message_kernel(xr_ref, yfp_ref, yfm_ref, plus_ref, minus_ref):
    size_y = xr_ref.shape[1]
    for sign, face, out in ((1, yfp_ref, plus_ref), (-1, yfm_ref, minus_ref)):
        out[0:5] = face[...]
        line = size_y - 1 if sign > 0 else 0
        for e, q in enumerate(Y_EDGES[sign]):
            out[5, e : e + 1, :] = x_plane(xr_ref, q)[line : line + 1, :]


def y_messages(x_halo, y_plus, y_minus):
    shape = jax.ShapeDtypeStruct((6,) + y_plus.shape[1:], F32)
    return pl.pallas_call(
        y_message_kernel,
        out_shape=(shape, shape),
        in_specs=[vmem()] * 3,
        out_specs=(vmem(), vmem()),
        compiler_params=settings(4),
        name="y_messages",
    )(x_halo, y_plus, y_minus)


def z_message_kernel(xr_ref, yrp_ref, yrm_ref, zfp_ref, zfm_ref, plus_ref, minus_ref):
    size_y, size_z = zfp_ref.shape
    y_halo = {1: yrp_ref, -1: yrm_ref}
    lane = lax.broadcasted_iota(jnp.int32, (size_y, size_z), 1)
    for sign, face, out in ((1, zfp_ref, plus_ref), (-1, zfm_ref, minus_ref)):
        column = size_z - 1 if sign > 0 else 0
        block = face[...]
        for e, q in enumerate(Z_EDGES[sign]):
            if VELOCITIES[q][0] != 0:
                plane = x_plane(xr_ref, q)
            else:
                y_sign = VELOCITIES[q][1]
                plane = y_halo[y_sign][Y_LISTS[y_sign].index(q)]
            spot = EDGE_LANE + e
            block = jnp.where(lane == spot, pltpu.roll(plane, (spot - column) % size_z, 1), block)
        out[...] = block


def z_messages(x_halo, y_plus, y_minus, z_plus, z_minus):
    shape = jax.ShapeDtypeStruct(z_plus.shape, F32)
    return pl.pallas_call(
        z_message_kernel,
        out_shape=(shape, shape),
        in_specs=[vmem()] * 5,
        out_specs=(vmem(), vmem()),
        compiler_params=settings(4),
        name="z_messages",
    )(x_halo, y_plus, y_minus, z_plus, z_minus)


def stream_kernel(
    post,
    xr_ref,
    yrp_ref,
    yrm_ref,
    zrp_ref,
    zrm_ref,
    read_hbm,
    read,
    out_sem,
):
    _, size_x, size_y, size_z = post.shape
    y_halo = {1: yrp_ref, -1: yrm_ref}
    z_halo = {1: zrp_ref, -1: zrm_ref}
    stores = [pltpu.make_async_copy(read.at[q], read_hbm.at[q], out_sem.at[q]) for q in range(19)]
    lane = lax.broadcasted_iota(jnp.int32, (size_y, size_z), 1)
    row = lax.broadcasted_iota(jnp.int32, (size_y, size_z), 0)

    def shift_z(plane, cz, place):
        moved = pltpu.roll(plane, cz % size_z, 1)
        target = 0 if cz > 0 else size_z - 1
        column = pltpu.roll(z_halo[cz][...], (target - place) % size_z, 1)
        return jnp.where(lane == target, column, moved)

    for q in range(19):
        cx, cy, cz = VELOCITIES[q]
        rows = None
        if cy != 0:
            rows = y_halo[cy][Y_LISTS[cy].index(q)]
            if cz != 0:
                rows = shift_z(rows, cz, EDGE_LANE + Z_EDGES[cz].index(q))
        for x in range(size_x):
            source = x - cx
            outside = source < 0 or source >= size_x
            plane = x_plane(xr_ref, q) if outside else post[q, source]
            if cz != 0:
                if outside:
                    place = EDGE_LANE + Z_EDGES[cz].index(q)
                else:
                    place = Z_LISTS[cz].index(q) * 16 + source
                plane = shift_z(plane, cz, place)
            if cy != 0:
                moved = pltpu.roll(plane, cy % size_y, 0)
                target = 0 if cy > 0 else size_y - 1
                if outside:
                    e = Y_EDGES[cy].index(q)
                    line = y_halo[cy][5, e : e + 1, :]
                else:
                    line = rows[source : source + 1, :]
                plane = jnp.where(row == target, jnp.broadcast_to(line, moved.shape), moved)
            read[q, x] = plane
        stores[q].start()
    for store in stores:
        store.wait()


def stream(post, x_halo, y_plus, y_minus, z_plus, z_minus):
    anyspace = pl.BlockSpec(memory_space=pl.ANY)
    return pl.pallas_call(
        stream_kernel,
        out_shape=jax.ShapeDtypeStruct(post.shape, F32),
        in_specs=[vmem()] * 6,
        out_specs=anyspace,
        scratch_shapes=[
            pltpu.VMEM(post.shape, F32),
            pltpu.SemaphoreType.DMA((19,)),
        ],
        compiler_params=settings(10),
        cost_estimate=cost(MIB, 16 * MIB),
        name="stream_populations",
    )(post, x_halo, y_plus, y_minus, z_plus, z_minus)


def collect_kernel(inter_ref, base_ref, rank_ref, back_ref, out_ref):
    patches, verts = rank_ref.shape[1:]
    line = lax.broadcasted_iota(jnp.int32, (16, verts), 0) & (SLOT_CAP - 1)
    for p in range(patches):
        value = None
        for i in range(2):
            brick = inter_ref[i, p]
            base = base_ref[2 * p + i]
            rank = jnp.broadcast_to(rank_ref[i, p : p + 1, :], (8, verts))
            spot = jnp.concatenate([rank + base] * 2, axis=0)
            rows = [back_ref[brick, c] for c in range(3)] + [jnp.zeros((4, verts), F32)]
            picked = jnp.concatenate(rows, axis=0)
            picked = jnp.take_along_axis(picked, spot & (verts - 1), axis=1)
            here = lax.shift_right_logical(spot, 7) == line
            picked = jnp.where(here & (jnp.concatenate([rank] * 2, axis=0) >= 0), picked, 0.0)
            value = picked if value is None else value + picked
        value = value + pltpu.roll(value, 15, 0)
        value = value + pltpu.roll(value, 14, 0)
        value = jnp.concatenate([value[4 * c : 4 * c + 1] for c in range(3)], axis=0)
        out_ref[:, p, :] = value


def collect(intersection, bases, ranks, back):
    _, patches, verts = ranks.shape
    return pl.pallas_call(
        collect_kernel,
        out_shape=jax.ShapeDtypeStruct((3, patches, verts), F32),
        in_specs=[smem()] * 2 + [vmem()] * 2,
        out_specs=vmem(),
        compiler_params=settings(4),
        name="collect_velocity",
    )(intersection, bases, ranks, back)


def shifted(value, axis, step):
    count = lax.axis_size(axis)
    return lax.ppermute(value, axis, [(i, (i + step) % count) for i in range(count)])


def exchanged(value):
    return lax.all_to_all(value, ("gy", "gz"), split_axis=0, concat_axis=0, tiled=True)


def body(populations, solid_flags, positions, anchors, base_cell, weights, intersection):
    extent = populations.shape[1:]
    axes = ("gx", "gy", "gz")
    bricks = lax.axis_size("gy") * lax.axis_size("gz")
    here = [lax.axis_index(axis) for axis in axes]
    place = jnp.stack(
        [here[d] * extent[d] for d in range(3)]
        + here
        + [jnp.int32(lax.axis_size(axis)) for axis in axes]
    ).astype(jnp.int32)
    lists = intersection.T
    outgoing, ranks, bases = build_lists(
        lists,
        jnp.transpose(positions, (1, 0, 2)),
        jnp.transpose(anchors, (1, 0, 2)),
        jnp.transpose(base_cell, (1, 0, 2)),
        weights,
        bricks,
        lax.axis_size("gz"),
        extent,
    )
    table = exchanged(outgoing)
    total, packed, spots, populations = spread(place, table, populations)
    x_face, field = x_faces(total, populations, solid_flags)
    post, y_plus, y_minus, z_plus, z_minus, unit = collide(field, populations, solid_flags)
    if lax.axis_size("gx") == 2:
        x_halo = shifted(x_face, "gx", 1)
    else:
        x_halo = jnp.concatenate(
            [shifted(x_face[:5], "gx", 1), shifted(x_face[5:], "gx", -1)], axis=0
        )
    y_plus, y_minus = y_messages(x_halo, y_plus, y_minus)
    y_plus = shifted(y_plus, "gy", 1)
    y_minus = shifted(y_minus, "gy", -1)
    steps = table.shape[0] // 2
    part = sample_part(place, table, unit, (x_halo,), 0, steps // 4 * 3, extent)
    order = (y_plus, y_minus)
    sampled = sample(place, spots, table, packed, unit, part, order, extent)
    back = exchanged(sampled)
    z_plus, z_minus = z_messages(x_halo, y_plus, y_minus, z_plus, z_minus)
    z_plus = shifted(z_plus, "gz", 1)
    z_minus = shifted(z_minus, "gz", -1)
    read = stream(post, x_halo, y_plus, y_minus, z_plus, z_minus)
    velocity = collect(lists, bases, ranks, back)
    return read, jnp.transpose(velocity, (1, 0, 2))


def solution(mesh):
    return jax.shard_map(
        body,
        mesh=mesh,
        in_specs=(
            P(None, "gx", "gy", "gz"),
            P("gx", "gy", "gz"),
            P(("gx", "gy", "gz"), None, None),
            P(("gx", "gy", "gz"), None, None),
            P(("gx", "gy", "gz"), None, None),
            P(("gx", "gy", "gz"), None, None),
            P(("gx", "gy", "gz"), None),
        ),
        out_specs=(P(None, "gx", "gy", "gz"), P(("gx", "gy", "gz"), None, None)),
        check_vma=False,
    )
```

```python
import functools

import jax
import jax.numpy as jnp
from jax import lax
from jax.experimental import pallas as pl
from jax.experimental.pallas import tpu as pltpu
from jax.sharding import PartitionSpec as P

SLOT_CAP = 4
GROUPS = 7
SPREAD_OWNERS = 4
SPREAD_BLOCKS = 2 * SPREAD_OWNERS
EDGE_LANE = 80

RELAXATION = 0.8
TENSION = 0.05
TETHER = 0.5
VELOCITIES = [
    (0, 0, 0),
    (1, 0, 0),
    (-1, 0, 0),
    (0, 1, 0),
    (0, -1, 0),
    (0, 0, 1),
    (0, 0, -1),
    (1, 1, 0),
    (-1, -1, 0),
    (1, -1, 0),
    (-1, 1, 0),
    (1, 0, 1),
    (-1, 0, -1),
    (1, 0, -1),
    (-1, 0, 1),
    (0, 1, 1),
    (0, -1, -1),
    (0, 1, -1),
    (0, -1, 1),
]
LATTICE_WEIGHTS = [1.0 / 3.0] + [1.0 / 18.0] * 6 + [1.0 / 36.0] * 12


def crossing(axis, sign):
    return [q for q in range(19) if VELOCITIES[q][axis] == sign]


X_LISTS = {1: crossing(0, 1), -1: crossing(0, -1)}
Y_LISTS = {1: crossing(1, 1), -1: crossing(1, -1)}
Z_LISTS = {1: crossing(2, 1), -1: crossing(2, -1)}
Y_EDGES = {s: [q for q in Y_LISTS[s] if VELOCITIES[q][0] != 0] for s in (1, -1)}
Z_EDGES = {
    s: [q for q in Z_LISTS[s] if VELOCITIES[q][0] != 0 or VELOCITIES[q][1] != 0] for s in (1, -1)
}

BF = jnp.bfloat16
F32 = jnp.float32
MIB = 1024 * 1024
NT = (((1,), (1,)), ((), ()))
NN = (((1,), (0,)), ((), ()))


def settings(mib):
    return pltpu.CompilerParams(vmem_limit_bytes=int(mib * MIB))


def cost(flops, size):
    return pl.CostEstimate(flops=flops, bytes_accessed=size, transcendentals=0)


def vmem():
    return pl.BlockSpec(memory_space=pltpu.VMEM)


def smem():
    return pl.BlockSpec(memory_space=pltpu.SMEM)


def list_kernel(
    bricks_z,
    inter_ref,
    pos_ref,
    anchor_ref,
    cell_ref,
    weight_ref,
    out_ref,
    rank_ref,
    base_ref,
    payload,
    lists,
    count_ref,
    extent,
):
    patches, verts = pos_ref.shape[1:]
    bricks = out_ref.shape[0]
    pos = pos_ref[...]
    cycle_term = pltpu.roll(pos, 1, 2) + pltpu.roll(pos, verts - 1, 2) - 2.0 * pos
    forces = TENSION * cycle_term + TETHER * (anchor_ref[...] - pos)
    cells = cell_ref[...].astype(F32)
    payload[:, 0:8, :] = weight_ref[...]
    for p in range(patches):
        payload[p, 8:11, :] = forces[:, p, :]
        payload[p, 11:14, :] = cells[:, p, :] + 1.0
        payload[p, 14:16, :] = jnp.zeros((2, verts), F32)
    lists[...] = jnp.zeros(lists.shape, F32)

    @pl.loop(0, bricks)
    def _(b):
        count_ref[b] = 0

    lane = lax.broadcasted_iota(jnp.int32, (patches, verts), 1)
    row = lax.broadcasted_iota(jnp.int32, (patches, verts), 0)
    upper = (
        lax.broadcasted_iota(jnp.int32, (verts, verts), 0)
        <= lax.broadcasted_iota(jnp.int32, (verts, verts), 1)
    ).astype(F32)
    codes, sums = [], []
    for i in range(2):
        first_y = jnp.zeros((patches, verts), F32)
        first_z = jnp.zeros((patches, verts), F32)
        for p in range(patches):
            brick = inter_ref[i, p]
            first_y = jnp.where(row == p, (brick // bricks_z * extent[1]).astype(F32), first_y)
            first_z = jnp.where(row == p, (brick % bricks_z * extent[2]).astype(F32), first_z)
        live = (
            (cells[1] >= first_y)
            & (cells[1] < first_y + extent[1])
            & (cells[2] >= first_z)
            & (cells[2] < first_z + extent[2])
        )
        mask = live.astype(F32)
        total = jnp.dot(mask.astype(BF), upper.astype(BF), preferred_element_type=F32)
        rank = (total - mask).astype(jnp.int32)
        rank_ref[i] = jnp.where(live, rank, -1)
        code = jnp.where(live, (lane - rank) + lane * 256 + 65536, 0)
        step = 1
        while step < verts:
            moving = jnp.where((code & step) != 0, code, 0)
            code = (code - moving) + pltpu.roll(moving, verts - step, 1)
            step *= 2
        codes.append(code)
        sums.append(total)
    wide_lane = lax.broadcasted_iota(jnp.int32, (16, verts), 1)
    for p in range(patches):
        for i in range(2):
            brick = inter_ref[i, p]
            base = count_ref[brick]
            base_ref[2 * p + i] = base
            count_ref[brick] = base + jnp.max(sums[i][p : p + 1, :]).astype(jnp.int32)
            block = lax.shift_right_logical(base, 7)
            shift = base & (verts - 1)
            code = jnp.broadcast_to(codes[i][p : p + 1, :], (8, verts))
            code = pltpu.roll(code, shift, 1)
            code = jnp.concatenate([code, code], axis=0)
            source = lax.shift_right_logical(code, 8) & (verts - 1)
            moved = jnp.take_along_axis(payload[p], source, axis=1)
            moved = jnp.where(code >= 65536, moved, 0.0)
            lists[brick, block] += jnp.where(wide_lane >= shift, moved, 0.0)
            lists[brick, block + 1] += jnp.where(wide_lane < shift, moved, 0.0)

    @pl.loop(0, bricks)
    def _(b):
        for j in range(SLOT_CAP):
            value = lists[b, j]
            first = j // 2 * GROUPS
            for g in range(3):
                out_ref[b, first + j % 2 * 3 + g] = value[4 * g : 4 * g + 4]
            out_ref[b, first + 6, j % 2 * 2 : j % 2 * 2 + 2] = value[12:14]


def build_lists(intersection, positions, anchors, base_cell, weights, bricks, bricks_z, extent):
    _, patches, verts = positions.shape

    def kernel(*refs):
        list_kernel(bricks_z, *refs, extent)

    return pl.pallas_call(
        kernel,
        out_shape=(
            jax.ShapeDtypeStruct((bricks, 2 * GROUPS, 4, verts), F32),
            jax.ShapeDtypeStruct((2, patches, verts), jnp.int32),
            jax.ShapeDtypeStruct((2 * patches,), jnp.int32),
        ),
        in_specs=[smem(), vmem(), vmem(), vmem(), vmem()],
        out_specs=(vmem(), vmem(), smem()),
        scratch_shapes=[
            pltpu.VMEM((patches, 16, verts), F32),
            pltpu.VMEM((bricks, SLOT_CAP + 1, 16, verts), F32),
            pltpu.SMEM((bricks,), jnp.int32),
        ],
        compiler_params=settings(56),
        name="vertex_lists",
    )(intersection, positions, anchors, base_cell, weights)


def block_rows(table_ref, owner, j):
    first = j // 2 * GROUPS
    group = first + j % 2 * 3
    weight = jnp.concatenate([table_ref[owner, group], table_ref[owner, group + 1]], axis=0)
    third = table_ref[owner, group + 2]
    line = j % 2 * 2
    last = table_ref[owner, first + 6, line : line + 2]
    return weight, third[0:3], jnp.concatenate([third[3:4], last], axis=0)


def pack_far(table_ref, packed, spot_ref, owner, spot):
    verts = table_ref.shape[3]
    lane = lax.broadcasted_iota(jnp.int32, (16, verts), 1)
    for j in range(2):
        weight, force, cells = block_rows(table_ref, owner, 2 + j)
        held = (cells[0:1] > 0.0).astype(F32)
        rows = jnp.concatenate([weight, force, cells, jnp.zeros((2, verts), F32)], axis=0)
        spot_ref[2 * owner + j] = spot
        block = lax.shift_right_logical(spot, 7)
        shift = spot & (verts - 1)
        rows = pltpu.roll(rows, shift, 1)
        packed[block] += jnp.where(lane >= shift, rows, 0.0)
        packed[block + 1] += jnp.where(lane < shift, rows, 0.0)
        spot = spot + jnp.sum(held).astype(jnp.int32)
    return spot


def packed_blocks(spot, verts):
    return lax.shift_right_logical(spot + verts - 1, 7)


def packed_rows(packed, block):
    return packed[block, 0:8], packed[block, 8:11], packed[block, 11:14]


def place_rows(place_ref, rows, extent):
    weight, force, cells = rows
    local, inside = [], None
    for d in range(3):
        value = cells[d : d + 1] - (place_ref[d] + 1).astype(F32)
        ok = (value >= 0.0) & (value < float(extent[d]))
        inside = ok if inside is None else inside & ok
        local.append(value)
    weight = weight * jnp.broadcast_to(inside.astype(F32), weight.shape)
    return weight, force, local


def halves(value):
    high = value.astype(BF).astype(F32)
    return high, value - high


def spread_scratch(extent, verts):
    size_x, size_y, size_z = extent
    depth = SPREAD_BLOCKS * 2 * verts
    return [
        pltpu.VMEM((2, 2, size_x * size_y, depth), BF),
        pltpu.VMEM((2, 6 * size_z, depth), BF),
        pltpu.VMEM((2, SPREAD_BLOCKS, 16, verts), F32),
        pltpu.VMEM((2, SPREAD_BLOCKS, 8, verts), F32),
        pltpu.VMEM((2, SPREAD_BLOCKS, 8, verts), F32),
    ]


def spread_tools(place_ref, extent, verts, total, a_buf, zf_buf, w_rows, f_rows, c_rows):
    size_x, size_y, size_z = extent
    iota_y = lax.broadcasted_iota(jnp.int32, (16, verts), 0).astype(F32).astype(BF)
    zero = jnp.zeros((16, verts), BF)

    def wide(ref, slot, j, row):
        return jnp.broadcast_to(ref[slot, j, row : row + 1, :], (16, verts)).astype(BF)

    def build(blocks, slot):
        for j, rows in enumerate(blocks):
            weight, force, local = place_rows(place_ref, rows, extent)
            w_hi, w_lo = halves(weight)
            f_hi, f_lo = halves(force)
            w_rows[slot, j, 0:8] = w_hi
            w_rows[slot, j, 8:16] = w_lo
            f_rows[slot, j, 0:3] = f_hi
            f_rows[slot, j, 4:7] = f_lo
            for d in range(3):
                c_rows[slot, j, d : d + 1] = local[d]
        for j in range(len(blocks)):
            xl = wide(c_rows, slot, j, 0)
            yl = wide(c_rows, slot, j, 1)
            zl = wide(c_rows, slot, j, 2)
            at_y0 = iota_y == yl
            at_y1 = iota_y == yl + 1.0
            lines = {}
            for part in range(2):
                for dx in range(2):
                    for dz in range(2):
                        first = part * 8 + dx * 4 + dz
                        lines[part, dx, dz] = jnp.where(
                            at_y0,
                            wide(w_rows, slot, j, first),
                            jnp.where(at_y1, wide(w_rows, slot, j, first + 2), zero),
                        )
            before = None
            for x in range(size_x):
                here = xl == float(x)
                for part in range(2):
                    for dz in range(2):
                        value = jnp.where(here, lines[part, 0, dz], zero)
                        if before is not None:
                            value = jnp.where(before, lines[part, 1, dz], value)
                        column = (j * 2 + dz) * verts
                        a_buf[slot, part, x * 16 : (x + 1) * 16, column : column + verts] = value
                before = here
            force = [wide(f_rows, slot, j, part * 4 + c) for part in range(2) for c in range(3)]
            for zb in range(size_z // 16):
                for dz in range(2):
                    at_z = iota_y == zl + float(dz - 16 * zb)
                    column = (j * 2 + dz) * verts
                    for part in range(2):
                        for c in range(3):
                            line = (part * 3 + c) * size_z + zb * 16
                            zf_buf[slot, line : line + 16, column : column + verts] = jnp.where(
                                at_z, force[part * 3 + c], zero
                            )

    def product(slot, blocks=SPREAD_BLOCKS):
        lines = 3 * size_z
        depth = blocks * 2 * verts
        high = lax.dot_general(
            zf_buf[slot, :, :depth], a_buf[slot, 0, :, :depth], NT, preferred_element_type=F32
        )
        low = lax.dot_general(
            zf_buf[slot, :lines, :depth],
            a_buf[slot, 1, :, :depth],
            NT,
            preferred_element_type=F32,
        )
        total[...] += high[:lines] + high[lines:] + low

    return build, product


def pair_blocks(table_ref, step, owners=2):
    return [block_rows(table_ref, owners * step + o, j) for o in range(owners) for j in range(2)]


def spread_kernel(
    extent,
    place_ref,
    table_ref,
    pop_any,
    total,
    packed,
    spot_ref,
    pop,
    sem,
    *scratch,
):
    load = pltpu.make_async_copy(pop_any, pop, sem)
    load.start()
    owners, _, _, verts = table_ref.shape
    build, product = spread_tools(place_ref, extent, verts, total, *scratch)
    steps = owners // SPREAD_OWNERS
    total[...] = jnp.zeros(total.shape, F32)
    packed[...] = jnp.zeros(packed.shape, F32)

    def fill(step, slot):
        build(pair_blocks(table_ref, step, SPREAD_OWNERS), slot)

    def pack(step, spot):
        for o in range(SPREAD_OWNERS):
            spot = pack_far(table_ref, packed, spot_ref, SPREAD_OWNERS * step + o, spot)
        return spot

    fill(0, 0)

    def near(i, spot):
        fill(2 * i + 1, 1)
        product(0)
        spot = pack(2 * i, spot)
        fill(2 * i + 2, 0)
        product(1)
        return pack(2 * i + 1, spot)

    spot = lax.fori_loop(0, steps // 2 - 1, near, jnp.int32(0))
    fill(steps - 1, 1)
    product(0)
    spot = pack(steps - 2, spot)
    product(1)
    spot_ref[2 * owners] = pack(steps - 1, spot)

    @pl.loop(0, packed_blocks(spot_ref[2 * owners], verts))
    def _(block):
        build([packed_rows(packed, block)], 0)
        product(0, 1)

    load.wait()


def spread(place, table, populations):
    owners, _, _, verts = table.shape
    extent = populations.shape[1:]
    size_x, size_y, size_z = extent
    anyspace = pl.BlockSpec(memory_space=pl.ANY)
    cross = size_x * size_y
    return pl.pallas_call(
        functools.partial(spread_kernel, extent),
        out_shape=(
            jax.ShapeDtypeStruct((3 * size_z, cross), F32),
            jax.ShapeDtypeStruct((2 * owners + 2, 16, verts), F32),
            jax.ShapeDtypeStruct((2 * owners + 1,), jnp.int32),
            jax.ShapeDtypeStruct(populations.shape, F32),
        ),
        in_specs=[smem(), vmem(), anyspace],
        out_specs=(vmem(), vmem(), smem(), vmem()),
        scratch_shapes=[pltpu.SemaphoreType.DMA] + spread_scratch(extent, verts),
        compiler_params=settings(49.5),
        cost_estimate=cost(18 * owners * 3 * size_z * cross * 4 * verts, MIB),
        name="spread",
    )(place, table, populations)


def along(vector, q):
    value = None
    for c in range(3):
        move = VELOCITIES[q][c]
        if move == 0:
            continue
        if value is None:
            value = vector[c] if move > 0 else -vector[c]
        else:
            value = value + vector[c] if move > 0 else value - vector[c]
    return value


def collide_plane(x, force, pop, solid):
    factor = 1.0 - 0.5 / RELAXATION
    rate = 1.0 / RELAXATION
    keep = 1.0 - rate
    cells = [pop[q, x] for q in range(19)]
    wall = solid[x] == 1
    rho = cells[0]
    for q in range(1, 19):
        rho = rho + cells[q]
    moment = []
    for c in range(3):
        value = None
        for q in range(1, 19, 2):
            if VELOCITIES[q][c] != 0:
                term = cells[q] - cells[q + 1]
                if VELOCITIES[q][c] < 0:
                    term = -term
                value = term if value is None else value + term
        moment.append(value)
    inverse = 1.0 / rho
    vel = [(moment[c] + 0.5 * force[c]) * inverse for c in range(3)]
    speed = vel[0] * vel[0] + vel[1] * vel[1] + vel[2] * vel[2]
    u_dot_f = vel[0] * force[0] + vel[1] * force[1] + vel[2] * force[2]
    three = 3.0 * factor
    nine = 9.0 * factor
    rest = (rate * rho) * (1.0 - 1.5 * speed) - three * u_dot_f
    quad = (4.5 * rate) * rho
    linear = (3.0 * rate) * rho
    results = [None] * 19
    results[0] = jnp.where(wall, cells[0], keep * cells[0] + LATTICE_WEIGHTS[0] * rest)

    for q in range(1, 19, 2):
        a = along(vel, q)
        b = along(force, q)
        weight = LATTICE_WEIGHTS[q]
        even = weight * (rest + a * (quad * a + nine * b))
        odd = weight * (linear * a + three * b)
        results[q] = jnp.where(wall, cells[q + 1], keep * cells[q] + (even + odd))
        results[q + 1] = jnp.where(wall, cells[q], keep * cells[q + 1] + (even - odd))
    return results, vel


def face_kernel(total, pop, solid, xface_ref, field):
    size_x, size_y, size_z = solid.shape
    for c in range(3):
        for half in range(size_x * size_y // 128):
            field[c, half * 128 : (half + 1) * 128, :] = jnp.transpose(
                total[c * size_z : (c + 1) * size_z, half * 128 : (half + 1) * 128]
            )
    for x, first, sign in ((size_x - 1, 0, 1), (0, 5, -1)):
        force = [field[c, x * size_y : (x + 1) * size_y, :] for c in range(3)]
        results, _ = collide_plane(x, force, pop, solid)
        for k, q in enumerate(X_LISTS[sign]):
            xface_ref[first + k] = results[q]


def x_faces(total, populations, solid):
    _, size_x, size_y, size_z = populations.shape
    return pl.pallas_call(
        face_kernel,
        out_shape=(
            jax.ShapeDtypeStruct((10, size_y, size_z), F32),
            jax.ShapeDtypeStruct((3, size_x * size_y, size_z), F32),
        ),
        in_specs=[vmem()] * 3,
        out_specs=(vmem(),) * 2,
        compiler_params=settings(12),
        cost_estimate=cost(2 * MIB, MIB),
        name="x_faces",
    )(total, populations, solid)


def collide_kernel(field, pop, solid, post, yfp_ref, yfm_ref, zfp_ref, zfm_ref, unit_ref):
    _, size_x, size_y, size_z = post.shape
    lane = lax.broadcasted_iota(jnp.int32, (size_y, size_z), 1)

    def plane(x, z_out):
        z_out = dict(zip((1, -1), z_out))
        lines = pl.ds(pl.multiple_of(x * 16, 16), 16)
        force = [field[c, lines, :] for c in range(3)]
        results, vel = collide_plane(x, force, pop, solid)
        for c in range(3):
            high, low = halves(vel[c])
            first = pl.ds(pl.multiple_of((x * 3 + c) * 16, 16), 16)
            unit_ref[first, 0:size_z] = high.astype(BF)
            unit_ref[first, size_z : 2 * size_z] = low.astype(BF)
        for q in range(19):
            post[q, x] = results[q]
        for sign, line, face in ((1, size_y - 1, yfp_ref), (-1, 0, yfm_ref)):
            for k, q in enumerate(Y_LISTS[sign]):
                face[k, pl.ds(x, 1), :] = results[q][line : line + 1, :]
        for sign, column in ((1, size_z - 1), (-1, 0)):
            for k, q in enumerate(Z_LISTS[sign]):
                place = k * 16 + x
                moved = pltpu.roll(results[q], (place - column + size_z) & (size_z - 1), 1)
                z_out[sign] = jnp.where(lane == place, moved, z_out[sign])
        return z_out[1], z_out[-1]

    empty = jnp.zeros((size_y, size_z), F32)
    zfp_ref[...], zfm_ref[...] = lax.fori_loop(0, size_x, plane, (empty, empty), unroll=2)


def collide(field, populations, solid):
    _, size_x, size_y, size_z = populations.shape
    face_y = jax.ShapeDtypeStruct((5, size_x, size_z), F32)
    face_z = jax.ShapeDtypeStruct((size_y, size_z), F32)
    return pl.pallas_call(
        collide_kernel,
        out_shape=(
            jax.ShapeDtypeStruct(populations.shape, F32),
            face_y,
            face_y,
            face_z,
            face_z,
            jax.ShapeDtypeStruct((size_x * size_y * 3, 2 * size_z), BF),
        ),
        in_specs=[vmem()] * 3,
        out_specs=(vmem(),) * 6,
        compiler_params=settings(12),
        cost_estimate=cost(16 * MIB, 8 * MIB),
        name="collide",
    )(field, populations, solid)


def sample_scratch(extent, verts):
    size_x, size_y, size_z = extent
    return [
        pltpu.VMEM((2, SLOT_CAP, 2 * size_z, 2 * verts), BF),
        pltpu.VMEM((2, 3 * size_x * size_y, 2 * verts), F32),
        pltpu.VMEM((2, SLOT_CAP, 8, verts), F32),
        pltpu.VMEM((2, SLOT_CAP, 8, verts), F32),
    ]


def sample_tools(place_ref, unit_ref, extent, verts, hot, grid_buf, w_rows, c_rows):
    size_x, size_y, size_z = extent
    iota_y = lax.broadcasted_iota(jnp.int32, (16, verts), 0).astype(F32)
    iota_b = iota_y.astype(BF)
    one = jnp.ones((16, verts), BF)
    zero_b = jnp.zeros((16, verts), BF)
    zero = jnp.zeros((16, verts), F32)

    def wide(ref, slot, j, row):
        return jnp.broadcast_to(ref[slot, j, row : row + 1, :], (16, verts))

    def prepare(blocks, slot):
        for j, rows in enumerate(blocks):
            weight, _, local = place_rows(place_ref, rows, extent)
            w_rows[slot, j] = weight
            for d in range(3):
                c_rows[slot, j, d : d + 1] = local[d]
        for j in range(len(blocks)):
            zl = wide(c_rows, slot, j, 2).astype(BF)
            for zb in range(size_z // 16):
                for dz in range(2):
                    value = jnp.where(iota_b == zl + float(dz - 16 * zb), one, zero_b)
                    for part in range(2):
                        line = part * size_z + zb * 16
                        hot[slot, j, line : line + 16, dz * verts : (dz + 1) * verts] = value

    def product(slot, j):
        grid_buf[j % 2] = lax.dot_general(unit_ref[...], hot[slot, j], NN, preferred_element_type=F32)

    def select(slot, j):
        xl = wide(c_rows, slot, j, 0)
        yl = wide(c_rows, slot, j, 1)
        at_y0 = iota_y == yl
        at_y1 = iota_y == yl + 1.0
        lines = {}
        for dx in range(2):
            for dz in range(2):
                first = dx * 4 + dz
                lines[dx, dz] = jnp.where(
                    at_y0,
                    wide(w_rows, slot, j, first),
                    jnp.where(at_y1, wide(w_rows, slot, j, first + 2), zero),
                )
        sums = [zero, zero, zero]
        before = None
        for x in range(size_x):
            here = xl == float(x)
            for dz in range(2):
                value = jnp.where(here, lines[0, dz], zero)
                if before is not None:
                    value = jnp.where(before, lines[1, dz], value)
                for c in range(3):
                    first = (x * 3 + c) * 16
                    part = grid_buf[j % 2, first : first + 16, dz * verts : (dz + 1) * verts]
                    sums[c] = sums[c] + value * part
            before = here
        return [jnp.sum(value, axis=0, keepdims=True) for value in sums]

    def work(slot, store):
        product(slot, 0)
        for j in range(SLOT_CAP):
            if j + 1 < SLOT_CAP:
                product(slot, j + 1)
            store(j, select(slot, j))

    return prepare, product, select, work


def x_plane(xr_ref, q):
    sign = VELOCITIES[q][0]
    return xr_ref[(0 if sign > 0 else 5) + X_LISTS[sign].index(q)]


def sample_steps(table_ref, first, last, prepare, work, put):
    def store(step):
        return lambda j, values: put(2 * step + j // 2, j % 2, values)

    prepare(pair_blocks(table_ref, first), 0)

    @pl.loop(0, (last - first) // 2)
    def _(i):
        step = first + 2 * i
        prepare(pair_blocks(table_ref, step + 1), 1)
        work(0, store(step))
        prepare(pair_blocks(table_ref, jnp.minimum(step + 2, last - 1)), 0)
        work(1, store(step + 1))


def sample_part_kernel(extent, first, last, place_ref, table_ref, unit_ref, *refs):
    out_ref, scratch = refs[-5], refs[-4:]
    verts = table_ref.shape[3]
    prepare, _, _, work = sample_tools(place_ref, unit_ref, extent, verts, *scratch)

    def put(owner, line, values):
        for c in range(3):
            out_ref[owner - 2 * first, c, line : line + 1, :] = values[c]

    sample_steps(table_ref, first, last, prepare, work, put)


def sample_part(place, table, unit, order, first, last, extent):
    owners, _, _, verts = table.shape
    size_x, size_y, size_z = extent
    return pl.pallas_call(
        functools.partial(sample_part_kernel, extent, first, last),
        out_shape=jax.ShapeDtypeStruct((2 * (last - first), 3, 2, verts), F32),
        in_specs=[smem(), vmem(), vmem()] + [pl.BlockSpec(memory_space=pl.ANY)] * len(order),
        out_specs=vmem(),
        scratch_shapes=sample_scratch(extent, verts),
        compiler_params=settings(12),
        cost_estimate=cost(
            32 * (last - first) * 3 * size_x * size_y * size_z * verts, MIB
        ),
        name="sample_part",
    )(place, table, unit, *order)


def sample_kernel(
    extent, place_ref, spot_ref, table_ref, packed, unit_ref, part_ref, *refs
):
    out_ref, found, scratch = refs[-6], refs[-5], refs[-4:]
    owners, _, _, verts = table_ref.shape
    prepare, product, select, work = sample_tools(place_ref, unit_ref, extent, verts, *scratch)
    done = part_ref.shape[0]
    for c in range(3):
        out_ref[0:done, c, 0:2] = part_ref[:, c]
        out_ref[:, c, 2:4] = jnp.zeros((owners, 2, verts), F32)

    def put(owner, line, values):
        for c in range(3):
            out_ref[owner, c, line : line + 1, :] = values[c]

    sample_steps(table_ref, done // 2, owners // 2, prepare, work, put)

    @pl.loop(0, packed_blocks(spot_ref[2 * owners], verts))
    def _(block):
        prepare([packed_rows(packed, block)], 0)
        product(0, 0)
        values = select(0, 0)
        for c in range(3):
            found[block, c : c + 1, :] = values[c]

    lane = lax.broadcasted_iota(jnp.int32, (4, verts), 1)
    for owner in range(owners):
        for j in range(2):
            spot = spot_ref[2 * owner + j]

            @pl.when(spot_ref[2 * owner + j + 1] > spot)
            def _(owner=owner, j=j, spot=spot):
                block = lax.shift_right_logical(spot, 7)
                shift = spot & (verts - 1)
                back = (verts - shift) & (verts - 1)
                first = pltpu.roll(found[block, 0:4], back, 1)
                second = pltpu.roll(found[block + 1, 0:4], back, 1)
                value = jnp.where(lane < verts - shift, first, second)
                for c in range(3):
                    out_ref[owner, c, 2 + j : 3 + j, :] = value[c : c + 1]


def sample(place, spots, table, packed, unit, part, order, extent):
    owners, _, _, verts = table.shape
    size_x, size_y, size_z = extent
    return pl.pallas_call(
        functools.partial(sample_kernel, extent),
        out_shape=jax.ShapeDtypeStruct((owners, 3, SLOT_CAP, verts), F32),
        in_specs=[smem(), smem()]
        + [vmem()] * 4
        + [pl.BlockSpec(memory_space=pl.ANY)] * len(order),
        out_specs=vmem(),
        scratch_shapes=[pltpu.VMEM((2 * owners + 2, 8, verts), F32)]
        + sample_scratch(extent, verts),
        compiler_params=settings(12),
        cost_estimate=cost(8 * owners * 3 * size_x * size_y * size_z * verts, MIB),
        name="sample_velocity",
    )(place, spots, table, packed, unit, part, *order)


def y_message_kernel(xr_ref, yfp_ref, yfm_ref, plus_ref, minus_ref):
    size_y = xr_ref.shape[1]
    for sign, face, out in ((1, yfp_ref, plus_ref), (-1, yfm_ref, minus_ref)):
        out[0:5] = face[...]
        line = size_y - 1 if sign > 0 else 0
        for e, q in enumerate(Y_EDGES[sign]):
            out[5, e : e + 1, :] = x_plane(xr_ref, q)[line : line + 1, :]


def y_messages(x_halo, y_plus, y_minus):
    shape = jax.ShapeDtypeStruct((6,) + y_plus.shape[1:], F32)
    return pl.pallas_call(
        y_message_kernel,
        out_shape=(shape, shape),
        in_specs=[vmem()] * 3,
        out_specs=(vmem(), vmem()),
        compiler_params=settings(4),
        name="y_messages",
    )(x_halo, y_plus, y_minus)


def z_message_kernel(xr_ref, yrp_ref, yrm_ref, zfp_ref, zfm_ref, plus_ref, minus_ref):
    size_y, size_z = zfp_ref.shape
    y_halo = {1: yrp_ref, -1: yrm_ref}
    lane = lax.broadcasted_iota(jnp.int32, (size_y, size_z), 1)
    for sign, face, out in ((1, zfp_ref, plus_ref), (-1, zfm_ref, minus_ref)):
        column = size_z - 1 if sign > 0 else 0
        block = face[...]
        for e, q in enumerate(Z_EDGES[sign]):
            if VELOCITIES[q][0] != 0:
                plane = x_plane(xr_ref, q)
            else:
                y_sign = VELOCITIES[q][1]
                plane = y_halo[y_sign][Y_LISTS[y_sign].index(q)]
            spot = EDGE_LANE + e
            block = jnp.where(lane == spot, pltpu.roll(plane, (spot - column) % size_z, 1), block)
        out[...] = block


def z_messages(x_halo, y_plus, y_minus, z_plus, z_minus):
    shape = jax.ShapeDtypeStruct(z_plus.shape, F32)
    return pl.pallas_call(
        z_message_kernel,
        out_shape=(shape, shape),
        in_specs=[vmem()] * 5,
        out_specs=(vmem(), vmem()),
        compiler_params=settings(4),
        name="z_messages",
    )(x_halo, y_plus, y_minus, z_plus, z_minus)


def stream_kernel(
    post,
    xr_ref,
    yrp_ref,
    yrm_ref,
    zrp_ref,
    zrm_ref,
    read_hbm,
    read,
    out_sem,
):
    _, size_x, size_y, size_z = post.shape
    y_halo = {1: yrp_ref, -1: yrm_ref}
    z_halo = {1: zrp_ref, -1: zrm_ref}
    stores = [pltpu.make_async_copy(read.at[q], read_hbm.at[q], out_sem.at[q]) for q in range(19)]
    lane = lax.broadcasted_iota(jnp.int32, (size_y, size_z), 1)
    row = lax.broadcasted_iota(jnp.int32, (size_y, size_z), 0)

    def shift_z(plane, cz, place):
        moved = pltpu.roll(plane, cz % size_z, 1)
        target = 0 if cz > 0 else size_z - 1
        column = pltpu.roll(z_halo[cz][...], (target - place) % size_z, 1)
        return jnp.where(lane == target, column, moved)

    for q in range(19):
        cx, cy, cz = VELOCITIES[q]
        rows = None
        if cy != 0:
            rows = y_halo[cy][Y_LISTS[cy].index(q)]
            if cz != 0:
                rows = shift_z(rows, cz, EDGE_LANE + Z_EDGES[cz].index(q))
        for x in range(size_x):
            source = x - cx
            outside = source < 0 or source >= size_x
            plane = x_plane(xr_ref, q) if outside else post[q, source]
            if cz != 0:
                if outside:
                    place = EDGE_LANE + Z_EDGES[cz].index(q)
                else:
                    place = Z_LISTS[cz].index(q) * 16 + source
                plane = shift_z(plane, cz, place)
            if cy != 0:
                moved = pltpu.roll(plane, cy % size_y, 0)
                target = 0 if cy > 0 else size_y - 1
                if outside:
                    e = Y_EDGES[cy].index(q)
                    line = y_halo[cy][5, e : e + 1, :]
                else:
                    line = rows[source : source + 1, :]
                plane = jnp.where(row == target, jnp.broadcast_to(line, moved.shape), moved)
            read[q, x] = plane
        stores[q].start()
    for store in stores:
        store.wait()


def stream(post, x_halo, y_plus, y_minus, z_plus, z_minus):
    anyspace = pl.BlockSpec(memory_space=pl.ANY)
    return pl.pallas_call(
        stream_kernel,
        out_shape=jax.ShapeDtypeStruct(post.shape, F32),
        in_specs=[vmem()] * 6,
        out_specs=anyspace,
        scratch_shapes=[
            pltpu.VMEM(post.shape, F32),
            pltpu.SemaphoreType.DMA((19,)),
        ],
        compiler_params=settings(10),
        cost_estimate=cost(MIB, 16 * MIB),
        name="stream_populations",
    )(post, x_halo, y_plus, y_minus, z_plus, z_minus)


def collect_kernel(inter_ref, base_ref, rank_ref, back_ref, out_ref):
    patches, verts = rank_ref.shape[1:]
    line = lax.broadcasted_iota(jnp.int32, (16, verts), 0) & (SLOT_CAP - 1)
    for p in range(patches):
        value = None
        for i in range(2):
            brick = inter_ref[i, p]
            base = base_ref[2 * p + i]
            rank = jnp.broadcast_to(rank_ref[i, p : p + 1, :], (8, verts))
            spot = jnp.concatenate([rank + base] * 2, axis=0)
            rows = [back_ref[brick, c] for c in range(3)] + [jnp.zeros((4, verts), F32)]
            picked = jnp.concatenate(rows, axis=0)
            picked = jnp.take_along_axis(picked, spot & (verts - 1), axis=1)
            here = lax.shift_right_logical(spot, 7) == line
            picked = jnp.where(here & (jnp.concatenate([rank] * 2, axis=0) >= 0), picked, 0.0)
            value = picked if value is None else value + picked
        value = value + pltpu.roll(value, 15, 0)
        value = value + pltpu.roll(value, 14, 0)
        value = jnp.concatenate([value[4 * c : 4 * c + 1] for c in range(3)], axis=0)
        out_ref[:, p, :] = value


def collect(intersection, bases, ranks, back):
    _, patches, verts = ranks.shape
    return pl.pallas_call(
        collect_kernel,
        out_shape=jax.ShapeDtypeStruct((3, patches, verts), F32),
        in_specs=[smem()] * 2 + [vmem()] * 2,
        out_specs=vmem(),
        compiler_params=settings(4),
        name="collect_velocity",
    )(intersection, bases, ranks, back)


def shifted(value, axis, step):
    count = lax.axis_size(axis)
    return lax.ppermute(value, axis, [(i, (i + step) % count) for i in range(count)])


def exchanged(value):
    return lax.all_to_all(value, ("gy", "gz"), split_axis=0, concat_axis=0, tiled=True)


def body(populations, solid_flags, positions, anchors, base_cell, weights, intersection):
    extent = populations.shape[1:]
    axes = ("gx", "gy", "gz")
    bricks = lax.axis_size("gy") * lax.axis_size("gz")
    here = [lax.axis_index(axis) for axis in axes]
    place = jnp.stack(
        [here[d] * extent[d] for d in range(3)]
        + here
        + [jnp.int32(lax.axis_size(axis)) for axis in axes]
    ).astype(jnp.int32)
    lists = intersection.T
    outgoing, ranks, bases = build_lists(
        lists,
        jnp.transpose(positions, (1, 0, 2)),
        jnp.transpose(anchors, (1, 0, 2)),
        jnp.transpose(base_cell, (1, 0, 2)),
        weights,
        bricks,
        lax.axis_size("gz"),
        extent,
    )
    table = exchanged(outgoing)
    total, packed, spots, populations = spread(place, table, populations)
    x_face, field = x_faces(total, populations, solid_flags)
    post, y_plus, y_minus, z_plus, z_minus, unit = collide(field, populations, solid_flags)
    if lax.axis_size("gx") == 2:
        x_halo = shifted(x_face, "gx", 1)
    else:
        x_halo = jnp.concatenate(
            [shifted(x_face[:5], "gx", 1), shifted(x_face[5:], "gx", -1)], axis=0
        )
    y_plus, y_minus = y_messages(x_halo, y_plus, y_minus)
    y_plus = shifted(y_plus, "gy", 1)
    y_minus = shifted(y_minus, "gy", -1)
    steps = table.shape[0] // 2
    part = sample_part(place, table, unit, (x_halo,), 0, steps // 4 * 3, extent)
    order = (y_plus, y_minus)
    sampled = sample(place, spots, table, packed, unit, part, order, extent)
    back = exchanged(sampled)
    z_plus, z_minus = z_messages(x_halo, y_plus, y_minus, z_plus, z_minus)
    z_plus = shifted(z_plus, "gz", 1)
    z_minus = shifted(z_minus, "gz", -1)
    read = stream(post, x_halo, y_plus, y_minus, z_plus, z_minus)
    velocity = collect(lists, bases, ranks, back)
    return read, jnp.transpose(velocity, (1, 0, 2))


def solution(mesh):
    return jax.shard_map(
        body,
        mesh=mesh,
        in_specs=(
            P(None, "gx", "gy", "gz"),
            P("gx", "gy", "gz"),
            P(("gx", "gy", "gz"), None, None),
            P(("gx", "gy", "gz"), None, None),
            P(("gx", "gy", "gz"), None, None),
            P(("gx", "gy", "gz"), None, None),
            P(("gx", "gy", "gz"), None),
        ),
        out_specs=(P(None, "gx", "gy", "gz"), P(("gx", "gy", "gz"), None, None)),
        check_vma=False,
    )
```
